32 devices in a mesh: img: 8 (over z, y), row: 4 (over x, core).
Axes of the slice: x: 2, y: 2, z: 4, core: 2. Of those that a mesh axis runs over, the one named last changes fastest.
Arguments:
- tokens: bfloat16 [8, 4064, 1024], P('img', 'row'), may hold values from -6 to 6
- counts: int32 [8, 8], P('img'), may hold values from 1 to 1024, 4032 in all within a row
- owner: int32 [8, 8], P('img'), may hold values from 0 to 7, each once within a row
- w_qkv: bfloat16 [1024, 3072], replicated, may hold values from -0.1875 to 0.1875
- qv_bias: float32 [2, 1024], replicated, may hold values from -3 to 3
- w_out: bfloat16 [1024, 1024], replicated, may hold values from -0.5 to 0.5
- out_bias: float32 [1024], replicated, may hold values from -3 to 3
- w_up: bfloat16 [1024, 4096], replicated, may hold values from -0.1875 to 0.1875
- up_bias: float32 [4096], replicated, may hold values from -3 to 3
- w_down: bfloat16 [4096, 1024], replicated, may hold values from -0.09375 to 0.09375
- down_bias: float32 [1024], replicated, may hold values from -3 to 3
- norm_gain: float32 [3, 1024], replicated, may hold values from 0.25 to 1.75
- norm_bias: float32 [3, 1024], replicated, may hold values from -2 to 2
- learn_in: bfloat16 [1024, 1024], replicated, may hold values from -0.1875 to 0.1875
- learn_in_bias: float32 [1024], replicated, may hold values from -3 to 3
- learn_out: bfloat16 [1024, 8], replicated, may hold values from -0.75 to 0.75
- learn_out_bias: float32 [8], replicated, may hold values from -3 to 3
- cotangent: float32 [8, 8, 8, 1024], P('img', 'row'), may hold values from -6 to 6
Outputs:
- learned: float32 [8, 8, 8, 1024], P('img', 'row')
- grad_tokens: float32 [8, 4064, 1024], P('img', 'row')
- grad_w_qkv: float32 [1024, 3072], P('img')
- grad_qv_bias: float32 [2, 1024], replicated
- grad_w_out: float32 [1024, 1024], P('img')
- grad_out_bias: float32 [1024], replicated
- grad_w_up: float32 [1024, 4096], P('img')
- grad_up_bias: float32 [4096], replicated
- grad_w_down: float32 [4096, 1024], P('img')
- grad_down_bias: float32 [1024], replicated
- grad_norm_gain: float32 [3, 1024], replicated
- grad_norm_bias: float32 [3, 1024], replicated
- grad_learn_in: float32 [1024, 1024], P('img')
- grad_learn_in_bias: float32 [1024], replicated
- grad_learn_out: float32 [1024, 8], P('img')
- grad_learn_out_bias: float32 [8], replicated
The draws below stay inside these ranges and needn't reach their ends.
Inputs may be any that keep to these rules, and one draw needn't show every extreme that they name: counts[g, i] is the number of patches of image i of group g; each group's counts sum to 4032, and one image of each group has exactly 1024. Each row of owner is a permutation: image i of group g has its learned tokens at slot owner[g, i].
All inputs are finite; a program needn't handle non-finite values.
Results may differ from the reference program's by a relative error of at most 0.018.
Values may be sent and summed in bfloat16 or wider, within the bound.
A program may use at most 512 MiB of HBM per device.

```python
import math
import jax
import jax.numpy as jnp
import numpy as np
from jax import lax

D = 1024
HEADS = 16
HEAD = 64
FF = 4096
LH = 1024
LT = 8
IMGS = 8
LONGEST = 1024
GROUPS = 8
TOTAL = 4032
TOK_DEV = 1016
ROWS = 4064
N_ROW = 4


def steps_of(rng, extent, pieces, smallest, largest):
    def one(axis_at, parts):
        heights = jax.random.uniform(jax.random.fold_in(jax.random.fold_in(rng, 6), axis_at), (parts,), jnp.float32, smallest / len(pieces), largest / len(pieces))
        return jnp.repeat(jnp.exp(heights), extent[axis_at] // parts).reshape((-1,) + (1,) * (len(extent) - axis_at - 1))

    level = one(*pieces[0])
    for cut in pieces[1:]:
        level = level * one(*cut)
    return level


def length_profile(number_of, total, reach, lean):
    portions = [(1 << 20) // math.isqrt(rank ** lean) + 1 for rank in range(2, number_of + 1)]
    rest, given = total - reach - (number_of - 1), [1] * (number_of - 1)
    while rest > 0:
        free = [i for i in range(number_of - 1) if given[i] < reach]
        whole, left = sum([portions[i] for i in free]), rest
        for i in free:
            more = min(reach - given[i], max(1, left * portions[i] // whole), rest)
            given[i] = given[i] + more
            rest = rest - more
    return np.array([reach] + given)


def uneven(stream_key, count, total, reach, lean):
    if count == 2:
        one = jax.random.randint(stream_key, (), max(1, total - reach), min(reach, total - 1) + 1)
        return jnp.stack([one, total - one])
    sizes = jnp.asarray(length_profile(count, total, reach, lean), jnp.int32)
    pairs = (count - 1) // 2
    giver, receiver = sizes[1:1 + 2 * pairs:2], sizes[2:2 + 2 * pairs:2]
    margin = jnp.minimum(giver - 1, reach - receiver)
    moved = jax.random.randint(jax.random.fold_in(stream_key, 1), (pairs,), 0, 1 << 20) % (margin + 1)
    sizes = sizes.at[1:1 + 2 * pairs:2].set(giver - moved).at[2:2 + 2 * pairs:2].set(receiver + moved)
    return sizes[jax.random.permutation(jax.random.fold_in(stream_key, 2), count)]


def bell_draw(own_key, extent, scale, reach, pieces=(), kind=jnp.bfloat16):
    values = jax.random.normal(own_key, extent, jnp.float32) * scale
    if len(pieces) > 0:
        values = steps_of(own_key, extent, pieces, -0.22, 0.18) * values
    return jnp.clip(values, min=-reach, max=reach).astype(kind)


def setup_inputs(seed: int = 0) -> dict:
    splits = jax.random.split(jax.random.key(seed), 19)
    tokens = bell_draw(splits[0], (GROUPS, ROWS, D), 1.0, 6.0, ((0, 8), (1, 4)))
    counts = jax.vmap(lambda own: uneven(own, IMGS, TOTAL, LONGEST, 2))(jax.random.split(splits[1], GROUPS)).reshape((GROUPS, IMGS)).astype(jnp.int32)
    owner = jax.vmap(lambda own: jax.random.permutation(own, IMGS))(jax.random.split(splits[2], GROUPS)).reshape((GROUPS, IMGS)).astype(jnp.int32)
    w_qkv = bell_draw(splits[3], (D, 3 * D), D ** -0.5, 0.1875)
    qv_bias = bell_draw(splits[4], (2, D), 0.5, 3.0, (), jnp.float32)
    w_out = bell_draw(splits[5], (D, D), (D // 8) ** -0.5, 0.5)
    out_bias = bell_draw(splits[6], (D,), 0.5, 3.0, (), jnp.float32)
    w_up = bell_draw(splits[7], (D, FF), D ** -0.5, 0.1875)
    up_bias = bell_draw(splits[8], (FF,), 0.5, 3.0, (), jnp.float32)
    w_down = bell_draw(splits[9], (FF, D), FF ** -0.5, 0.09375)
    down_bias = bell_draw(splits[10], (D,), 0.5, 3.0, (), jnp.float32)
    norm_gain = jnp.clip(1.0 + 0.15 * jax.random.normal(splits[11], (3, D), jnp.float32), 0.25, 1.75)
    norm_bias = bell_draw(splits[12], (3, D), 0.3, 2.0, (), jnp.float32)
    learn_in = bell_draw(splits[13], (D, LH), D ** -0.5, 0.1875)
    learn_in_bias = bell_draw(splits[14], (LH,), 0.5, 3.0, (), jnp.float32)
    learn_out = bell_draw(splits[15], (LH, LT), (LH // 16) ** -0.5, 0.75)
    learn_out_bias = bell_draw(splits[16], (LT,), 1.0, 3.0, (), jnp.float32)
    cotangent = bell_draw(splits[17], (GROUPS, IMGS, LT, D), 1.0, 6.0, ((0, 8), (1, 4)), jnp.float32)
    return dict(tokens=tokens, counts=counts, owner=owner, w_qkv=w_qkv, qv_bias=qv_bias, w_out=w_out, out_bias=out_bias, w_up=w_up, up_bias=up_bias, w_down=w_down, down_bias=down_bias, norm_gain=norm_gain, norm_bias=norm_bias, learn_in=learn_in, learn_in_bias=learn_in_bias, learn_out=learn_out, learn_out_bias=learn_out_bias, cotangent=cotangent)


@jax.custom_vjp
def low(v):
    return lax.optimization_barrier(v.astype(jnp.bfloat16)).astype(jnp.float32)

@jax.custom_vjp
def low_back(v):
    return v

def low_keep(v):
    return (low(v), None)

def low_pass(kept, grad):
    return (grad,)

def back_keep(v):
    return (v, None)

def back_low(kept, grad):
    return (low(grad),)
low.defvjp(low_keep, low_pass)
low_back.defvjp(back_keep, back_low)
highest = lax.Precision.HIGHEST
epsilon = 1e-06

def normalize(values, gain, shift):
    centre = values - lax.optimization_barrier(jnp.mean(values, axis=-1, keepdims=True))
    spread = lax.optimization_barrier(jnp.mean(centre * centre, axis=-1, keepdims=True))
    return centre * lax.rsqrt(spread + epsilon) * gain + shift

def smooth(values):
    return jax.nn.gelu(values, approximate=False)

def row_images(counts, device, local_rows, row_count):
    upper_end = counts * (device + 1) // row_count
    lower_end = counts * device // row_count
    run_ends = jnp.cumsum(upper_end - lower_end).astype(jnp.int32)
    positions = jnp.arange(local_rows, dtype=jnp.int32)
    return lax.optimization_barrier(jnp.sum((positions[:, None] >= run_ends[None, :]).astype(jnp.int32), axis=1)).astype(jnp.int32)

def by_head(array):
    return array.reshape(-1, HEADS, HEAD).transpose(1, 0, 2)

def group_forward(inputs_f32, params, image_of, group_counts, group_owner):
    w_qkv, qv_bias, w_out, out_bias, w_up, up_bias, w_down, down_bias, norm_gain, norm_bias, learn_in, learn_in_bias, learn_out, learn_out_bias = params
    normed_one = low(normalize(inputs_f32, norm_gain[0], norm_bias[0]))
    mixed = low_back(jnp.dot(normed_one, w_qkv, precision=highest))
    queries = low((mixed[:, :D] + qv_bias[0]) * 0.125)
    key_rows = low(mixed[:, D:2 * D])
    value_rows = low(mixed[:, 2 * D:] + qv_bias[1])
    allowed = image_of[:, None] == image_of[None, :]

    def one_head(inputs):
        query_head, key_head, value_head = inputs
        scores = low_back(jnp.dot(query_head, key_head.T, precision=highest))
        scores = jnp.where(allowed, scores, -1e+30)
        row_max = lax.optimization_barrier(jnp.max(scores, axis=1, keepdims=True))
        exponent = jnp.exp(scores - row_max)
        row_total = lax.optimization_barrier(jnp.sum(exponent, axis=1, keepdims=True))
        probability = low(exponent / row_total)
        return jnp.dot(probability, value_head, precision=highest)
    per_head = lax.map(jax.checkpoint(one_head), (by_head(queries), by_head(key_rows), by_head(value_rows)))
    attended = low(low_back(per_head.transpose(1, 0, 2).reshape(-1, D)))
    hidden = inputs_f32 + low_back(jnp.dot(attended, w_out, precision=highest)) + out_bias
    normed_two = low(normalize(hidden, norm_gain[1], norm_bias[1]))
    gated = low(smooth(low_back(jnp.dot(normed_two, w_up, precision=highest)) + up_bias))
    result = hidden + low_back(jnp.dot(gated, w_down, precision=highest)) + down_bias
    normed_three = low(normalize(result, norm_gain[2], norm_bias[2]))
    inner = low(smooth(low_back(jnp.dot(normed_three, learn_in, precision=highest)) + learn_in_bias))
    maps = jax.nn.sigmoid(low_back(jnp.dot(inner, learn_out, precision=highest)) + learn_out_bias)
    maps_low = low(maps)
    result_low = low(result)
    member = (image_of[:, None] == jnp.arange(IMGS, dtype=jnp.int32)[None, :]).astype(jnp.float32)
    spread_maps = (member[:, :, None] * maps_low[:, None, :]).reshape(-1, IMGS * LT)
    pooled = low_back(jnp.dot(spread_maps.T, result_low, precision=highest)).reshape(IMGS, LT, D)
    pooled = pooled * lax.rsqrt(group_counts.astype(jnp.float32))[:, None, None]
    return jnp.zeros_like(pooled).at[group_owner].set(pooled)

def add_pair(first, second):
    return first + second

def reference(tokens, counts, owner, w_qkv, qv_bias, w_out, out_bias, w_up, up_bias, w_down, down_bias, norm_gain, norm_bias, learn_in, learn_in_bias, learn_out, learn_out_bias, cotangent):
    params = tuple((weight.astype(jnp.float32) for weight in (w_qkv, qv_bias, w_out, out_bias, w_up, up_bias, w_down, down_bias, norm_gain, norm_bias, learn_in, learn_in_bias, learn_out, learn_out_bias)))
    device_ids = jnp.arange(N_ROW, dtype=jnp.int32)

    def one_group(carry, inputs):
        group_tokens, group_counts, group_owner, group_cotangent = inputs

        def images_of(device):
            return row_images(group_counts, device, TOK_DEV, N_ROW)
        image_of = jax.vmap(images_of)(device_ids).reshape(-1)

        def forward(inputs_f32, weights):
            return group_forward(inputs_f32, weights, image_of, group_counts, group_owner)
        learned, pullback = jax.vjp(forward, group_tokens.astype(jnp.float32), params)
        grad_inputs, grad_params = pullback(group_cotangent)
        carry = jax.tree.map(add_pair, carry, grad_params)
        return (carry, (learned, grad_inputs))
    zeros = jax.tree.map(jnp.zeros_like, params)
    totals, (learned, grad_tokens) = lax.scan(one_group, zeros, (tokens, counts, owner, cotangent))
    return (learned, grad_tokens, totals[0], totals[1], totals[2], totals[3], totals[4], totals[5], totals[6], totals[7], totals[8], totals[9], totals[10], totals[11], totals[12], totals[13])
```

```python
import functools

import jax
import jax.numpy as jnp
from jax import lax
from jax.experimental import pallas as pl
from jax.experimental.pallas import tpu as pltpu
from jax.sharding import PartitionSpec as P

HEADS = 16
HEAD = 64
LT = 8
IMGS = 8
BLK = 256
NEG = -1e30
VMEM = 58 << 20

highest = lax.Precision.HIGHEST
epsilon = 1e-06
f32 = jnp.float32
bf16 = jnp.bfloat16


def normalize(values, gain, shift):
    centre = values - jnp.mean(values, axis=-1, keepdims=True)
    spread = jnp.mean(centre * centre, axis=-1, keepdims=True)
    return centre * lax.rsqrt(spread + epsilon) * gain + shift


def smooth(values):
    return jax.nn.gelu(values, approximate=False)


def matmul(left, right):
    return jnp.dot(left, right, preferred_element_type=f32)


def nt(left, right):
    return lax.dot_general(left, right, (((1,), (1,)), ((), ())), preferred_element_type=f32)


def tn(left, right):
    return lax.dot_general(left, right, (((0,), (0,)), ((), ())), preferred_element_type=f32)


def row_images(counts, device, local_rows, row_count):
    upper_end = counts * (device + 1) // row_count
    lower_end = counts * device // row_count
    run_ends = jnp.cumsum(upper_end - lower_end)
    positions = jnp.arange(local_rows, dtype=jnp.int32)
    return jnp.sum((positions[:, None] >= run_ends[None, :]).astype(jnp.int32), axis=1)


def swap(value, axis, bit):
    size = lax.axis_size(axis)
    return lax.ppermute(value, axis, [(i, i ^ bit) for i in range(size)])


def bits_of(size):
    return [1 << i for i in range(size.bit_length() - 1)]


def gather_pieces(value, axis):
    pieces = {0: value}
    for d in range(1, lax.axis_size(axis)):
        low = d & -d
        pieces[d] = swap(pieces[d ^ low], axis, low)
    return [pieces[d] for d in range(lax.axis_size(axis))]


def send_pieces(pieces, axis):
    size = lax.axis_size(axis)
    return [pieces[0]] + [
        lax.ppermute(pieces[d], axis, [(i, i ^ d) for i in range(size)]) for d in range(1, size)
    ]


def reduce_pieces(pieces, axis):
    pieces = list(pieces)
    for bit in bits_of(lax.axis_size(axis)):
        half = [d for d in range(len(pieces)) if d % (2 * bit) == 0]
        arrived = {d: swap(pieces[d + bit], axis, bit) for d in reversed(half)}
        for d in half:
            pieces[d] = (pieces[d].astype(f32) + arrived[d].astype(f32)).astype(pieces[d].dtype)
    return pieces[0]


def all_sum(value, axes):
    for axis in axes:
        for bit in bits_of(lax.axis_size(axis)):
            value = value + swap(value, axis, bit)
    return value


def halve(value, axis, bit, dim):
    mine = (lax.axis_index(axis) // bit) % 2
    length = value.shape[dim] // 2
    sent = lax.dynamic_slice_in_dim(value, (1 - mine) * length, length, dim)
    kept = lax.dynamic_slice_in_dim(value, mine * length, length, dim)
    arrived = swap(sent, axis, bit)
    return (kept.astype(f32) + arrived.astype(f32)).astype(bf16)


def double(value, axis, bit, dim):
    mine = (lax.axis_index(axis) // bit) % 2
    arrived = swap(value, axis, bit)
    return jnp.where(
        mine == 0,
        jnp.concatenate([value, arrived], dim),
        jnp.concatenate([arrived, value], dim),
    )


def reduce_weight(grad, row_first):
    rows, columns = grad.shape
    images = lax.axis_size("img")
    row_bits, img_bits = bits_of(lax.axis_size("row")), bits_of(images)
    value = grad.reshape((2,) * len(img_bits) + (rows // images, columns))

    def over_row(value, bits):
        for bit in bits:
            value = halve(value, "row", bit, value.ndim - 1)
        return value

    def over_img(value):
        for bit in img_bits:
            dim = len(img_bits) - bit.bit_length()
            value = halve(value, "img", bit, dim)
        return value

    if row_first:
        value = over_img(over_row(value, row_bits))
    else:
        value = over_row(over_img(over_row(value, row_bits[:1])), row_bits[1:])
    value = value.reshape(rows // images, -1)
    for bit in reversed(row_bits):
        value = double(value, "row", bit, 1)
    return value.astype(f32)


def params(flags=("arbitrary",)):
    return pltpu.CompilerParams(dimension_semantics=flags, vmem_limit_bytes=VMEM)


def valid_rows(block, piece_rows, local_rows):
    position = lax.broadcasted_iota(jnp.int32, (BLK, 1), 0) % piece_rows + block * piece_rows
    return position < local_rows


def load_block(refs, block, piece_rows, local_rows):
    value = jnp.concatenate([ref[...] for ref in refs], axis=0).astype(f32)
    return jnp.where(valid_rows(block, piece_rows, local_rows), value, 0.0)


def norm_parts(value):
    centre = value - jnp.mean(value, axis=-1, keepdims=True)
    rstd = lax.rsqrt(jnp.mean(centre * centre, axis=-1, keepdims=True) + epsilon)
    return centre * rstd, rstd


def qkv_kernel(count, local_rows, features, *refs):
    pieces, (w_ref, bias_ref, gain_ref, shift_ref) = refs[:count], refs[count : count + 4]
    q_ref, k_ref, v_ref, kt_ref, vt_ref = refs[count + 4 :]
    block = pl.program_id(0)
    unit, _ = norm_parts(load_block(pieces, block, BLK // count, local_rows))
    normed = (unit * gain_ref[...] + shift_ref[...]).astype(bf16)
    mixed = matmul(normed, w_ref[...])
    keys = mixed[:, features : 2 * features]
    values = mixed[:, 2 * features :] + bias_ref[1:2, :]
    q_ref[...] = ((mixed[:, :features] + bias_ref[0:1, :]) * 0.125).astype(bf16)
    k_ref[...] = keys.astype(bf16)
    v_ref[...] = values.astype(bf16)
    kt_ref[0] = keys.T.astype(bf16)
    vt_ref[0] = values.T.astype(bf16)


def qkv_call(pieces, weight, bias, gain, shift):
    count, (local_rows, width) = len(pieces), pieces[0].shape
    features = weight.shape[1] // 3
    piece_rows = BLK // count
    blocks = pl.cdiv(local_rows, piece_rows)
    whole = lambda a: pl.BlockSpec(a.shape, lambda b: (0,) * a.ndim)
    flat = pl.BlockSpec((BLK, features), lambda b: (b, 0))
    turned = pl.BlockSpec((1, features, BLK), lambda b: (b, 0, 0))
    return pl.pallas_call(
        functools.partial(qkv_kernel, count, local_rows, features),
        grid=(blocks,),
        in_specs=[pl.BlockSpec((piece_rows, width), lambda b: (b, 0))] * count
        + [whole(weight), whole(bias), whole(gain), whole(shift)],
        out_specs=[flat, flat, flat, turned, turned],
        out_shape=[jax.ShapeDtypeStruct((blocks * BLK, features), bf16)] * 3
        + [jax.ShapeDtypeStruct((blocks, features, BLK), bf16)] * 2,
        compiler_params=params(),
        cost_estimate=pl.CostEstimate(
            flops=2 * blocks * BLK * width * 3 * features,
            bytes_accessed=2 * blocks * BLK * (width + 5 * features),
            transcendentals=0,
        ),
    )(*pieces, weight, bias, gain, shift)


def per_head(stack_ref, value, heads):
    lane = lax.broadcasted_iota(jnp.int32, value.shape, 1) // HEAD
    for h in range(heads):
        stack_ref[h] = jnp.where(lane == h, value, jnp.zeros_like(value))


def attend_kernel(count, heads, lo_ref, hi_ref, *refs):
    q_ref, k_ref, vt_ref, imgq_ref, imgk_ref = refs[:5]
    outs, (ot_ref, lse_ref) = refs[5 : 5 + count], refs[5 + count : 7 + count]
    s_ref, qs_ref, acc_ref = refs[7 + count :]
    block = pl.program_id(0)
    lo, hi = lo_ref[block], hi_ref[block]
    per_head(qs_ref, q_ref[...], heads)
    imgq = imgq_ref[...]

    def first(kb, tops):
        rows = pl.ds(pl.multiple_of(kb * BLK, BLK), BLK)
        keys = k_ref[rows, :]
        allowed = imgk_ref[rows, :] == imgq
        new = []
        for h in range(heads):
            s = jnp.where(allowed, nt(keys, qs_ref[h]), NEG)
            s_ref[kb - lo, h] = s
            new.append(jnp.maximum(tops[h], jnp.max(s.reshape(BLK // 8, 8, BLK), axis=0)))
        return tuple(new)

    tops = lax.fori_loop(lo, hi, first, (jnp.full((8, BLK), NEG, f32),) * heads)
    tops = [jnp.max(t, axis=0, keepdims=True) for t in tops]
    acc_ref[...] = jnp.zeros_like(acc_ref)

    def second(kb, sums):
        new = []
        for h in range(heads):
            p = jnp.exp(s_ref[kb - lo, h] - tops[h])
            new.append(sums[h] + jnp.sum(p.reshape(BLK // 8, 8, BLK), axis=0))
            rows = slice(h * HEAD, (h + 1) * HEAD)
            acc_ref[rows, :] += matmul(vt_ref[kb, rows, :], p.astype(bf16))
        return tuple(new)

    sums = lax.fori_loop(lo, hi, second, (jnp.zeros((8, BLK), f32),) * heads)
    sums = [jnp.sum(t, axis=0, keepdims=True) for t in sums]
    for h in range(heads):
        rows = slice(h * HEAD, (h + 1) * HEAD)
        acc_ref[rows, :] = acc_ref[rows, :] / sums[h]
    lse_ref[...] = jnp.concatenate(
        [t + jnp.log(s) for t, s in zip(tops, sums)] + [jnp.zeros((8 - heads, BLK), f32)], axis=0
    )
    ot_ref[0] = acc_ref[...]
    out = acc_ref[...].T.astype(bf16)
    for d in range(count):
        outs[d][...] = out[d * (BLK // count) : (d + 1) * (BLK // count)]


def attend_call(q, k, vt, imgq, imgk, lo, hi, count, local_rows):
    blocks, features = vt.shape[0], q.shape[1]
    heads = features // HEAD
    piece_rows = BLK // count
    whole = lambda a: pl.BlockSpec(a.shape, lambda b, *_: (0,) * a.ndim)
    return pl.pallas_call(
        functools.partial(attend_kernel, count, heads),
        grid_spec=pltpu.PrefetchScalarGridSpec(
            num_scalar_prefetch=2,
            grid=(blocks,),
            in_specs=[
                pl.BlockSpec((BLK, features), lambda b, *_: (b, 0)),
                whole(k),
                whole(vt),
                pl.BlockSpec((1, BLK), lambda b, *_: (0, b)),
                whole(imgk),
            ],
            out_specs=[pl.BlockSpec((piece_rows, features), lambda b, *_: (b, 0))] * count
            + [
                pl.BlockSpec((1, features, BLK), lambda b, *_: (b, 0, 0)),
                pl.BlockSpec((8, BLK), lambda b, *_: (0, b)),
            ],
            scratch_shapes=[
                pltpu.VMEM((blocks, heads, BLK, BLK), f32),
                pltpu.VMEM((heads, BLK, features), bf16),
                pltpu.VMEM((features, BLK), f32),
            ],
        ),
        out_shape=[jax.ShapeDtypeStruct((local_rows, features), bf16)] * count
        + [
            jax.ShapeDtypeStruct((blocks, features, BLK), f32),
            jax.ShapeDtypeStruct((8, blocks * BLK), f32),
        ],
        compiler_params=params(),
        cost_estimate=pl.CostEstimate(
            flops=2 * (blocks * BLK) ** 2 * features,
            bytes_accessed=2 * blocks * BLK * features * 8,
            transcendentals=(blocks * BLK) ** 2 * heads // 4,
        ),
    )(lo, hi, q, k, vt, imgq, imgk)


def attend_back_kernel(count, heads, local_rows, lo_ref, hi_ref, *refs):
    pieces = refs[:count]
    q_ref, k_ref, v_ref, kt_ref, ot_ref, lse_ref, imgq_ref, imgk_ref = refs[count : count + 8]
    dq_ref, dk_out, dv_out, sums_ref = refs[count + 8 : count + 12]
    qs_ref, dos_ref, p_ref, ds_ref, dqt_ref, dk_ref, dv_ref = refs[count + 12 :]
    block = pl.program_id(0)
    lo, hi = lo_ref[block], hi_ref[block]

    @pl.when(block == 0)
    def _():
        dk_ref[...] = jnp.zeros_like(dk_ref)
        dv_ref[...] = jnp.zeros_like(dv_ref)
        sums_ref[...] = jnp.zeros_like(sums_ref)

    grad = load_block(pieces, block, BLK // count, local_rows)
    per_head(qs_ref, q_ref[...], heads)
    lane = lax.broadcasted_iota(jnp.int32, grad.shape, 1) // HEAD
    for h in range(heads):
        dos_ref[h * BLK : (h + 1) * BLK] = jnp.where(lane == h, grad, 0.0).astype(bf16)
    both = grad.T * ot_ref[0]
    delta = [
        jnp.sum(both[h * HEAD : (h + 1) * HEAD], axis=0, keepdims=True) for h in range(heads)
    ]
    imgq = imgq_ref[...]
    dqt_ref[...] = jnp.zeros_like(dqt_ref)

    def body(kb, _):
        rows = pl.ds(pl.multiple_of(kb * BLK, BLK), BLK)
        keys, values = k_ref[rows, :], v_ref[rows, :]
        allowed = imgk_ref[rows, :] == imgq
        for h in range(heads):
            s = nt(keys, qs_ref[h])
            p = jnp.exp(jnp.where(allowed, s - lse_ref[h : h + 1, :], NEG))
            dp = nt(values, dos_ref[h * BLK : (h + 1) * BLK])
            ds = (p * (dp - delta[h])).astype(bf16)
            p_ref[:, h * BLK : (h + 1) * BLK] = p.astype(bf16)
            ds_ref[:, h * BLK : (h + 1) * BLK] = ds
            feats = slice(h * HEAD, (h + 1) * HEAD)
            dqt_ref[feats, :] += matmul(kt_ref[kb, feats, :], ds)
        dv_ref[rows, :] += matmul(p_ref[...], dos_ref[...])
        dk_ref[rows, :] += matmul(
            ds_ref[...], jnp.concatenate([qs_ref[h] for h in range(heads)], axis=0)
        )
        return 0

    lax.fori_loop(lo, hi, body, 0)
    dq = dqt_ref[...].T * 0.125
    dq_ref[...] = dq.astype(bf16)
    sums_ref[0:1, :] += jnp.sum(dq, axis=0, keepdims=True)

    @pl.when(block == pl.num_programs(0) - 1)
    def _():
        dk_out[...] = dk_ref[...].astype(bf16)
        dv = dv_ref[...]
        dv_out[...] = dv.astype(bf16)
        sums_ref[1:2, :] = jnp.sum(dv, axis=0, keepdims=True)


def attend_back_call(pieces, q, k, v, kt, ot, lse, imgq, imgk, lo, hi):
    count, (local_rows, features) = len(pieces), pieces[0].shape
    blocks = kt.shape[0]
    heads = features // HEAD
    whole = lambda a: pl.BlockSpec(a.shape, lambda b, *_: (0,) * a.ndim)
    once = lambda a: pl.BlockSpec(
        a.shape, lambda b, *_: (0,) * a.ndim, pipeline_mode=pl.Buffered(1)
    )
    flat = jax.ShapeDtypeStruct((blocks * BLK, features), bf16)
    return pl.pallas_call(
        functools.partial(attend_back_kernel, count, heads, local_rows),
        grid_spec=pltpu.PrefetchScalarGridSpec(
            num_scalar_prefetch=2,
            grid=(blocks,),
            in_specs=[pl.BlockSpec((BLK // count, features), lambda b, *_: (b, 0))] * count
            + [
                pl.BlockSpec((BLK, features), lambda b, *_: (b, 0)),
                once(k),
                once(v),
                once(kt),
                pl.BlockSpec((1, features, BLK), lambda b, *_: (b, 0, 0)),
                pl.BlockSpec((8, BLK), lambda b, *_: (0, b)),
                pl.BlockSpec((1, BLK), lambda b, *_: (0, b)),
                once(imgk),
            ],
            out_specs=[
                pl.BlockSpec((BLK, features), lambda b, *_: (b, 0)),
                whole(flat),
                whole(flat),
                pl.BlockSpec((8, features), lambda b, *_: (0, 0)),
            ],
            scratch_shapes=[
                pltpu.VMEM((heads, BLK, features), bf16),
                pltpu.VMEM((heads * BLK, features), bf16),
                pltpu.VMEM((BLK, heads * BLK), bf16),
                pltpu.VMEM((BLK, heads * BLK), bf16),
                pltpu.VMEM((features, BLK), f32),
                pltpu.VMEM((blocks * BLK, features), f32),
                pltpu.VMEM((blocks * BLK, features), f32),
            ],
        ),
        out_shape=[flat, flat, flat, jax.ShapeDtypeStruct((8, features), f32)],
        compiler_params=params(),
        cost_estimate=pl.CostEstimate(
            flops=5 * (blocks * BLK) ** 2 * features,
            bytes_accessed=2 * blocks * BLK * features * 12,
            transcendentals=(blocks * BLK) ** 2 * heads // 4,
        ),
    )(lo, hi, *pieces, q, k, v, kt, ot, lse, imgq, imgk)


def qkv_back_kernel(count, local_rows, features, *refs):
    pieces = refs[:count]
    dq_ref, dk_ref, dv_ref, w_ref, gain_ref, shift_ref = refs[count : count + 6]
    outs = refs[count + 6 : 2 * count + 6]
    gw_ref, sums_ref, acc_ref = refs[2 * count + 6 :]
    block = pl.program_id(0)

    @pl.when(block == 0)
    def _():
        acc_ref[...] = jnp.zeros_like(acc_ref)
        sums_ref[...] = jnp.zeros_like(sums_ref)

    unit, _ = norm_parts(load_block(pieces, block, BLK // count, local_rows))
    normed = (unit * gain_ref[...] + shift_ref[...]).astype(bf16)
    mixed = jnp.concatenate([dq_ref[...], dk_ref[...], dv_ref[...]], axis=1)
    back = nt(mixed, w_ref[...])
    sums_ref[0:1, :] += jnp.sum(back * unit, axis=0, keepdims=True)
    sums_ref[1:2, :] += jnp.sum(back, axis=0, keepdims=True)
    acc_ref[...] += tn(normed, mixed)
    low = back.astype(bf16)
    for d in range(count):
        outs[d][...] = low[d * (BLK // count) : (d + 1) * (BLK // count)]

    @pl.when(block == pl.num_programs(0) - 1)
    def _():
        gw_ref[...] = acc_ref[...].astype(bf16)


def qkv_back_call(pieces, dq, dk, dv, weight, gain, shift):
    count, (local_rows, width) = len(pieces), pieces[0].shape
    features = dq.shape[1]
    piece_rows = BLK // count
    blocks = dq.shape[0] // BLK
    whole = lambda a: pl.BlockSpec(a.shape, lambda b: (0,) * len(a.shape))
    flat = pl.BlockSpec((BLK, features), lambda b: (b, 0))
    piece = pl.BlockSpec((piece_rows, width), lambda b: (b, 0))
    gw = jax.ShapeDtypeStruct(weight.shape, bf16)
    sums = jax.ShapeDtypeStruct((8, width), f32)
    return pl.pallas_call(
        functools.partial(qkv_back_kernel, count, local_rows, features),
        grid=(blocks,),
        in_specs=[piece] * count + [flat] * 3 + [whole(weight), whole(gain), whole(shift)],
        out_specs=[piece] * count + [whole(gw), whole(sums)],
        out_shape=[jax.ShapeDtypeStruct((local_rows, width), bf16)] * count + [gw, sums],
        scratch_shapes=[pltpu.VMEM(weight.shape, f32)],
        compiler_params=params(),
        cost_estimate=pl.CostEstimate(
            flops=4 * blocks * BLK * width * 3 * features,
            bytes_accessed=2 * blocks * BLK * (2 * width + 3 * features),
            transcendentals=0,
        ),
    )(*pieces, dq, dk, dv, weight, gain, shift)


def rows_of(array, index, length):
    return lax.dynamic_slice_in_dim(array, index * length, length, 0)


def on_device(
    tokens,
    counts,
    owner,
    w_qkv,
    qv_bias,
    w_out,
    out_bias,
    w_up,
    up_bias,
    w_down,
    down_bias,
    norm_gain,
    norm_bias,
    learn_in,
    learn_in_bias,
    learn_out,
    learn_out_bias,
    cotangent,
):
    width = tokens.shape[2]
    local_rows = tokens.shape[1]
    row_count = lax.axis_size("row")
    device = lax.axis_index("row")
    image_device = lax.axis_index("img")
    features = width // row_count
    slots_here = IMGS // row_count
    group_counts = counts[0]
    partners = [device ^ d for d in range(row_count)]

    pieces = gather_pieces(tokens[0], "row")
    grads_in = gather_pieces(cotangent[0].reshape(slots_here, LT * width).astype(bf16), "row")

    piece_rows = BLK // row_count
    blocks = pl.cdiv(local_rows, piece_rows)
    images = jnp.stack([row_images(group_counts, p, local_rows, row_count) for p in partners])
    image_here = images[0]
    extra = blocks * piece_rows - local_rows
    images = jnp.pad(images, ((0, 0), (0, extra)), constant_values=IMGS + 1)
    images = images.reshape(row_count, blocks, piece_rows).transpose(1, 0, 2).reshape(blocks, BLK)
    least, most = jnp.min(images, axis=1), jnp.max(images, axis=1)
    lo = jnp.sum((most[None, :] < least[:, None]).astype(jnp.int32), axis=1)
    hi = jnp.sum((least[None, :] <= most[:, None]).astype(jnp.int32), axis=1)
    imgq, imgk = images.reshape(1, -1), images.reshape(-1, 1)

    w_here = lax.dynamic_slice_in_dim(
        w_qkv.reshape(width, 3, width), device * features, features, 2
    ).reshape(width, 3 * features)
    bias_here = lax.dynamic_slice_in_dim(qv_bias, device * features, features, 1)
    q, k, v, kt, vt = qkv_call(pieces, w_here, bias_here, norm_gain[0:1], norm_bias[0:1])
    *attended, ot, lse = attend_call(q, k, vt, imgq, imgk, lo, hi, row_count, local_rows)
    attended = send_pieces(attended, "row")
    attended_low = jnp.concatenate(attended, axis=1)
    w_out_here = jnp.concatenate([rows_of(w_out, p, features) for p in partners], axis=0)

    inputs_f32 = tokens[0].astype(f32)
    hidden = inputs_f32 + matmul(attended_low, w_out_here) + out_bias
    normed_two, back_two = jax.vjp(normalize, hidden, norm_gain[1], norm_bias[1])
    normed_two_low = normed_two.astype(bf16)
    gated, back_gate = jax.vjp(smooth, matmul(normed_two_low, w_up) + up_bias)
    gated_low = gated.astype(bf16)
    result = hidden + matmul(gated_low, w_down) + down_bias
    normed_three, back_three = jax.vjp(normalize, result, norm_gain[2], norm_bias[2])
    normed_three_low = normed_three.astype(bf16)
    inner, back_inner = jax.vjp(smooth, matmul(normed_three_low, learn_in) + learn_in_bias)
    inner_low = inner.astype(bf16)
    maps = jax.nn.sigmoid(matmul(inner_low, learn_out) + learn_out_bias)
    maps_low = maps.astype(bf16)
    result_low = result.astype(bf16)
    member = (image_here[:, None] == jnp.arange(IMGS, dtype=jnp.int32)[None, :]).astype(bf16)
    spread_maps = (member[:, :, None] * maps_low[:, None, :]).reshape(local_rows, IMGS * LT)
    partial_value = matmul(spread_maps.T, result_low)

    slot_rel = ((owner[0] // slots_here) ^ device) * slots_here + owner[0] % slots_here
    select = (slot_rel[:, None] == jnp.arange(IMGS, dtype=jnp.int32)[None, :]).astype(f32)
    scale = lax.rsqrt(group_counts.astype(f32))
    by_slot = jnp.dot(select.T, partial_value.reshape(IMGS, LT * width), precision=highest)
    by_slot = by_slot.astype(bf16).reshape(row_count, slots_here, LT * width)
    arrived = send_pieces([by_slot[d] for d in range(row_count)], "row")
    summed = sum(a.astype(f32) for a in arrived)
    scale_here = jnp.dot(scale, select, precision=highest)[:slots_here]
    learned = (summed * scale_here[:, None]).reshape(1, slots_here, LT, width)

    incoming = jnp.concatenate(grads_in, axis=0).astype(f32)
    grad_pooled = jnp.dot(select, incoming, precision=highest) * scale[:, None]
    grad_pooled_low = grad_pooled.reshape(IMGS * LT, width).astype(bf16)
    grad_result = matmul(spread_maps, grad_pooled_low)
    grad_spread = matmul(result_low, grad_pooled_low.T)
    grad_maps = jnp.sum(
        grad_spread.reshape(local_rows, IMGS, LT) * member.astype(f32)[:, :, None], axis=1
    )
    grad_logit = grad_maps * maps * (1.0 - maps)
    grad_learn_out_bias = jnp.sum(grad_logit, axis=0)
    grad_logit_low = grad_logit.astype(bf16)
    grad_learn_out = matmul(inner_low.T, grad_logit_low)
    (grad_learn_pre,) = back_inner(matmul(grad_logit_low, learn_out.T))
    grad_learn_in_bias = jnp.sum(grad_learn_pre, axis=0)
    grad_learn_low = grad_learn_pre.astype(bf16)
    grad_from_three, gain_three, shift_three = back_three(matmul(grad_learn_low, learn_in.T))
    grad_result = grad_result + grad_from_three
    grad_down_bias = jnp.sum(grad_result, axis=0)
    grad_result_low = grad_result.astype(bf16)
    grad_w_down = tn(gated_low, grad_result_low).astype(bf16)
    (grad_up_pre,) = back_gate(matmul(grad_result_low, w_down.T))
    grad_up_bias = jnp.sum(grad_up_pre, axis=0)
    grad_up_low = grad_up_pre.astype(bf16)
    grad_w_up = tn(normed_two_low, grad_up_low).astype(bf16)
    grad_from_two, gain_two, shift_two = back_two(matmul(grad_up_low, w_up.T))
    grad_hidden = grad_result + grad_from_two
    grad_out_bias = jnp.sum(grad_hidden, axis=0)
    grad_hidden_low = grad_hidden.astype(bf16)
    grad_attended = [
        nt(grad_hidden_low, w_out_here[d * features : (d + 1) * features]).astype(bf16)
        for d in range(row_count)
    ]
    grad_attended = send_pieces(grad_attended, "row")
    grad_learn_in = tn(normed_three_low, grad_learn_low).astype(bf16)
    grad_w_out = jnp.concatenate(
        [
            tn(a, grad_hidden_low)
            for a in [
                lax.dynamic_slice_in_dim(attended_low, (device ^ d) * features, features, 1)
                for d in range(row_count)
            ]
        ],
        axis=0,
    ).astype(bf16)

    share_down = reduce_weight(grad_w_down, True)
    share_up = reduce_weight(grad_w_up, False)
    share_learn = reduce_weight(grad_learn_in, True)
    share_out = reduce_weight(grad_w_out, False)
    early = jnp.concatenate(
        [
            grad_up_bias,
            grad_out_bias,
            grad_down_bias,
            gain_two,
            gain_three,
            shift_two,
            shift_three,
            grad_learn_in_bias,
            grad_learn_out.reshape(-1),
            grad_learn_out_bias,
        ]
    )
    early = all_sum(jnp.pad(early, (0, -early.shape[0] % 1024)).reshape(-1, 128), ("row", "img"))
    early = early.reshape(-1)

    dq, dk, dv, qv_sums = attend_back_call(
        grad_attended, q, k, v, kt, ot, lse, imgq, imgk, lo, hi
    )
    *back, grad_w_here, sums = qkv_back_call(
        pieces, dq, dk, dv, w_here, norm_gain[0:1], norm_bias[0:1]
    )
    grad_normed = reduce_pieces(back, "row").astype(f32)
    centred, rstd = norm_parts(inputs_f32)
    e = grad_normed * norm_gain[0]
    grad_tokens = (
        grad_hidden
        + (
            e
            - jnp.mean(e, axis=-1, keepdims=True)
            - centred * jnp.mean(e * centred, axis=-1, keepdims=True)
        )
        * rstd
    )[None]

    images_count = lax.axis_size("img")
    img_bits = bits_of(images_count)
    value = grad_w_here.reshape((2,) * len(img_bits) + (width // images_count, 3 * features))
    for bit in img_bits:
        value = halve(value, "img", bit, len(img_bits) - bit.bit_length())
    value = value.reshape(width // images_count, 3, features)
    for bit in bits_of(row_count):
        value = double(value, "row", bit, 2)
    share_qkv = value.reshape(width // images_count, 3 * width).astype(f32)

    spread_qv = lax.dynamic_update_slice(
        jnp.zeros((2, width), f32), qv_sums[0:2], (0, device * features)
    )
    late = all_sum(jnp.concatenate([spread_qv, sums[0:2]], axis=0), ("row", "img"))

    sizes = [up_bias.shape[0]] + [width] * 7 + [learn_out.size, learn_out.shape[1]]
    parts, at = [], 0
    for size in sizes:
        parts.append(early[at : at + size])
        at += size
    up_sum, out_sum, down_sum, gain_two, gain_three, shift_two, shift_three = parts[:7]
    learn_in_sum, learn_out_sum, learn_out_bias_sum = parts[7:]
    share_learn_out = rows_of(
        learn_out_sum.reshape(learn_out.shape), image_device, learn_out.shape[0] // images_count
    )
    return (
        learned,
        grad_tokens,
        share_qkv,
        late[0:2],
        share_out,
        out_sum,
        share_up,
        up_sum,
        share_down,
        down_sum,
        jnp.stack([late[2], gain_two, gain_three]),
        jnp.stack([late[3], shift_two, shift_three]),
        share_learn,
        learn_in_sum,
        share_learn_out,
        learn_out_bias_sum,
    )


def solution(mesh):
    by_image = P("img", None)
    in_specs = (
        (P("img", "row", None), by_image, by_image) + (P(),) * 14 + (P("img", "row", None, None),)
    )
    out_specs = (
        P("img", "row", None, None),
        P("img", "row", None),
        by_image,
        P(),
        by_image,
        P(),
        by_image,
        P(),
        by_image,
        P(),
        P(),
        P(),
        by_image,
        P(),
        by_image,
        P(),
    )
    return jax.shard_map(
        on_device, mesh=mesh, in_specs=in_specs, out_specs=out_specs, check_vma=False
    )
```

```python
import functools

import jax
import jax.numpy as jnp
from jax import lax
from jax.experimental import pallas as pl
from jax.experimental.pallas import tpu as pltpu
from jax.sharding import PartitionSpec as P

HEADS = 16
HEAD = 64
LT = 8
IMGS = 8
BLK = 256
NEG = -1e30
VMEM = 60 << 20
ROW_BLOCK = 256
GRAD_BLOCK = 512

highest = lax.Precision.HIGHEST
epsilon = 1e-06
f32 = jnp.float32
bf16 = jnp.bfloat16


def smooth_both(v):
    half = jnp.abs(v) * 0.7071067811865476
    t = 1.0 / (1.0 + 0.3275911 * half)
    bell = jnp.exp(-half * half)
    poly = t * (
        0.127414796
        + t * (-0.142248368 + t * (0.7107068705 + t * (-0.7265760135 + t * 0.5307027145)))
    )
    tail = poly * bell
    cdf = jnp.where(v >= 0.0, 1.0 - tail, tail)
    return v * cdf, cdf + v * (bell * 0.3989422804014327)


def matmul(left, right):
    return jnp.dot(left, right, preferred_element_type=f32)


def nt(left, right):
    return lax.dot_general(left, right, (((1,), (1,)), ((), ())), preferred_element_type=f32)


def tn(left, right):
    return lax.dot_general(left, right, (((0,), (0,)), ((), ())), preferred_element_type=f32)


def row_images(counts, device, local_rows, row_count):
    upper_end = counts * (device + 1) // row_count
    lower_end = counts * device // row_count
    run_ends = jnp.cumsum(upper_end - lower_end)
    positions = jnp.arange(local_rows, dtype=jnp.int32)
    return jnp.sum((positions[:, None] >= run_ends[None, :]).astype(jnp.int32), axis=1)


def bits_of(size):
    return [1 << i for i in range(size.bit_length() - 1)]


def jump(value, row_mask, img_mask=0):
    rows, imgs = lax.axis_size("row"), lax.axis_size("img")
    if img_mask == 0:
        return lax.ppermute(value, "row", [(i, i ^ row_mask) for i in range(rows)])
    if row_mask == 0:
        return lax.ppermute(value, "img", [(i, i ^ img_mask) for i in range(imgs)])
    mask = img_mask * rows + row_mask
    return lax.ppermute(value, ("img", "row"), [(i, i ^ mask) for i in range(rows * imgs)])


def masks_of(bits):
    masks = []
    for e in range(1 << len(bits)):
        masks.append(
            tuple(
                sum(bit for j, (axis, bit) in enumerate(bits) if axis == name and e >> j & 1)
                for name in ("row", "img")
            )
        )
    return masks


def gather_pieces(value):
    pieces = {0: value}
    order = sorted(range(1, lax.axis_size("row")), key=lambda d: (d & 1, d))
    for d in order:
        low = d & -d
        pieces[d] = jump(pieces[d ^ low], low)
    return [pieces[d] for d in range(lax.axis_size("row"))]


def send_pieces(pieces):
    far_first = sorted(range(1, len(pieces)), reverse=True)
    arrived = {d: jump(pieces[d], d) for d in far_first}
    return [pieces[0]] + [arrived[d] for d in range(1, len(pieces))]


def stages():
    row_bits = [("row", b) for b in bits_of(lax.axis_size("row"))]
    img_bits = [("img", b) for b in bits_of(lax.axis_size("img"))]
    return row_bits, img_bits


def tree(values):
    while len(values) > 1:
        values = [values[i] + values[i + 1] for i in range(0, len(values), 2)]
    return values[0]


def behind(value, after):
    return lax.optimization_barrier((value, *after))[0] if after else value


def reduce_stage(value, bits, img_count, after=()):
    mine = {"row": lax.axis_index("row"), "img": lax.axis_index("img")}

    def part(e):
        piece = value
        for j, (axis, bit) in enumerate(bits):
            want = (mine[axis] // bit) % 2 ^ (e >> j & 1)
            dim = value.ndim - 1 if axis == "row" else img_count - bit.bit_length()
            length = piece.shape[dim] // 2
            piece = lax.dynamic_slice_in_dim(piece, want * length, length, dim)
        return piece

    masks = masks_of(bits)
    arrived = {
        e: behind(jump(part(e), *masks[e]), after) for e in reversed(range(1, len(masks)))
    }
    arrived[0] = part(0)
    return tree([arrived[e].astype(f32) for e in range(len(masks))]).astype(bf16)


def spread_img(grad):
    rows, columns = grad.shape
    images = lax.axis_size("img")
    return grad.reshape((2,) * len(bits_of(images)) + (rows // images, columns))


def gather_columns(value, order, bits):
    masks = [row_mask for row_mask, _ in masks_of(bits)]
    device = lax.axis_index("row") % len(masks)
    stack = jnp.stack([value if m == 0 else jump(value, m) for m in masks])
    return [
        lax.dynamic_index_in_dim(stack, order(c) ^ device, 0, False) for c in range(len(masks))
    ]


def exchange_sum(value, bits):
    values = [value] + [jump(value, *mask) for mask in masks_of(bits)[1:]]
    return tree([v.astype(f32) for v in values]).astype(bf16)


def reversed_bits(index, size):
    width = size.bit_length() - 1
    return int(format(index, f"0{width}b")[::-1], 2) if width else 0


def finish_weight(value, bits):
    value = value.reshape(value.shape[-2:])
    count = 1 << len(bits)
    blocks = gather_columns(value, lambda c: reversed_bits(c, count), bits)
    return jnp.concatenate(blocks, axis=1).astype(f32)


def params(flags=("arbitrary",)):
    return pltpu.CompilerParams(dimension_semantics=flags, vmem_limit_bytes=VMEM)


ANYWHERE = pl.BlockSpec(memory_space=pl.ANY)


def own_columns(w_qkv, device, features, splits):
    width = w_qkv.shape[0]
    wide = features // splits

    def spec(s, part):
        def index(b, me):
            return 0, part * (width // wide) + me[0] * splits + s

        return pl.BlockSpec((width, wide), index, pipeline_mode=pl.Buffered(1))

    return [spec(s, part) for s in range(splits) for part in range(3)], [w_qkv] * (3 * splits)


def valid_rows(block, piece_rows, local_rows):
    position = lax.broadcasted_iota(jnp.int32, (BLK, 1), 0) % piece_rows + block * piece_rows
    return position < local_rows


def load_block(refs, block, piece_rows, local_rows):
    value = jnp.concatenate([ref[...] for ref in refs], axis=0).astype(f32)
    return jnp.where(valid_rows(block, piece_rows, local_rows), value, 0.0)


def norm_parts(value):
    centre = value - jnp.mean(value, axis=-1, keepdims=True)
    rstd = lax.rsqrt(jnp.mean(centre * centre, axis=-1, keepdims=True) + epsilon)
    return centre * rstd, rstd


def qkv_kernel(count, splits, local_rows, features, me_ref, *refs):
    n_w = 3 * splits
    pieces, columns = refs[:count], refs[count : count + n_w]
    bias_ref, gain_ref, shift_ref = refs[count + n_w : count + n_w + 3]
    n_ref, q_ref, k_ref, v_ref, kt_ref, vt_ref, w_ref = refs[count + n_w + 3 :]
    block = pl.program_id(0)
    wide = features // splits

    @pl.when(block == 0)
    def _():
        for i, ref in enumerate(columns):
            w_ref[:, i * wide : (i + 1) * wide] = ref[...]

    unit, _ = norm_parts(load_block(pieces, block, BLK // count, local_rows))
    normed = (unit * gain_ref[...] + shift_ref[...]).astype(bf16)
    n_ref[...] = normed.reshape(n_ref.shape)
    mixed = matmul(normed, w_ref[...])
    for s in range(splits):
        at = slice(s * wide, (s + 1) * wide)
        part = mixed[:, 3 * s * wide : 3 * (s + 1) * wide]
        keys = part[:, wide : 2 * wide]
        values = part[:, 2 * wide :] + bias_ref[1:2, at]
        q_ref[:, at] = ((part[:, :wide] + bias_ref[0:1, at]) * 0.125).astype(bf16)
        k_ref[:, at] = keys.astype(bf16)
        v_ref[:, at] = values.astype(bf16)
        kt_ref[0, at] = keys.T.astype(bf16)
        vt_ref[0, at] = values.T.astype(bf16)


def qkv_call(me, pieces, w_qkv, bias, gain, shift, splits):
    count, (local_rows, width) = len(pieces), pieces[0].shape
    features = width // count
    piece_rows = BLK // count
    blocks = pl.cdiv(local_rows, piece_rows)
    whole = lambda a: pl.BlockSpec(a.shape, lambda b, m: (0,) * a.ndim)
    flat = pl.BlockSpec((BLK, features), lambda b, m: (b, 0))
    turned = pl.BlockSpec((1, features, BLK), lambda b, m: (b, 0, 0))
    specs, operands = own_columns(w_qkv, me, features, splits)
    return pl.pallas_call(
        functools.partial(qkv_kernel, count, splits, local_rows, features),
        grid_spec=pltpu.PrefetchScalarGridSpec(
            num_scalar_prefetch=1,
            grid=(blocks,),
            in_specs=[pl.BlockSpec((piece_rows, width), lambda b, m: (b, 0))] * count
            + specs
            + [whole(bias), whole(gain), whole(shift)],
            out_specs=[
                pl.BlockSpec((count, piece_rows, width), lambda b, m: (0, b, 0)),
                flat,
                flat,
                flat,
                turned,
                turned,
            ],
            scratch_shapes=[pltpu.VMEM((width, 3 * features), bf16)],
        ),
        out_shape=[jax.ShapeDtypeStruct((count, blocks * piece_rows, width), bf16)]
        + [jax.ShapeDtypeStruct((blocks * BLK, features), bf16)] * 3
        + [jax.ShapeDtypeStruct((blocks, features, BLK), bf16)] * 2,
        compiler_params=params(),
        cost_estimate=pl.CostEstimate(
            flops=6 * blocks * BLK * width * 3 * features,
            bytes_accessed=2 * blocks * BLK * (2 * width + 5 * features),
            transcendentals=0,
        ),
    )(me, *pieces, *operands, bias, gain, shift)


def per_head(stack_ref, value, heads):
    lane = lax.broadcasted_iota(jnp.int32, value.shape, 1) // HEAD
    for h in range(heads):
        stack_ref[h] = jnp.where(lane == h, value, jnp.zeros_like(value))


def attend_kernel(count, heads, lo_ref, hi_ref, *refs):
    q_ref, k_ref, vt_ref, imgq_ref, imgk_ref = refs[:5]
    outs, (ot_ref, lse_ref) = refs[5 : 5 + count], refs[5 + count : 7 + count]
    s_ref, qs_ref, acc_ref = refs[7 + count :]
    block = pl.program_id(0)
    lo, hi = lo_ref[block], hi_ref[block]
    per_head(qs_ref, q_ref[...], heads)
    imgq = imgq_ref[...]

    def first(kb, tops):
        rows = pl.ds(pl.multiple_of(kb * BLK, BLK), BLK)
        keys = k_ref[rows, :]
        allowed = imgk_ref[rows, :] == imgq
        new = []
        for h in range(heads):
            s = jnp.where(allowed, nt(keys, qs_ref[h]), NEG)
            s_ref[kb - lo, h] = s
            new.append(jnp.maximum(tops[h], jnp.max(s.reshape(BLK // 8, 8, BLK), axis=0)))
        return tuple(new)

    tops = lax.fori_loop(lo, hi, first, (jnp.full((8, BLK), NEG, f32),) * heads)
    tops = [jnp.max(t, axis=0, keepdims=True) for t in tops]
    acc_ref[...] = jnp.zeros_like(acc_ref)

    def second(kb, sums):
        new = []
        for h in range(heads):
            p = jnp.exp(s_ref[kb - lo, h] - tops[h])
            new.append(sums[h] + jnp.sum(p.reshape(BLK // 8, 8, BLK), axis=0))
            rows = slice(h * HEAD, (h + 1) * HEAD)
            acc_ref[rows, :] += matmul(vt_ref[kb, rows, :], p.astype(bf16))
        return tuple(new)

    sums = lax.fori_loop(lo, hi, second, (jnp.zeros((8, BLK), f32),) * heads)
    sums = [jnp.sum(t, axis=0, keepdims=True) for t in sums]
    for h in range(heads):
        rows = slice(h * HEAD, (h + 1) * HEAD)
        acc_ref[rows, :] = acc_ref[rows, :] / sums[h]
    lse_ref[...] = jnp.concatenate(
        [t + jnp.log(s) for t, s in zip(tops, sums)] + [jnp.zeros((8 - heads, BLK), f32)], axis=0
    )
    ot_ref[0] = acc_ref[...]
    out = acc_ref[...].T.astype(bf16)
    for d in range(count):
        outs[d][...] = out[d * (BLK // count) : (d + 1) * (BLK // count)]


def attend_call(q, k, vt, imgq, imgk, lo, hi, count):
    blocks, features = vt.shape[0], q.shape[1]
    heads = features // HEAD
    piece_rows = BLK // count
    whole = lambda a: pl.BlockSpec(a.shape, lambda b, *_: (0,) * a.ndim)
    return pl.pallas_call(
        functools.partial(attend_kernel, count, heads),
        grid_spec=pltpu.PrefetchScalarGridSpec(
            num_scalar_prefetch=2,
            grid=(blocks,),
            in_specs=[
                pl.BlockSpec((BLK, features), lambda b, *_: (b, 0)),
                whole(k),
                whole(vt),
                pl.BlockSpec((1, BLK), lambda b, *_: (0, b)),
                whole(imgk),
            ],
            out_specs=[pl.BlockSpec((piece_rows, features), lambda b, *_: (b, 0))] * count
            + [
                pl.BlockSpec((1, features, BLK), lambda b, *_: (b, 0, 0)),
                pl.BlockSpec((8, BLK), lambda b, *_: (0, b)),
            ],
            scratch_shapes=[
                pltpu.VMEM((blocks, heads, BLK, BLK), f32),
                pltpu.VMEM((heads, BLK, features), bf16),
                pltpu.VMEM((features, BLK), f32),
            ],
        ),
        out_shape=[jax.ShapeDtypeStruct((blocks * piece_rows, features), bf16)] * count
        + [
            jax.ShapeDtypeStruct((blocks, features, BLK), f32),
            jax.ShapeDtypeStruct((8, blocks * BLK), f32),
        ],
        compiler_params=params(),
        cost_estimate=pl.CostEstimate(
            flops=10 * (blocks * BLK) ** 2 * features,
            bytes_accessed=2 * blocks * BLK * features * 8,
            transcendentals=0,
        ),
    )(lo, hi, q, k, vt, imgq, imgk)


def attend_back_kernel(count, heads, first, waits, lo_ref, hi_ref, *refs):
    pieces, refs = refs[:count], refs[:count] + refs[count + waits :]
    q_ref, k_ref, v_ref, kt_ref, ot_ref, lse_ref, imgq_ref, imgk_ref = refs[count : count + 8]
    groups = count // 2
    outs, sums_ref = refs[count + 8 : count + groups + 8], refs[count + groups + 8]
    qs_ref, dos_ref, p_ref, ds_ref, dqt_ref, dk_ref, dv_ref = refs[count + groups + 9 :]
    block = pl.program_id(0)
    lo, hi = lo_ref[block], hi_ref[block]
    piece_rows = BLK // count
    wide = heads * HEAD

    @pl.when(block == 0)
    def _():
        dk_ref[...] = jnp.zeros_like(dk_ref)
        dv_ref[...] = jnp.zeros_like(dv_ref)
        sums_ref[...] = jnp.zeros_like(sums_ref)

    grad = jnp.concatenate([ref[...] for ref in pieces], axis=0)
    query = q_ref[...]
    lane = lax.broadcasted_iota(jnp.int32, grad.shape, 1) // HEAD
    for h in range(heads):
        dos_ref[h * BLK : (h + 1) * BLK] = jnp.where(lane == h, grad, jnp.zeros_like(grad))
        qs_ref[h * BLK : (h + 1) * BLK] = jnp.where(lane == h, query, jnp.zeros_like(query))
    both = grad.astype(f32).T * ot_ref[0]
    delta = [
        jnp.sum(both[h * HEAD : (h + 1) * HEAD], axis=0, keepdims=True) for h in range(heads)
    ]
    logsum = [lse_ref[first + h : first + h + 1, :] for h in range(heads)]
    imgq = imgq_ref[...]
    dqt_ref[...] = jnp.zeros_like(dqt_ref)

    def step(kb, width):
        length = width * BLK
        rows = pl.ds(pl.multiple_of(kb * BLK, BLK), length)
        keys, values = k_ref[rows, :], v_ref[rows, :]
        allowed = imgk_ref[rows, :] == imgq
        s = nt(keys, qs_ref[...])
        dp = nt(values, dos_ref[...])
        for h in range(heads):
            cols = slice(h * BLK, (h + 1) * BLK)
            p = jnp.exp(jnp.where(allowed, s[:, cols] - logsum[h], NEG))
            p_ref[:length, cols] = p.astype(bf16)
            ds_ref[:length, cols] = (p * (dp[:, cols] - delta[h])).astype(bf16)
        dv_ref[rows, :] += matmul(p_ref[:length], dos_ref[...])
        dk_ref[rows, :] += matmul(ds_ref[:length], qs_ref[...])
        for h in range(heads):
            cols, feats = slice(h * BLK, (h + 1) * BLK), slice(h * HEAD, (h + 1) * HEAD)
            total = 0.0
            for j in range(width):
                ds = ds_ref[j * BLK : (j + 1) * BLK, cols]
                total = total + matmul(kt_ref[kb + j, feats, :], ds)
            dqt_ref[feats, :] += total

    def pair(i, _):
        step(lo + 2 * i, 2)
        return 0

    lax.fori_loop(0, (hi - lo) // 2, pair, 0)

    @pl.when((hi - lo) % 2 == 1)
    def _():
        step(hi - 1, 1)

    dq = dqt_ref[...].T * 0.125
    sums_ref[0:1, :] += jnp.sum(dq, axis=0, keepdims=True)
    here = pl.ds(pl.multiple_of(block * piece_rows, piece_rows), piece_rows)
    for d in range(count):
        outs[d // 2][d % 2, here, :wide] = dq[d * piece_rows : (d + 1) * piece_rows].astype(bf16)

    @pl.when(block == pl.num_programs(0) - 1)
    def _():
        sums_ref[1:2, :] = jnp.sum(dv_ref[...], axis=0, keepdims=True)

        def move(b, _):
            to = pl.ds(pl.multiple_of(b * piece_rows, piece_rows), piece_rows)
            for d in range(count):
                at = pl.ds(pl.multiple_of(b * BLK + d * piece_rows, piece_rows), piece_rows)
                outs[d // 2][d % 2, to, wide : 2 * wide] = dk_ref[at, :].astype(bf16)
                outs[d // 2][d % 2, to, 2 * wide :] = dv_ref[at, :].astype(bf16)
            return 0

        lax.fori_loop(0, pl.num_programs(0), move, 0)


def attend_back_call(pieces, q, k, v, kt, ot, lse, imgq, imgk, lo, hi, split, after):
    count, (rows, wide) = len(pieces), pieces[0].shape
    blocks = kt.shape[0]
    heads = wide // HEAD
    once = pl.Buffered(1)
    half = pl.BlockSpec((blocks * BLK, wide), lambda b, *_: (0, split), pipeline_mode=once)
    out = jax.ShapeDtypeStruct((2, rows, 3 * wide), bf16)
    return pl.pallas_call(
        functools.partial(attend_back_kernel, count, heads, split * heads, len(after)),
        grid_spec=pltpu.PrefetchScalarGridSpec(
            num_scalar_prefetch=2,
            grid=(blocks,),
            in_specs=[pl.BlockSpec((BLK // count, wide), lambda b, *_: (b, 0))] * count
            + [ANYWHERE] * len(after)
            + [
                pl.BlockSpec((BLK, wide), lambda b, *_: (b, split)),
                half,
                half,
                pl.BlockSpec((blocks, wide, BLK), lambda b, *_: (0, split, 0), pipeline_mode=once),
                pl.BlockSpec((1, wide, BLK), lambda b, *_: (b, split, 0)),
                pl.BlockSpec((8, BLK), lambda b, *_: (0, b)),
                pl.BlockSpec((1, BLK), lambda b, *_: (0, b)),
                pl.BlockSpec(imgk.shape, lambda b, *_: (0, 0), pipeline_mode=once),
            ],
            out_specs=[pl.BlockSpec(out.shape, lambda b, *_: (0, 0, 0), pipeline_mode=once)] * (count // 2)
            + [pl.BlockSpec((8, wide), lambda b, *_: (0, 0))],
            scratch_shapes=[
                pltpu.VMEM((heads * BLK, wide), bf16),
                pltpu.VMEM((heads * BLK, wide), bf16),
                pltpu.VMEM((2 * BLK, heads * BLK), bf16),
                pltpu.VMEM((2 * BLK, heads * BLK), bf16),
                pltpu.VMEM((wide, BLK), f32),
                pltpu.VMEM((blocks * BLK, wide), f32),
                pltpu.VMEM((blocks * BLK, wide), f32),
            ],
        ),
        out_shape=[out] * (count // 2) + [jax.ShapeDtypeStruct((8, wide), f32)],
        compiler_params=params(),
        cost_estimate=pl.CostEstimate(
            flops=16 * (blocks * BLK) ** 2 * wide,
            bytes_accessed=2 * blocks * BLK * wide * 12,
            transcendentals=0,
        ),
    )(lo, hi, *pieces, *after, q, k, v, kt, ot, lse, imgq, imgk)


def norm_back(grad, unit, rstd, gain):
    e = grad * gain
    mean = jnp.mean(e, axis=-1, keepdims=True)
    return (e - mean - unit * jnp.mean(e * unit, axis=-1, keepdims=True)) * rstd


def total(value):
    return jnp.sum(value, axis=0, keepdims=True)


def rows_kernel(count, splits, local_rows, *refs):
    (
        tok_ref,
        img_ref,
        w_out_ref,
        w_up_ref,
        w_down_ref,
        learn_in_ref,
        learn_out_ref,
        vec_ref,
        up_bias_ref,
        out_bias_ref,
        pooled_grad_ref,
    ) = refs[:11]
    attended = refs[11 : 11 + count]
    at = 11 + count
    (
        n2_ref,
        gated_ref,
        gup_ref,
        gres_ref,
        n3_ref,
        glearn_ref,
        inner_ref,
        glogit_ref,
        ghid_ref,
        ghid_f32_ref,
    ) = refs[at : at + 10]
    gatt = refs[at + 10 : at + 10 + count * splits]
    at += 10 + count * splits
    pooled_ref, vsum_ref, usum_ref, lsum_ref = refs[at : at + 4]
    hid_ref, res_ref, dgate_ref, up0_ref, up1_ref = refs[at + 4 :]
    step = pl.program_id(0)
    rows, width = tok_ref.shape
    hidden_units = w_up_ref.shape[1]
    chunk = up0_ref.shape[1]
    chunks = hidden_units // chunk

    @pl.when(step == 0)
    def _():
        for ref in (pooled_ref, vsum_ref, usum_ref, lsum_ref):
            ref[...] = jnp.zeros_like(ref)

    def vec(i):
        return vec_ref[i : i + 1, :]

    position = lax.broadcasted_iota(jnp.int32, (rows, 1), 0) + step * rows
    tok = jnp.where(position < local_rows, tok_ref[...].astype(f32), 0.0)
    low = jnp.concatenate([ref[...] for ref in attended], axis=1)
    hidden = tok + matmul(low, w_out_ref[...]) + vec(0)
    hid_ref[...] = hidden
    unit, _ = norm_parts(hidden)
    n2_ref[...] = (unit * vec(2) + vec(3)).astype(bf16)

    def columns(j):
        return pl.ds(pl.multiple_of(j * chunk, chunk), chunk)

    def up(ref, j):
        ref[...] = matmul(n2_ref[...], w_up_ref[:, columns(j)])

    def gate(ref, j):
        value, slope = smooth_both(ref[...] + up_bias_ref[:, columns(j)])
        gated_ref[:, columns(j)] = value.astype(bf16)
        dgate_ref[:, columns(j)] = slope

    up(up0_ref, 0)

    def pair(i, _):
        up(up1_ref, 2 * i + 1)
        gate(up0_ref, 2 * i)
        up(up0_ref, jnp.minimum(2 * i + 2, chunks - 1))
        gate(up1_ref, 2 * i + 1)
        return 0

    lax.fori_loop(0, chunks // 2, pair, 0)
    result = hid_ref[...] + matmul(gated_ref[...], w_down_ref[...]) + vec(1)
    res_ref[...] = result
    unit, rstd = norm_parts(result)
    n3_ref[...] = (unit * vec(4) + vec(5)).astype(bf16)
    inner, slope = smooth_both(matmul(n3_ref[...], learn_in_ref[...]) + vec(6))
    inner_ref[...] = inner.astype(bf16)
    maps = jax.nn.sigmoid(matmul(inner_ref[...], learn_out_ref[...]) + out_bias_ref[...])
    member = lax.broadcasted_iota(jnp.int32, maps.shape, 1) // LT == img_ref[...]
    spread = jnp.where(member, maps, 0.0).astype(bf16)
    result_low = res_ref[...].astype(bf16)
    pooled_ref[...] += tn(spread, result_low)
    grad_spread = nt(result_low, pooled_grad_ref[...])
    grad_logit = jnp.where(member, grad_spread * maps * (1.0 - maps), 0.0)
    lsum_ref[...] += total(grad_logit)
    glogit_ref[...] = grad_logit.astype(bf16)
    grad_pre = nt(glogit_ref[...], learn_out_ref[...]) * slope
    vsum_ref[6:7, :] += total(grad_pre)
    glearn_ref[...] = grad_pre.astype(bf16)
    back = nt(glearn_ref[...], learn_in_ref[...])
    unit, rstd = norm_parts(res_ref[...])
    vsum_ref[4:5, :] += total(back * unit)
    vsum_ref[5:6, :] += total(back)
    grad_result = matmul(spread, pooled_grad_ref[...]) + norm_back(back, unit, rstd, vec(4))
    vsum_ref[1:2, :] += total(grad_result)
    res_ref[...] = grad_result
    gres_ref[...] = grad_result.astype(bf16)

    def down_back(j, _):
        grad = nt(gres_ref[...], w_down_ref[columns(j), :]) * dgate_ref[:, columns(j)]
        usum_ref[:, columns(j)] += total(grad)
        gup_ref[:, columns(j)] = grad.astype(bf16)
        return 0

    lax.fori_loop(0, chunks, down_back, 0)
    back = nt(gup_ref[...], w_up_ref[...])
    unit, rstd = norm_parts(hid_ref[...])
    vsum_ref[2:3, :] += total(back * unit)
    vsum_ref[3:4, :] += total(back)
    grad_hidden = res_ref[...] + norm_back(back, unit, rstd, vec(2))
    vsum_ref[0:1, :] += total(grad_hidden)
    ghid_f32_ref[...] = grad_hidden
    ghid_ref[...] = grad_hidden.astype(bf16)
    grad = nt(ghid_ref[...], w_out_ref[...]).astype(bf16)
    wide = width // (count * splits)
    for i in range(count * splits):
        gatt[i][...] = grad[:, i * wide : (i + 1) * wide]


def rows_call(tok, img, attended, w_out, w_up, w_down, learn_in, learn_out, vecs, up_bias, out_bias, pooled_grad, splits):
    count, (rows, features) = len(attended), attended[0].shape
    local_rows, width = tok.shape
    hidden_units = w_up.shape[1]
    inner = learn_in.shape[1]
    spread = learn_out.shape[1]
    block = min(ROW_BLOCK, rows)
    chunk = 512
    wide = features // splits
    once = lambda a: pl.BlockSpec(a.shape, lambda i: (0,) * a.ndim, pipeline_mode=pl.Buffered(1))
    by_rows = lambda n: pl.BlockSpec((block, n), lambda i: (i, 0))
    kept = lambda a: pl.BlockSpec(a.shape, lambda i: (0, 0))
    low = lambda n: jax.ShapeDtypeStruct((rows, n), bf16)
    lows = [width, hidden_units, hidden_units, width, width, inner, inner, spread, width]
    sums = [
        jax.ShapeDtypeStruct((spread, width), f32),
        jax.ShapeDtypeStruct((8, width), f32),
        jax.ShapeDtypeStruct((1, hidden_units), f32),
        jax.ShapeDtypeStruct((1, spread), f32),
    ]
    resident = [w_out, w_up, w_down, learn_in, learn_out, vecs, up_bias, out_bias, pooled_grad]
    return pl.pallas_call(
        functools.partial(rows_kernel, count, splits, local_rows),
        grid=(rows // block,),
        in_specs=[by_rows(width), by_rows(1)]
        + [once(a) for a in resident]
        + [by_rows(features)] * count,
        out_specs=[by_rows(n) for n in lows]
        + [by_rows(width)]
        + [by_rows(wide)] * (count * splits)
        + [kept(a) for a in sums],
        out_shape=[low(n) for n in lows]
        + [jax.ShapeDtypeStruct((rows, width), f32)]
        + [low(wide)] * (count * splits)
        + sums,
        scratch_shapes=[
            pltpu.VMEM((block, width), f32),
            pltpu.VMEM((block, width), f32),
            pltpu.VMEM((block, hidden_units), f32),
            pltpu.VMEM((block, chunk), f32),
            pltpu.VMEM((block, chunk), f32),
        ],
        compiler_params=params(),
        cost_estimate=pl.CostEstimate(
            flops=4 * rows * width * (width + 2 * hidden_units + inner),
            bytes_accessed=2 * (rows * 20 * width + 2 * width * hidden_units),
            transcendentals=0,
        ),
    )(tok, img, *resident, *attended)


def grad_kernel(waits, left_ref, right_ref, *refs):
    refs[waits][...] = tn(left_ref[...], right_ref[...]).astype(bf16)


def grad_call(left, right, by_left, after=()):
    rows, m = left.shape
    n = right.shape[1]
    once = pl.Buffered(1)
    if by_left:
        grid, left_block, right_block, out_block = m // GRAD_BLOCK, GRAD_BLOCK, n, (GRAD_BLOCK, n)
        specs = [
            pl.BlockSpec((rows, left_block), lambda j: (0, j)),
            pl.BlockSpec((rows, right_block), lambda j: (0, 0), pipeline_mode=once),
        ]
        out_spec = pl.BlockSpec(out_block, lambda j: (j, 0))
    else:
        grid, left_block, right_block, out_block = n // GRAD_BLOCK, m, GRAD_BLOCK, (m, GRAD_BLOCK)
        specs = [
            pl.BlockSpec((rows, left_block), lambda j: (0, 0), pipeline_mode=once),
            pl.BlockSpec((rows, right_block), lambda j: (0, j)),
        ]
        out_spec = pl.BlockSpec(out_block, lambda j: (0, j))
    return pl.pallas_call(
        functools.partial(grad_kernel, len(after)),
        grid=(grid,),
        in_specs=specs + [ANYWHERE] * len(after),
        out_specs=out_spec,
        out_shape=jax.ShapeDtypeStruct((m, n), bf16),
        compiler_params=params(),
        cost_estimate=pl.CostEstimate(
            flops=3 * rows * m * n, bytes_accessed=4 * m * n, transcendentals=0
        ),
    )(left, right, *after)


def small_grad_kernel(count, waits, me_ref, *refs):
    n3_ref, glearn_ref, ghid_ref, inner_ref, glogit_ref = refs[:5]
    attended = refs[5 : 5 + count]
    out_ref, lout_ref = refs[5 + count + waits :]
    learn_columns = glearn_ref.shape[1]
    out_ref[:, :learn_columns] = tn(n3_ref[...], glearn_ref[...]).astype(bf16)
    lout_ref[...] = tn(inner_ref[...], glogit_ref[...])
    features = attended[0].shape[1]
    for d in range(count):
        owner = jnp.bitwise_xor(me_ref[0], d)
        to = pl.ds(pl.multiple_of(owner * features, features), features)
        out_ref[to, learn_columns:] = tn(attended[d][...], ghid_ref[...]).astype(bf16)


def small_grad_call(me, n3, glearn, ghid, inner, glogit, attended, after=()):
    rows, width = n3.shape
    operands = [n3, glearn, ghid, inner, glogit, *attended]
    out = jax.ShapeDtypeStruct((width, glearn.shape[1] + ghid.shape[1]), bf16)
    lout = jax.ShapeDtypeStruct((inner.shape[1], glogit.shape[1]), f32)
    once = lambda a: pl.BlockSpec(a.shape, lambda j, m: (0, 0), pipeline_mode=pl.Buffered(1))
    return pl.pallas_call(
        functools.partial(small_grad_kernel, len(attended), len(after)),
        grid_spec=pltpu.PrefetchScalarGridSpec(
            num_scalar_prefetch=1,
            grid=(1,),
            in_specs=[once(a) for a in operands] + [ANYWHERE] * len(after),
            out_specs=[once(out), once(lout)],
        ),
        out_shape=[out, lout],
        compiler_params=params(),
        cost_estimate=pl.CostEstimate(
            flops=6 * rows * width * width, bytes_accessed=20 * width * width, transcendentals=0
        ),
    )(me, *operands, *after)


def qkv_grad_kernel(groups, splits, waits, n_ref, *refs):
    parts = refs[: groups * splits]
    out_ref, acc_ref = refs[groups * splits + waits :]
    step = pl.program_id(0)
    columns = parts[0].shape[2]
    for d in range(2 * groups):

        @pl.when(step == d)
        def _():
            for s in range(splits):
                at = slice(s * columns, (s + 1) * columns)
                part = tn(n_ref[0], parts[s * groups + d // 2][d % 2])
                acc_ref[:, at] = part if d == 0 else acc_ref[:, at] + part

    @pl.when(step == 2 * groups - 1)
    def _():
        out_ref[...] = acc_ref[...].astype(bf16)


def qkv_grad_call(normed, parts, splits, after=()):
    count, rows, width = normed.shape
    columns = parts[0].shape[2] * splits
    once = lambda a: pl.BlockSpec(a.shape, lambda d: (0, 0, 0), pipeline_mode=pl.Buffered(1))
    return pl.pallas_call(
        functools.partial(qkv_grad_kernel, count // 2, splits, len(after)),
        grid=(count,),
        in_specs=[pl.BlockSpec((1, rows, width), lambda d: (d, 0, 0))]
        + [once(a) for a in parts]
        + [ANYWHERE] * len(after),
        out_specs=pl.BlockSpec((width, columns), lambda d: (0, 0)),
        out_shape=jax.ShapeDtypeStruct((width, columns), bf16),
        scratch_shapes=[pltpu.VMEM((width, columns), f32)],
        compiler_params=params(),
        cost_estimate=pl.CostEstimate(
            flops=3 * count * rows * width * columns,
            bytes_accessed=2 * count * rows * width,
            transcendentals=0,
        ),
    )(normed, *parts, *after)


def norm_sums_kernel(count, splits, local_rows, waits, me_ref, *refs):
    groups = count // 2
    pieces, parts = refs[:count], refs[count : count + groups * splits]
    at = count + groups * splits
    columns, (sums_ref, w_ref) = refs[at : at + 3 * splits], refs[at + 3 * splits + waits :]
    wide = columns[0].shape[1]
    block = pl.program_id(0)

    @pl.when(block == 0)
    def _():
        sums_ref[...] = jnp.zeros_like(sums_ref)
        for i, ref in enumerate(columns):
            w_ref[:, i * wide : (i + 1) * wide] = ref[...]

    unit, _ = norm_parts(load_block(pieces, block, BLK // count, local_rows))
    mixed = jnp.concatenate(
        [
            jnp.concatenate(
                [parts[s * groups + d // 2][d % 2] for d in range(count)], axis=0
            )
            for s in range(splits)
        ],
        axis=1,
    )
    back = nt(mixed, w_ref[...])
    sums_ref[0:1, :] += total(back * unit)
    sums_ref[1:2, :] += total(back)


def norm_sums_call(me, pieces, parts, w_qkv, after=()):
    count, (local_rows, width) = len(pieces), pieces[0].shape
    splits, columns = 2 * len(parts) // count, parts[0].shape[2]
    piece_rows = BLK // count
    blocks = parts[0].shape[1] // piece_rows
    specs, operands = own_columns(w_qkv, me, width // count, splits)
    return pl.pallas_call(
        functools.partial(norm_sums_kernel, count, splits, local_rows, len(after)),
        grid_spec=pltpu.PrefetchScalarGridSpec(
            num_scalar_prefetch=1,
            grid=(blocks,),
            in_specs=[pl.BlockSpec((piece_rows, width), lambda b, m: (b, 0))] * count
            + [pl.BlockSpec((2, piece_rows, columns), lambda b, m: (0, b, 0))] * len(parts)
            + specs
            + [ANYWHERE] * len(after),
            out_specs=pl.BlockSpec((8, width), lambda b, m: (0, 0)),
            scratch_shapes=[pltpu.VMEM((width, columns * splits), bf16)],
        ),
        out_shape=jax.ShapeDtypeStruct((8, width), f32),
        compiler_params=params(),
        cost_estimate=pl.CostEstimate(
            flops=4 * blocks * BLK * width * columns * splits,
            bytes_accessed=2 * blocks * BLK * width,
            transcendentals=0,
        ),
    )(me, *pieces, *parts, *operands, *after)


def tokens_kernel(groups, splits, me_ref, tok_ref, ghid_ref, w_ref, gain_ref, *refs):
    same, other = refs[: groups * splits], refs[groups * splits : groups * splits + splits]
    out_ref, mixed_ref = refs[groups * splits + splits :]
    width = tok_ref.shape[1]
    features = width // (2 * groups)
    wide = features // splits
    for d in range(2 * groups):
        owner = jnp.bitwise_xor(me_ref[0], d) * features
        for s in range(splits):
            for part in range(3):
                to = pl.ds(pl.multiple_of(part * width + owner + s * wide, wide), wide)
                at = slice(part * wide, (part + 1) * wide)
                if d % 2 == 0:
                    mixed_ref[:, to] = same[s * groups + d // 2][0, :, at]
                else:
                    mixed_ref[:, to] = other[s][d // 2, :, at]
    back = nt(mixed_ref[...], w_ref[...])
    unit, rstd = norm_parts(tok_ref[...].astype(f32))
    out_ref[0] = ghid_ref[...] + norm_back(back, unit, rstd, gain_ref[...])


def tokens_call(me, tok, ghid, w_qkv, gain, same, other, count):
    local_rows, width = tok.shape
    columns = same[0].shape[2]
    groups, splits = count // 2, len(other)
    block = 256
    by_rows = lambda n: pl.BlockSpec((block, n), lambda i, m: (i, 0))
    return pl.pallas_call(
        functools.partial(tokens_kernel, groups, splits),
        grid_spec=pltpu.PrefetchScalarGridSpec(
            num_scalar_prefetch=1,
            grid=(pl.cdiv(local_rows, block),),
            in_specs=[
                by_rows(width),
                by_rows(width),
                pl.BlockSpec(w_qkv.shape, lambda i, m: (0, 0), pipeline_mode=pl.Buffered(1)),
                pl.BlockSpec(gain.shape, lambda i, m: (0, 0)),
            ]
            + [pl.BlockSpec((1, block, columns), lambda i, m: (0, i, 0))] * len(same)
            + [pl.BlockSpec((groups, block, columns), lambda i, m: (0, i, 0))] * splits,
            out_specs=pl.BlockSpec((1, block, width), lambda i, m: (0, i, 0)),
            scratch_shapes=[pltpu.VMEM((block, 3 * width), bf16)],
        ),
        out_shape=jax.ShapeDtypeStruct((1, local_rows, width), f32),
        compiler_params=params(),
        cost_estimate=pl.CostEstimate(
            flops=12 * local_rows * width * width,
            bytes_accessed=local_rows * width * 16,
            transcendentals=0,
        ),
    )(me, tok, ghid, w_qkv, gain, *same, *other)


def flip(index, bit):
    return index + bit - 2 * bit * ((index // bit) % 2)


def vectors_kernel(count, row_bits, img_bits, vec_ref, slot_ref, out_ref, sum_ref, *scratch):
    recv, slot_recv, send_sem, recv_sem, slot_send, slot_got = scratch
    row, img = lax.axis_index("row"), lax.axis_index("img")

    def partner(row_mask, img_mask=0):
        r, g = row, img
        for bit in row_bits:
            r = flip(r, bit) if row_mask & bit else r
        for bit in img_bits:
            g = flip(g, bit) if img_mask & bit else g
        return (g, r)

    steps = [(bit, 0) for bit in row_bits] + [(0, bit) for bit in img_bits]
    everyone = sorted(set(steps) | {(d, 0) for d in range(1, count)})
    barrier = pltpu.get_barrier_semaphore()
    for masks in everyone:
        pl.semaphore_signal(
            barrier, inc=1, device_id=partner(*masks), device_id_type=pl.DeviceIdType.MESH
        )
    pl.semaphore_wait(barrier, len(everyone))
    slots = []
    for d in range(1, count):
        copy = pltpu.make_async_remote_copy(
            src_ref=slot_ref.at[d],
            dst_ref=slot_recv.at[d - 1],
            send_sem=slot_send.at[d - 1],
            recv_sem=slot_got.at[d - 1],
            device_id=partner(d),
            device_id_type=pl.DeviceIdType.MESH,
        )
        copy.start()
        slots.append(copy)
    out_ref[...] = vec_ref[...]
    for i, masks in enumerate(steps):
        copy = pltpu.make_async_remote_copy(
            src_ref=out_ref,
            dst_ref=recv.at[i],
            send_sem=send_sem.at[i],
            recv_sem=recv_sem.at[i],
            device_id=partner(*masks),
            device_id_type=pl.DeviceIdType.MESH,
        )
        copy.start()
        copy.wait()
        out_ref[...] = out_ref[...] + recv[i]
    for copy in slots:
        copy.wait()
    sum_ref[...] = tree(
        [slot_ref[0].astype(f32)] + [slot_recv[d - 1].astype(f32) for d in range(1, count)]
    )


def vectors_call(vec, slots):
    count = lax.axis_size("row")
    row_bits, img_bits = bits_of(count), bits_of(lax.axis_size("img"))
    steps = len(row_bits) + len(img_bits)
    whole = pl.BlockSpec(memory_space=pltpu.VMEM)
    return pl.pallas_call(
        functools.partial(vectors_kernel, count, row_bits, img_bits),
        in_specs=[whole, whole],
        out_specs=[whole, whole],
        out_shape=[
            jax.ShapeDtypeStruct(vec.shape, f32),
            jax.ShapeDtypeStruct(slots.shape[1:], f32),
        ],
        scratch_shapes=[
            pltpu.VMEM((steps,) + vec.shape, f32),
            pltpu.VMEM((count - 1,) + slots.shape[1:], bf16),
            pltpu.SemaphoreType.DMA((steps,)),
            pltpu.SemaphoreType.DMA((steps,)),
            pltpu.SemaphoreType.DMA((count - 1,)),
            pltpu.SemaphoreType.DMA((count - 1,)),
        ],
        compiler_params=pltpu.CompilerParams(
            collective_id=0, has_side_effects=True, vmem_limit_bytes=32 << 20
        ),
        cost_estimate=pl.CostEstimate(flops=1 << 33, bytes_accessed=1 << 20, transcendentals=0),
    )(vec, slots)


def rows_of(array, index, length):
    return lax.dynamic_slice_in_dim(array, index * length, length, 0)


def on_device(
    tokens,
    counts,
    owner,
    w_qkv,
    qv_bias,
    w_out,
    out_bias,
    w_up,
    up_bias,
    w_down,
    down_bias,
    norm_gain,
    norm_bias,
    learn_in,
    learn_in_bias,
    learn_out,
    learn_out_bias,
    cotangent,
):
    width = tokens.shape[2]
    local_rows = tokens.shape[1]
    row_count = lax.axis_size("row")
    images_count = lax.axis_size("img")
    device = lax.axis_index("row")
    image_device = lax.axis_index("img")
    features = width // row_count
    wide = min(features, 128)
    splits = features // wide
    slots_here = IMGS // row_count
    group_counts = counts[0]
    partners = [device ^ d for d in range(row_count)]
    row_bits, img_bits = stages()
    n_img = len(img_bits)

    pieces = gather_pieces(tokens[0])
    grads_in = gather_pieces(cotangent[0].reshape(slots_here, LT * width).astype(bf16))

    piece_rows = BLK // row_count
    blocks = pl.cdiv(local_rows, piece_rows)
    images = jnp.stack([row_images(group_counts, p, local_rows, row_count) for p in partners])
    extra = blocks * piece_rows - local_rows
    images = jnp.pad(images, ((0, 0), (0, extra)), constant_values=IMGS + 1)
    image_here = images[0].reshape(-1, 1)
    images = images.reshape(row_count, blocks, piece_rows).transpose(1, 0, 2).reshape(blocks, BLK)
    least, most = jnp.min(images, axis=1), jnp.max(images, axis=1)
    lo = jnp.sum((most[None, :] < least[:, None]).astype(jnp.int32), axis=1)
    hi = jnp.sum((least[None, :] <= most[:, None]).astype(jnp.int32), axis=1)
    imgq, imgk = images.reshape(1, -1), images.reshape(-1, 1)

    me = device.reshape(1)
    w_out_here = jnp.concatenate([rows_of(w_out, p, features) for p in partners], axis=0)
    bias_here = lax.dynamic_slice_in_dim(qv_bias, device * features, features, 1)

    normed, q, k, v, kt, vt = qkv_call(
        me, pieces, w_qkv, bias_here, norm_gain[0:1], norm_bias[0:1], splits
    )
    *attended, ot, lse = attend_call(q, k, vt, imgq, imgk, lo, hi, row_count)
    attended = send_pieces(attended)

    slot_rel = ((owner[0] // slots_here) ^ device) * slots_here + owner[0] % slots_here
    select = (slot_rel[:, None] == jnp.arange(IMGS, dtype=jnp.int32)[None, :]).astype(f32)
    scale = lax.rsqrt(group_counts.astype(f32))
    incoming = jnp.concatenate(grads_in, axis=0).astype(f32)
    grad_pooled = jnp.dot(select, incoming, precision=highest) * scale[:, None]
    grad_pooled_low = grad_pooled.reshape(IMGS * LT, width).astype(bf16)

    vecs = jnp.concatenate(
        [
            out_bias[None],
            down_bias[None],
            norm_gain[1:2],
            norm_bias[1:2],
            norm_gain[2:3],
            norm_bias[2:3],
            learn_in_bias[None],
            jnp.zeros((1, width), f32),
        ],
        axis=0,
    )
    out = rows_call(
        tokens[0],
        image_here,
        attended,
        w_out_here,
        w_up,
        w_down,
        learn_in,
        jnp.tile(learn_out, (1, IMGS)),
        vecs,
        up_bias[None],
        jnp.tile(learn_out_bias, IMGS)[None],
        grad_pooled_low,
        splits,
    )
    n2, gated, gup, gres, n3, glearn, inner, glogit, ghid, grad_hidden = out[:10]
    grad_attended = out[10 : 10 + row_count * splits]
    pooled, vec_sums, up_sums, logit_sums = out[10 + row_count * splits :]
    grad_attended = [send_pieces(grad_attended[s::splits]) for s in range(splits)]

    core, far_row = row_bits[:1], row_bits[1:]
    y_bits, z_bits = img_bits[:1], [[bit] for bit in img_bits[1:]]
    stage = lambda value, bits, after=(): reduce_stage(value, bits, n_img, after)
    stack_other = lambda groups: jump(jnp.stack([g[1] for g in groups]), 1)

    small, grad_learn_out = small_grad_call(me, n3, glearn, ghid, inner, glogit, attended)
    small = spread_img(small)
    grad_down = grad_call(gated, gres, True, [small])
    small = stage(small, core, [grad_down])
    grad_up = grad_call(n2, gup, False, [grad_down, small])
    down = stage(spread_img(grad_down), core, [grad_up])

    def back_call(s, after):
        *parts, sums = attend_back_call(
            grad_attended[s], q, k, v, kt, ot, lse, imgq, imgk, lo, hi, s, after
        )
        return parts, sums

    mixed, same, other, qkv_sums = [], [], [], []
    ups = spread_img(grad_up)
    for s in range(splits):
        parts, sums = back_call(s, [down, ups] if s == 0 else [small, ups, down])
        mixed += parts
        qkv_sums.append(sums[0:2])
        here = [parts[0]] + [jump(parts[g], 2 * g) for g in range(1, len(parts))]
        if s == 0:
            small = stage(small, y_bits, [sums])
            ups = stage(ups, core, [sums])
            down = stage(down, far_row, [sums])
            first = here
    if splits > 1:
        first = [first[0]] + [behind(h, [sums]) for h in first[1:]]
        same = first + here
    else:
        same = here
    ups = stage(ups, y_bits, [sums])
    down = stage(down, z_bits[0], [sums])
    small = stage(small, z_bits[0], [sums])
    other = [stack_other(first)]
    grad_qkv = qkv_grad_call(normed, mixed, splits, [down, ups, small])
    if splits > 1:
        other.append(stack_other([here[0]] + [behind(h, [grad_qkv]) for h in here[1:]]))
    norm_sums = norm_sums_call(me, pieces, mixed, w_qkv, [grad_qkv])
    down = stage(down, z_bits[1], [norm_sums])
    small = stage(small, z_bits[1], [norm_sums])
    ups = stage(ups, z_bits[0], [norm_sums])
    grad_qkv = stage(spread_img(grad_qkv), y_bits, [norm_sums])
    for bits in z_bits[1:]:
        ups = stage(ups, bits)
    for bits in z_bits[2:]:
        down = stage(down, bits)
        small = stage(small, bits)
    down = stage(down, y_bits)
    for bits in z_bits:
        grad_qkv = stage(grad_qkv, bits)
    grad_tokens = tokens_call(
        me, tokens[0], grad_hidden, w_qkv, norm_gain[0:1], same, other, row_count
    )

    by_slot = jnp.dot(select.T, pooled.reshape(IMGS, LT * width), precision=highest)
    by_slot = by_slot.astype(bf16).reshape(row_count, -1, 128)
    late = lax.dynamic_update_slice(
        jnp.zeros((2, width), f32), jnp.concatenate(qkv_sums, axis=1), (0, device * features)
    )
    vectors = jnp.concatenate(
        [
            up_sums.reshape(-1),
            vec_sums.reshape(-1),
            jnp.sum(grad_learn_out.reshape(-1, IMGS, LT), axis=1).reshape(-1),
            late.reshape(-1),
            norm_sums[0:2].reshape(-1),
            jnp.sum(logit_sums.reshape(IMGS, LT), axis=0),
        ]
    )
    vectors = jnp.pad(vectors, (0, -vectors.shape[0] % 1024)).reshape(-1, 128)
    vectors, learned = vectors_call(vectors, by_slot)
    vectors = vectors.reshape(-1)
    scale_here = jnp.dot(scale, select, precision=highest)[:slots_here]
    learned = learned.reshape(slots_here, LT * width) * scale_here[:, None]
    learned = learned.reshape(1, slots_here, LT, width)

    share_down = finish_weight(down, row_bits)
    share_small = finish_weight(exchange_sum(small, far_row), core)
    share_up = finish_weight(exchange_sum(ups, far_row), core)
    share_learn = share_small[:, : learn_in.shape[1]]
    share_out = share_small[:, learn_in.shape[1] :]
    shares = gather_columns(grad_qkv.reshape(grad_qkv.shape[-2:]), lambda c: c, row_bits)
    share_qkv = jnp.concatenate(
        [
            shares[c][:, (3 * s + part) * wide : (3 * s + part + 1) * wide]
            for part in range(3)
            for c in range(row_count)
            for s in range(splits)
        ],
        axis=1,
    ).astype(f32)

    at = up_bias.shape[0]
    up_sum, vec_sums = vectors[:at], vectors[at : at + 8 * width].reshape(8, width)
    at += 8 * width
    learn_out_sum = vectors[at : at + learn_out.size].reshape(learn_out.shape)
    at += learn_out.size
    late = vectors[at : at + 4 * width].reshape(4, width)
    at += 4 * width
    out_sum, down_sum, gain_two, shift_two, gain_three, shift_three, learn_in_sum = vec_sums[:7]
    share_learn_out = rows_of(learn_out_sum, image_device, learn_out.shape[0] // images_count)
    return (
        learned,
        grad_tokens,
        share_qkv,
        late[0:2],
        share_out,
        out_sum,
        share_up,
        up_sum,
        share_down,
        down_sum,
        jnp.stack([late[2], gain_two, gain_three]),
        jnp.stack([late[3], shift_two, shift_three]),
        share_learn,
        learn_in_sum,
        share_learn_out,
        vectors[at : at + learn_out.shape[1]],
    )


def solution(mesh):
    by_image = P("img", None)
    in_specs = (
        (P("img", "row", None), by_image, by_image) + (P(),) * 14 + (P("img", "row", None, None),)
    )
    out_specs = (
        P("img", "row", None, None),
        P("img", "row", None),
        by_image,
        P(),
        by_image,
        P(),
        by_image,
        P(),
        by_image,
        P(),
        P(),
        P(),
        by_image,
        P(),
        by_image,
        P(),
    )
    return jax.shard_map(
        on_device, mesh=mesh, in_specs=in_specs, out_specs=out_specs, check_vma=False
    )
```

```python
import functools

import jax
import jax.numpy as jnp
from jax import lax
from jax.experimental import pallas as pl
from jax.experimental.pallas import tpu as pltpu
from jax.sharding import PartitionSpec as P

HEADS = 16
HEAD = 64
LT = 8
IMGS = 8
BLK = 256
NEG = -1e30
VMEM = 60 << 20
ROW_BLOCK = 256
UP_BLOCK = 1024
GRAD_BLOCK = 1024

highest = lax.Precision.HIGHEST
epsilon = 1e-06
f32 = jnp.float32
bf16 = jnp.bfloat16


def smooth_both(v):
    half = jnp.abs(v) * 0.7071067811865476
    t = 1.0 / (1.0 + 0.3275911 * half)
    bell = jnp.exp(-half * half)
    poly = t * (
        0.127414796
        + t * (-0.142248368 + t * (0.7107068705 + t * (-0.7265760135 + t * 0.5307027145)))
    )
    tail = poly * bell
    cdf = jnp.where(v >= 0.0, 1.0 - tail, tail)
    return v * cdf, cdf + v * (bell * 0.3989422804014327)


def matmul(left, right):
    return jnp.dot(left, right, preferred_element_type=f32)


def nt(left, right):
    return lax.dot_general(left, right, (((1,), (1,)), ((), ())), preferred_element_type=f32)


def tn(left, right):
    return lax.dot_general(left, right, (((0,), (0,)), ((), ())), preferred_element_type=f32)


def row_images(counts, device, local_rows, row_count):
    upper_end = counts * (device + 1) // row_count
    lower_end = counts * device // row_count
    run_ends = jnp.cumsum(upper_end - lower_end)
    positions = jnp.arange(local_rows, dtype=jnp.int32)
    return jnp.sum((positions[:, None] >= run_ends[None, :]).astype(jnp.int32), axis=1)


def bits_of(size):
    return [1 << i for i in range(size.bit_length() - 1)]


def jump(value, row_mask, img_mask=0):
    rows, imgs = lax.axis_size("row"), lax.axis_size("img")
    if img_mask == 0:
        return lax.ppermute(value, "row", [(i, i ^ row_mask) for i in range(rows)])
    if row_mask == 0:
        return lax.ppermute(value, "img", [(i, i ^ img_mask) for i in range(imgs)])
    mask = img_mask * rows + row_mask
    return lax.ppermute(value, ("img", "row"), [(i, i ^ mask) for i in range(rows * imgs)])


def masks_of(bits):
    masks = []
    for e in range(1 << len(bits)):
        masks.append(
            tuple(
                sum(bit for j, (axis, bit) in enumerate(bits) if axis == name and e >> j & 1)
                for name in ("row", "img")
            )
        )
    return masks


def gather_pieces(value, after=()):
    pieces = {0: value}
    order = sorted(range(1, lax.axis_size("row")), key=lambda d: (d & 1, d))
    for d in order:
        low = d & -d
        pieces[d] = jump(pieces[d ^ low], low)
        if d % 2 == 0:
            pieces[d] = behind(pieces[d], after)
    return [pieces[d] for d in range(lax.axis_size("row"))]


def send_pieces(pieces):
    far_first = sorted(range(1, len(pieces)), reverse=True)
    arrived = {d: jump(pieces[d], d) for d in far_first}
    return [pieces[0]] + [arrived[d] for d in range(1, len(pieces))]


def stages():
    row_bits = [("row", b) for b in bits_of(lax.axis_size("row"))]
    img_bits = [("img", b) for b in bits_of(lax.axis_size("img"))]
    return row_bits, img_bits


def tree(values):
    while len(values) > 1:
        values = [values[i] + values[i + 1] for i in range(0, len(values), 2)]
    return values[0]


def behind(value, after):
    return lax.optimization_barrier((value, *after))[0] if after else value


def reduce_stage(value, bits, img_count, after=()):
    mine = {"row": lax.axis_index("row"), "img": lax.axis_index("img")}

    def part(e):
        piece = value
        for j, (axis, bit) in enumerate(bits):
            want = (mine[axis] // bit) % 2 ^ (e >> j & 1)
            dim = value.ndim - 1 if axis == "row" else img_count - bit.bit_length()
            length = piece.shape[dim] // 2
            piece = lax.dynamic_slice_in_dim(piece, want * length, length, dim)
        return piece

    masks = masks_of(bits)
    arrived = {
        e: behind(jump(part(e), *masks[e]), after) for e in reversed(range(1, len(masks)))
    }
    arrived[0] = part(0)
    return tree([arrived[e].astype(f32) for e in range(len(masks))]).astype(bf16)


def spread_img(grad):
    rows, columns = grad.shape
    images = lax.axis_size("img")
    return grad.reshape((2,) * len(bits_of(images)) + (rows // images, columns))


def gather_columns(value, order, bits, after=()):
    masks = [row_mask for row_mask, _ in masks_of(bits)]
    device = lax.axis_index("row") % len(masks)
    stack = jnp.stack([value if m == 0 else behind(jump(value, m), after) for m in masks])
    return [
        lax.dynamic_index_in_dim(stack, order(c) ^ device, 0, False) for c in range(len(masks))
    ]


def exchange_sum(value, bits, after=()):
    values = [value] + [behind(jump(value, *mask), after) for mask in masks_of(bits)[1:]]
    return tree([v.astype(f32) for v in values]).astype(bf16)


def reversed_bits(index, size):
    width = size.bit_length() - 1
    return int(format(index, f"0{width}b")[::-1], 2) if width else 0


def finish_weight(value, bits, after=()):
    value = value.reshape(value.shape[-2:])
    count = 1 << len(bits)
    blocks = gather_columns(value, lambda c: reversed_bits(c, count), bits, after)
    return jnp.concatenate(blocks, axis=1).astype(f32)


def params(flags=("arbitrary",)):
    return pltpu.CompilerParams(dimension_semantics=flags, vmem_limit_bytes=VMEM)


ANYWHERE = pl.BlockSpec(memory_space=pl.ANY)


def own_columns(w_qkv, features, splits, chosen):
    width = w_qkv.shape[0]
    wide = features // splits

    def spec(s, part):
        def index(b, me):
            return 0, part * (width // wide) + me[0] * splits + s

        return pl.BlockSpec((width, wide), index, pipeline_mode=pl.Buffered(1))

    return [spec(s, part) for s in chosen for part in range(3)], [w_qkv] * (3 * len(chosen))


def valid_rows(block, piece_rows, local_rows):
    position = lax.broadcasted_iota(jnp.int32, (BLK, 1), 0) % piece_rows + block * piece_rows
    return position < local_rows


def load_block(refs, block, piece_rows, local_rows):
    value = jnp.concatenate([ref[...] for ref in refs], axis=0).astype(f32)
    return jnp.where(valid_rows(block, piece_rows, local_rows), value, 0.0)


def norm_parts(value):
    centre = value - jnp.mean(value, axis=-1, keepdims=True)
    rstd = lax.rsqrt(jnp.mean(centre * centre, axis=-1, keepdims=True) + epsilon)
    return centre * rstd, rstd


def qkv_kernel(count, splits, local_rows, features, me_ref, *refs):
    n_w = 3 * splits
    pieces, columns = refs[:count], refs[count : count + n_w]
    bias_ref, gain_ref, shift_ref = refs[count + n_w : count + n_w + 3]
    n_ref, q_ref, k_ref, v_ref, kt_ref, vt_ref, w_ref = refs[count + n_w + 3 :]
    block = pl.program_id(0)
    wide = features // splits

    @pl.when(block == 0)
    def _():
        for i, ref in enumerate(columns):
            w_ref[:, i * wide : (i + 1) * wide] = ref[...]

    unit, _ = norm_parts(load_block(pieces, block, BLK // count, local_rows))
    normed = (unit * gain_ref[...] + shift_ref[...]).astype(bf16)
    n_ref[...] = unit.astype(bf16).reshape(n_ref.shape)
    mixed = matmul(normed, w_ref[...])
    for s in range(splits):
        at = slice(s * wide, (s + 1) * wide)
        part = mixed[:, 3 * s * wide : 3 * (s + 1) * wide]
        keys = part[:, wide : 2 * wide]
        values = part[:, 2 * wide :] + bias_ref[1:2, at]
        q_ref[:, at] = ((part[:, :wide] + bias_ref[0:1, at]) * 0.125).astype(bf16)
        k_ref[:, at] = keys.astype(bf16)
        v_ref[:, at] = values.astype(bf16)
        kt_ref[0, at] = keys.T.astype(bf16)
        vt_ref[0, at] = values.T.astype(bf16)


def qkv_call(me, pieces, w_qkv, bias, gain, shift, splits):
    count, (local_rows, width) = len(pieces), pieces[0].shape
    features = width // count
    piece_rows = BLK // count
    blocks = pl.cdiv(local_rows, piece_rows)
    whole = lambda a: pl.BlockSpec(a.shape, lambda b, m: (0,) * a.ndim)
    flat = pl.BlockSpec((BLK, features), lambda b, m: (b, 0))
    turned = pl.BlockSpec((1, features, BLK), lambda b, m: (b, 0, 0))
    specs, operands = own_columns(w_qkv, features, splits, range(splits))
    return pl.pallas_call(
        functools.partial(qkv_kernel, count, splits, local_rows, features),
        grid_spec=pltpu.PrefetchScalarGridSpec(
            num_scalar_prefetch=1,
            grid=(blocks,),
            in_specs=[pl.BlockSpec((piece_rows, width), lambda b, m: (b, 0))] * count
            + specs
            + [whole(bias), whole(gain), whole(shift)],
            out_specs=[
                pl.BlockSpec((count, piece_rows, width), lambda b, m: (0, b, 0)),
                flat,
                flat,
                flat,
                turned,
                turned,
            ],
            scratch_shapes=[pltpu.VMEM((width, 3 * features), bf16)],
        ),
        out_shape=[jax.ShapeDtypeStruct((count, blocks * piece_rows, width), bf16)]
        + [jax.ShapeDtypeStruct((blocks * BLK, features), bf16)] * 3
        + [jax.ShapeDtypeStruct((blocks, features, BLK), bf16)] * 2,
        compiler_params=params(),
        cost_estimate=pl.CostEstimate(
            flops=6 * blocks * BLK * width * 3 * features,
            bytes_accessed=2 * blocks * BLK * (2 * width + 5 * features),
            transcendentals=0,
        ),
    )(me, *pieces, *operands, bias, gain, shift)


def per_head(stack_ref, value, heads):
    lane = lax.broadcasted_iota(jnp.int32, value.shape, 1) // HEAD
    for h in range(heads):
        stack_ref[h * BLK : (h + 1) * BLK] = jnp.where(lane == h, value, jnp.zeros_like(value))


def in_pairs(lo, hi, step, carry):
    pairs = (hi - lo) // 2
    carry = lax.fori_loop(0, pairs, lambda i, c: step(lo + 2 * i, 2, c), carry)
    return lax.fori_loop(lo + 2 * pairs, hi, lambda kb, c: step(kb, 1, c), carry)


def attend_kernel(count, heads, lo_ref, hi_ref, *refs):
    q_ref, k_ref, vt_ref, imgq_ref, imgk_ref = refs[:5]
    outs, (ot_ref, lse_ref) = refs[5 : 5 + count], refs[5 + count : 7 + count]
    s_ref, qs_ref, acc_ref = refs[7 + count :]
    block = pl.program_id(0)
    lo, hi = lo_ref[block], hi_ref[block]
    per_head(qs_ref, q_ref[...], heads)
    imgq = imgq_ref[...]

    def first(kb, width, tops):
        rows = pl.ds(pl.multiple_of(kb * BLK, BLK), width * BLK)
        allowed = imgk_ref[rows, :] == imgq
        s = nt(k_ref[rows, :], qs_ref[...])
        new = []
        for h in range(heads):
            cols = slice(h * BLK, (h + 1) * BLK)
            part = jnp.where(allowed, s[:, cols], NEG)
            for j in range(width):
                s_ref[kb - lo + j, :, cols] = part[j * BLK : (j + 1) * BLK]
            high = jnp.max(part.reshape(width * BLK // 8, 8, BLK), axis=0)
            new.append(jnp.maximum(tops[h], high))
        return tuple(new)

    tops = in_pairs(lo, hi, first, (jnp.full((8, BLK), NEG, f32),) * heads)
    tops = [jnp.max(t, axis=0, keepdims=True) for t in tops]
    acc_ref[...] = jnp.zeros_like(acc_ref)

    def second(kb, width, sums):
        new = []
        for h in range(heads):
            rows, cols = slice(h * HEAD, (h + 1) * HEAD), slice(h * BLK, (h + 1) * BLK)
            part, weights = 0.0, sums[h]
            for j in range(width):
                p = jnp.exp(s_ref[kb - lo + j, :, cols] - tops[h])
                weights = weights + jnp.sum(p.reshape(BLK // 8, 8, BLK), axis=0)
                part = part + matmul(vt_ref[kb + j, rows, :], p.astype(bf16))
            new.append(weights)
            acc_ref[rows, :] += part
        return tuple(new)

    sums = in_pairs(lo, hi, second, (jnp.zeros((8, BLK), f32),) * heads)
    sums = [jnp.sum(t, axis=0, keepdims=True) for t in sums]
    for h in range(heads):
        rows = slice(h * HEAD, (h + 1) * HEAD)
        acc_ref[rows, :] = acc_ref[rows, :] / sums[h]
    lse_ref[...] = jnp.concatenate(
        [t + jnp.log(s) for t, s in zip(tops, sums)] + [jnp.zeros((8 - heads, BLK), f32)], axis=0
    )
    ot_ref[0] = acc_ref[...]
    out = acc_ref[...].T.astype(bf16)
    for d in range(count):
        outs[d][...] = out[d * (BLK // count) : (d + 1) * (BLK // count)]


def attend_call(q, k, vt, imgq, imgk, lo, hi, count):
    blocks, features = vt.shape[0], q.shape[1]
    heads = features // HEAD
    piece_rows = BLK // count
    whole = lambda a: pl.BlockSpec(
        a.shape, lambda b, *_: (0,) * a.ndim, pipeline_mode=pl.Buffered(1)
    )
    return pl.pallas_call(
        functools.partial(attend_kernel, count, heads),
        grid_spec=pltpu.PrefetchScalarGridSpec(
            num_scalar_prefetch=2,
            grid=(blocks,),
            in_specs=[
                pl.BlockSpec((BLK, features), lambda b, *_: (b, 0)),
                whole(k),
                whole(vt),
                pl.BlockSpec((1, BLK), lambda b, *_: (0, b)),
                whole(imgk),
            ],
            out_specs=[pl.BlockSpec((piece_rows, features), lambda b, *_: (b, 0))] * count
            + [
                pl.BlockSpec((1, features, BLK), lambda b, *_: (b, 0, 0)),
                pl.BlockSpec((8, BLK), lambda b, *_: (0, b)),
            ],
            scratch_shapes=[
                pltpu.VMEM((blocks, BLK, heads * BLK), f32),
                pltpu.VMEM((heads * BLK, features), bf16),
                pltpu.VMEM((features, BLK), f32),
            ],
        ),
        out_shape=[jax.ShapeDtypeStruct((blocks * piece_rows, features), bf16)] * count
        + [
            jax.ShapeDtypeStruct((blocks, features, BLK), f32),
            jax.ShapeDtypeStruct((8, blocks * BLK), f32),
        ],
        compiler_params=params(),
        cost_estimate=pl.CostEstimate(
            flops=10 * (blocks * BLK) ** 2 * features,
            bytes_accessed=2 * blocks * BLK * features * 8,
            transcendentals=0,
        ),
    )(lo, hi, q, k, vt, imgq, imgk)


def attend_back_kernel(count, heads, first, waits, lo_ref, hi_ref, *refs):
    pieces, refs = refs[:count], refs[:count] + refs[count + waits :]
    q_ref, k_ref, v_ref, kt_ref, ot_ref, lse_ref, imgq_ref, imgk_ref = refs[count : count + 8]
    groups = count // 2
    outs, sums_ref = refs[count + 8 : count + groups + 8], refs[count + groups + 8]
    qs_ref, dos_ref, p_ref, ds_ref, dqt_ref, dk_ref, dv_ref = refs[count + groups + 9 :]
    block = pl.program_id(0)
    lo, hi = lo_ref[block], hi_ref[block]
    piece_rows = BLK // count
    wide = heads * HEAD

    @pl.when(block == 0)
    def _():
        dk_ref[...] = jnp.zeros_like(dk_ref)
        dv_ref[...] = jnp.zeros_like(dv_ref)
        sums_ref[...] = jnp.zeros_like(sums_ref)

    grad = jnp.concatenate([ref[...] for ref in pieces], axis=0)
    query = q_ref[...]
    lane = lax.broadcasted_iota(jnp.int32, grad.shape, 1) // HEAD
    for h in range(heads):
        dos_ref[h * BLK : (h + 1) * BLK] = jnp.where(lane == h, grad, jnp.zeros_like(grad))
        qs_ref[h * BLK : (h + 1) * BLK] = jnp.where(lane == h, query, jnp.zeros_like(query))
    both = grad.astype(f32).T * ot_ref[0]
    delta = [
        jnp.sum(both[h * HEAD : (h + 1) * HEAD], axis=0, keepdims=True) for h in range(heads)
    ]
    logsum = [lse_ref[first + h : first + h + 1, :] for h in range(heads)]
    imgq = imgq_ref[...]
    dqt_ref[...] = jnp.zeros_like(dqt_ref)

    def step(kb, width):
        length = width * BLK
        rows = pl.ds(pl.multiple_of(kb * BLK, BLK), length)
        keys, values = k_ref[rows, :], v_ref[rows, :]
        allowed = imgk_ref[rows, :] == imgq
        s = nt(keys, qs_ref[...])
        dp = nt(values, dos_ref[...])
        for h in range(heads):
            cols = slice(h * BLK, (h + 1) * BLK)
            p = jnp.exp(jnp.where(allowed, s[:, cols] - logsum[h], NEG))
            p_ref[:length, cols] = p.astype(bf16)
            ds_ref[:length, cols] = (p * (dp[:, cols] - delta[h])).astype(bf16)
        dv_ref[rows, :] += matmul(p_ref[:length], dos_ref[...])
        dk_ref[rows, :] += matmul(ds_ref[:length], qs_ref[...])
        for h in range(heads):
            cols, feats = slice(h * BLK, (h + 1) * BLK), slice(h * HEAD, (h + 1) * HEAD)
            total = 0.0
            for j in range(width):
                ds = ds_ref[j * BLK : (j + 1) * BLK, cols]
                total = total + matmul(kt_ref[kb + j, feats, :], ds)
            dqt_ref[feats, :] += total

    def pair(i, _):
        step(lo + 2 * i, 2)
        return 0

    lax.fori_loop(0, (hi - lo) // 2, pair, 0)

    @pl.when((hi - lo) % 2 == 1)
    def _():
        step(hi - 1, 1)

    dq = dqt_ref[...].T * 0.125
    sums_ref[0:1, :] += jnp.sum(dq, axis=0, keepdims=True)
    here = pl.ds(pl.multiple_of(block * piece_rows, piece_rows), piece_rows)
    for d in range(count):
        outs[d // 2][d % 2, here, :wide] = dq[d * piece_rows : (d + 1) * piece_rows].astype(bf16)

    @pl.when(block == pl.num_programs(0) - 1)
    def _():
        sums_ref[1:2, :] = jnp.sum(dv_ref[...], axis=0, keepdims=True)

        def move(b, _):
            to = pl.ds(pl.multiple_of(b * piece_rows, piece_rows), piece_rows)
            for d in range(count):
                at = pl.ds(pl.multiple_of(b * BLK + d * piece_rows, piece_rows), piece_rows)
                outs[d // 2][d % 2, to, wide : 2 * wide] = dk_ref[at, :].astype(bf16)
                outs[d // 2][d % 2, to, 2 * wide :] = dv_ref[at, :].astype(bf16)
            return 0

        lax.fori_loop(0, pl.num_programs(0), move, 0)


def attend_back_call(pieces, q, k, v, kt, ot, lse, imgq, imgk, lo, hi, split, after):
    count, (rows, wide) = len(pieces), pieces[0].shape
    blocks = kt.shape[0]
    heads = wide // HEAD
    once = pl.Buffered(1)
    half = pl.BlockSpec((blocks * BLK, wide), lambda b, *_: (0, split), pipeline_mode=once)
    out = jax.ShapeDtypeStruct((2, rows, 3 * wide), bf16)
    return pl.pallas_call(
        functools.partial(attend_back_kernel, count, heads, split * heads, len(after)),
        grid_spec=pltpu.PrefetchScalarGridSpec(
            num_scalar_prefetch=2,
            grid=(blocks,),
            in_specs=[pl.BlockSpec((BLK // count, wide), lambda b, *_: (b, 0))] * count
            + [ANYWHERE] * len(after)
            + [
                pl.BlockSpec((BLK, wide), lambda b, *_: (b, split)),
                half,
                half,
                pl.BlockSpec((blocks, wide, BLK), lambda b, *_: (0, split, 0), pipeline_mode=once),
                pl.BlockSpec((1, wide, BLK), lambda b, *_: (b, split, 0)),
                pl.BlockSpec((8, BLK), lambda b, *_: (0, b)),
                pl.BlockSpec((1, BLK), lambda b, *_: (0, b)),
                pl.BlockSpec(imgk.shape, lambda b, *_: (0, 0), pipeline_mode=once),
            ],
            out_specs=[pl.BlockSpec(out.shape, lambda b, *_: (0, 0, 0), pipeline_mode=once)] * (count // 2)
            + [pl.BlockSpec((8, wide), lambda b, *_: (0, 0))],
            scratch_shapes=[
                pltpu.VMEM((heads * BLK, wide), bf16),
                pltpu.VMEM((heads * BLK, wide), bf16),
                pltpu.VMEM((2 * BLK, heads * BLK), bf16),
                pltpu.VMEM((2 * BLK, heads * BLK), bf16),
                pltpu.VMEM((wide, BLK), f32),
                pltpu.VMEM((blocks * BLK, wide), f32),
                pltpu.VMEM((blocks * BLK, wide), f32),
            ],
        ),
        out_shape=[out] * (count // 2) + [jax.ShapeDtypeStruct((8, wide), f32)],
        compiler_params=params(),
        cost_estimate=pl.CostEstimate(
            flops=16 * (blocks * BLK) ** 2 * wide,
            bytes_accessed=2 * blocks * BLK * wide * 12,
            transcendentals=0,
        ),
    )(lo, hi, *pieces, *after, q, k, v, kt, ot, lse, imgq, imgk)


def norm_back(grad, unit, rstd, gain):
    e = grad * gain
    mean = jnp.mean(e, axis=-1, keepdims=True)
    return (e - mean - unit * jnp.mean(e * unit, axis=-1, keepdims=True)) * rstd


def total(value):
    return jnp.sum(value, axis=0, keepdims=True)


def rows_kernel(count, splits, local_rows, *refs):
    (
        tok_ref,
        img_ref,
        w_out_ref,
        w_up_ref,
        w_down_ref,
        learn_in_ref,
        learn_out_ref,
        vec_ref,
        up_bias_ref,
        out_bias_ref,
        pooled_grad_ref,
    ) = refs[:11]
    attended = refs[11 : 11 + count]
    at = 11 + count
    (
        n2_ref,
        gated_ref,
        gup_ref,
        gres_ref,
        n3_ref,
        glearn_ref,
        inner_ref,
        glogit_ref,
        ghid_ref,
        ghid_f32_ref,
    ) = refs[at : at + 10]
    gatt = refs[at + 10 : at + 10 + count * splits]
    at += 10 + count * splits
    pooled_ref, vsum_ref, usum_ref, lsum_ref = refs[at : at + 4]
    hid_ref, res_ref, dgate_ref, up0_ref, up1_ref = refs[at + 4 :]
    step = pl.program_id(0)
    rows, width = tok_ref.shape
    hidden_units = w_up_ref.shape[1]
    chunk = up0_ref.shape[1]
    chunks = hidden_units // chunk

    @pl.when(step == 0)
    def _():
        for ref in (pooled_ref, vsum_ref, usum_ref, lsum_ref):
            ref[...] = jnp.zeros_like(ref)

    def vec(i):
        return vec_ref[i : i + 1, :]

    position = lax.broadcasted_iota(jnp.int32, (rows, 1), 0) + step * rows
    tok = jnp.where(position < local_rows, tok_ref[...].astype(f32), 0.0)
    low = jnp.concatenate([ref[...] for ref in attended], axis=1)
    hidden = tok + matmul(low, w_out_ref[...]) + vec(0)
    hid_ref[...] = hidden
    unit, _ = norm_parts(hidden)
    n2_ref[...] = (unit * vec(2) + vec(3)).astype(bf16)

    def columns(j):
        return pl.ds(pl.multiple_of(j * chunk, chunk), chunk)

    def up(ref, j):
        ref[...] = matmul(n2_ref[...], w_up_ref[:, columns(j)])

    def gate(ref, j):
        value, slope = smooth_both(ref[...] + up_bias_ref[:, columns(j)])
        gated_ref[:, columns(j)] = value.astype(bf16)
        dgate_ref[:, columns(j)] = slope

    up(up0_ref, 0)

    def pair(i, _):
        up(up1_ref, 2 * i + 1)
        gate(up0_ref, 2 * i)
        up(up0_ref, jnp.minimum(2 * i + 2, chunks - 1))
        gate(up1_ref, 2 * i + 1)
        return 0

    lax.fori_loop(0, chunks // 2, pair, 0)
    result = hid_ref[...] + matmul(gated_ref[...], w_down_ref[...]) + vec(1)
    res_ref[...] = result
    unit, rstd = norm_parts(result)
    n3_ref[...] = (unit * vec(4) + vec(5)).astype(bf16)
    inner, slope = smooth_both(matmul(n3_ref[...], learn_in_ref[...]) + vec(6))
    inner_ref[...] = inner.astype(bf16)
    maps = jax.nn.sigmoid(matmul(inner_ref[...], learn_out_ref[...]) + out_bias_ref[...])
    member = lax.broadcasted_iota(jnp.int32, maps.shape, 1) // LT == img_ref[...]
    spread = jnp.where(member, maps, 0.0).astype(bf16)
    result_low = res_ref[...].astype(bf16)
    pooled_ref[...] += tn(spread, result_low)
    grad_spread = nt(result_low, pooled_grad_ref[...])
    grad_logit = jnp.where(member, grad_spread * maps * (1.0 - maps), 0.0)
    lsum_ref[...] += total(grad_logit)
    glogit_ref[...] = grad_logit.astype(bf16)
    grad_pre = nt(glogit_ref[...], learn_out_ref[...]) * slope
    vsum_ref[6:7, :] += total(grad_pre)
    glearn_ref[...] = grad_pre.astype(bf16)
    back = nt(glearn_ref[...], learn_in_ref[...])
    unit, rstd = norm_parts(res_ref[...])
    vsum_ref[4:5, :] += total(back * unit)
    vsum_ref[5:6, :] += total(back)
    grad_result = matmul(spread, pooled_grad_ref[...]) + norm_back(back, unit, rstd, vec(4))
    vsum_ref[1:2, :] += total(grad_result)
    res_ref[...] = grad_result
    gres_ref[...] = grad_result.astype(bf16)

    def down_back(j, _):
        grad = nt(gres_ref[...], w_down_ref[columns(j), :]) * dgate_ref[:, columns(j)]
        usum_ref[:, columns(j)] += total(grad)
        gup_ref[:, columns(j)] = grad.astype(bf16)
        return 0

    lax.fori_loop(0, chunks, down_back, 0)
    back = nt(gup_ref[...], w_up_ref[...])
    unit, rstd = norm_parts(hid_ref[...])
    vsum_ref[2:3, :] += total(back * unit)
    vsum_ref[3:4, :] += total(back)
    grad_hidden = res_ref[...] + norm_back(back, unit, rstd, vec(2))
    vsum_ref[0:1, :] += total(grad_hidden)
    ghid_f32_ref[...] = grad_hidden
    ghid_ref[...] = grad_hidden.astype(bf16)
    grad = nt(ghid_ref[...], w_out_ref[...]).astype(bf16)
    wide = width // (count * splits)
    for i in range(count * splits):
        gatt[i][...] = grad[:, i * wide : (i + 1) * wide]


def rows_call(tok, img, attended, w_out, w_up, w_down, learn_in, learn_out, vecs, up_bias, out_bias, pooled_grad, splits):
    count, (rows, features) = len(attended), attended[0].shape
    local_rows, width = tok.shape
    hidden_units = w_up.shape[1]
    inner = learn_in.shape[1]
    spread = learn_out.shape[1]
    block = min(ROW_BLOCK, rows)
    chunk = UP_BLOCK
    wide = features // splits
    once = lambda a: pl.BlockSpec(a.shape, lambda i: (0,) * a.ndim, pipeline_mode=pl.Buffered(1))
    by_rows = lambda n: pl.BlockSpec((block, n), lambda i: (i, 0))
    kept = lambda a: pl.BlockSpec(a.shape, lambda i: (0, 0))
    low = lambda n: jax.ShapeDtypeStruct((rows, n), bf16)
    lows = [width, hidden_units, hidden_units, width, width, inner, inner, spread, width]
    sums = [
        jax.ShapeDtypeStruct((spread, width), f32),
        jax.ShapeDtypeStruct((8, width), f32),
        jax.ShapeDtypeStruct((1, hidden_units), f32),
        jax.ShapeDtypeStruct((1, spread), f32),
    ]
    resident = [w_out, w_up, w_down, learn_in, learn_out, vecs, up_bias, out_bias, pooled_grad]
    return pl.pallas_call(
        functools.partial(rows_kernel, count, splits, local_rows),
        grid=(rows // block,),
        in_specs=[by_rows(width), by_rows(1)]
        + [once(a) for a in resident]
        + [by_rows(features)] * count,
        out_specs=[by_rows(n) for n in lows]
        + [by_rows(width)]
        + [by_rows(wide)] * (count * splits)
        + [kept(a) for a in sums],
        out_shape=[low(n) for n in lows]
        + [jax.ShapeDtypeStruct((rows, width), f32)]
        + [low(wide)] * (count * splits)
        + sums,
        scratch_shapes=[
            pltpu.VMEM((block, width), f32),
            pltpu.VMEM((block, width), f32),
            pltpu.VMEM((block, hidden_units), f32),
            pltpu.VMEM((block, chunk), f32),
            pltpu.VMEM((block, chunk), f32),
        ],
        compiler_params=params(),
        cost_estimate=pl.CostEstimate(
            flops=4 * rows * width * (width + 2 * hidden_units + inner),
            bytes_accessed=2 * (rows * 20 * width + 2 * width * hidden_units),
            transcendentals=0,
        ),
    )(tok, img, *resident, *attended)


def part_halves(me_ref, value, keep_ref, send_ref, whole_ref):
    half = value.shape[1] // 2
    core = me_ref[0] % 2
    whole_ref[...] = value
    keep_ref[...] = whole_ref[:, pl.ds(pl.multiple_of(core * half, half), half)]
    send_ref[...] = whole_ref[:, pl.ds(pl.multiple_of((1 - core) * half, half), half)]


def down_grad_kernel(waits, me_ref, left_ref, right_ref, *refs):
    part_halves(me_ref, tn(left_ref[...], right_ref[...]).astype(bf16), *refs[waits:])


def down_grad_call(me, left, right, after=()):
    rows, m = left.shape
    n = right.shape[1]
    out = pl.BlockSpec((GRAD_BLOCK, n // 2), lambda j, m: (j, 0))
    return pl.pallas_call(
        functools.partial(down_grad_kernel, len(after)),
        grid_spec=pltpu.PrefetchScalarGridSpec(
            num_scalar_prefetch=1,
            grid=(m // GRAD_BLOCK,),
            in_specs=[
                pl.BlockSpec((rows, GRAD_BLOCK), lambda j, m: (0, j)),
                pl.BlockSpec((rows, n), lambda j, m: (0, 0), pipeline_mode=pl.Buffered(1)),
            ]
            + [ANYWHERE] * len(after),
            out_specs=[out, out],
            scratch_shapes=[pltpu.VMEM((GRAD_BLOCK, n), bf16)],
        ),
        out_shape=[jax.ShapeDtypeStruct((m, n // 2), bf16)] * 2,
        compiler_params=params(),
        cost_estimate=pl.CostEstimate(
            flops=3 * rows * m * n, bytes_accessed=4 * m * n, transcendentals=0
        ),
    )(me, left, right, *after)


def up_grad_kernel(half, waits, me_ref, left_ref, right_ref, *refs):
    keep_ref, send_ref = refs[waits:]
    value = tn(left_ref[...], right_ref[...]).astype(bf16)

    @pl.when(pl.program_id(0) < half)
    def _():
        send_ref[...] = value

    @pl.when(pl.program_id(0) >= half)
    def _():
        keep_ref[...] = value


def up_grad_call(me, left, right, after=()):
    rows, m = left.shape
    n = right.shape[1]
    half = n // GRAD_BLOCK // 2

    def column(j, core):
        return jnp.where(j < half, (1 - core) * half + j, core * half + j - half)

    return pl.pallas_call(
        functools.partial(up_grad_kernel, half, len(after)),
        grid_spec=pltpu.PrefetchScalarGridSpec(
            num_scalar_prefetch=1,
            grid=(2 * half,),
            in_specs=[
                pl.BlockSpec((rows, m), lambda j, me: (0, 0), pipeline_mode=pl.Buffered(1)),
                pl.BlockSpec((rows, GRAD_BLOCK), lambda j, me: (0, column(j, me[0] % 2))),
            ]
            + [ANYWHERE] * len(after),
            out_specs=[
                pl.BlockSpec((m, GRAD_BLOCK), lambda j, me: (0, jnp.maximum(j - half, 0))),
                pl.BlockSpec((m, GRAD_BLOCK), lambda j, me: (0, jnp.minimum(j, half - 1))),
            ],
        ),
        out_shape=[jax.ShapeDtypeStruct((m, n // 2), bf16)] * 2,
        compiler_params=params(),
        cost_estimate=pl.CostEstimate(
            flops=3 * rows * m * n, bytes_accessed=4 * m * n, transcendentals=0
        ),
    )(me, left, right, *after)


def small_grad_kernel(count, me_ref, *refs):
    n3_ref, glearn_ref, ghid_ref, inner_ref, glogit_ref = refs[:5]
    attended = refs[5 : 5 + count]
    keep_ref, send_ref, lout_ref, learn_ref, wout_ref = refs[5 + count :]
    learn_ref[...] = tn(n3_ref[...], glearn_ref[...]).astype(bf16)
    lout_ref[...] = tn(inner_ref[...], glogit_ref[...])
    features = attended[0].shape[1]
    for d in range(count):
        owner = jnp.bitwise_xor(me_ref[0], d)
        to = pl.ds(pl.multiple_of(owner * features, features), features)
        wout_ref[to, :] = tn(attended[d][...], ghid_ref[...]).astype(bf16)
    first = me_ref[0] % 2 == 0

    @pl.when(first)
    def _():
        keep_ref[...] = learn_ref[...]
        send_ref[...] = wout_ref[...]

    @pl.when(jnp.logical_not(first))
    def _():
        keep_ref[...] = wout_ref[...]
        send_ref[...] = learn_ref[...]


def small_grad_call(me, n3, glearn, ghid, inner, glogit, attended):
    rows, width = n3.shape
    operands = [n3, glearn, ghid, inner, glogit, *attended]
    out = jax.ShapeDtypeStruct((width, ghid.shape[1]), bf16)
    lout = jax.ShapeDtypeStruct((inner.shape[1], glogit.shape[1]), f32)
    once = lambda a: pl.BlockSpec(a.shape, lambda j, m: (0, 0), pipeline_mode=pl.Buffered(1))
    return pl.pallas_call(
        functools.partial(small_grad_kernel, len(attended)),
        grid_spec=pltpu.PrefetchScalarGridSpec(
            num_scalar_prefetch=1,
            grid=(1,),
            in_specs=[once(a) for a in operands],
            out_specs=[once(out), once(out), once(lout)],
            scratch_shapes=[pltpu.VMEM(out.shape, bf16), pltpu.VMEM(out.shape, bf16)],
        ),
        out_shape=[out, out, lout],
        compiler_params=params(),
        cost_estimate=pl.CostEstimate(
            flops=6 * rows * width * width, bytes_accessed=20 * width * width, transcendentals=0
        ),
    )(me, *operands)


def qkv_grad_kernel(groups, waits, me_ref, n_ref, gain_ref, shift_ref, *refs):
    parts, weights = refs[:groups], refs[groups : groups + 3]
    out_ref, sums_ref, acc_ref, sum_ref = refs[groups + 3 + waits :]
    step = pl.program_id(0)
    wide = weights[0].shape[1]
    for d in range(2 * groups):

        @pl.when(step == d)
        def _():
            mixed = parts[d // 2][d % 2]
            part = tn(n_ref[0], mixed)
            column = total(mixed.astype(f32))
            acc_ref[...] = part if d == 0 else acc_ref[...] + part
            sum_ref[...] = column if d == 0 else sum_ref[...] + column

    @pl.when(step == 2 * groups - 1)
    def _():
        by_unit, column = acc_ref[...], sum_ref[...]
        out_ref[...] = (by_unit * gain_ref[...] + shift_ref[...] * column).astype(bf16)
        weight = jnp.concatenate([ref[...].astype(f32) for ref in weights], axis=1)
        sums_ref[:, 0:1] = jnp.sum(by_unit * weight, axis=1, keepdims=True)
        sums_ref[:, 1:2] = jnp.sum(weight * column, axis=1, keepdims=True)


def qkv_grad_call(me, unit, parts, w_qkv, gain, shift, split, splits, after=()):
    count, rows, width = unit.shape
    columns = parts[0].shape[2]
    once = lambda a: pl.BlockSpec(
        a.shape, lambda d, m: (0,) * len(a.shape), pipeline_mode=pl.Buffered(1)
    )
    specs, operands = own_columns(w_qkv, width // count, splits, [split])
    return pl.pallas_call(
        functools.partial(qkv_grad_kernel, count // 2, len(after)),
        grid_spec=pltpu.PrefetchScalarGridSpec(
            num_scalar_prefetch=1,
            grid=(count,),
            in_specs=[pl.BlockSpec((1, rows, width), lambda d, m: (d, 0, 0)), once(gain), once(shift)]
            + [once(a) for a in parts]
            + specs
            + [ANYWHERE] * len(after),
            out_specs=[
                pl.BlockSpec((width, columns), lambda d, m: (0, 0)),
                pl.BlockSpec((width, 2), lambda d, m: (0, 0)),
            ],
            scratch_shapes=[pltpu.VMEM((width, columns), f32), pltpu.VMEM((1, columns), f32)],
        ),
        out_shape=[
            jax.ShapeDtypeStruct((width, columns), bf16),
            jax.ShapeDtypeStruct((width, 2), f32),
        ],
        compiler_params=params(),
        cost_estimate=pl.CostEstimate(flops=1 << 20, bytes_accessed=1 << 10, transcendentals=0),
    )(me, unit, gain, shift, *parts, *operands, *after)


def tokens_kernel(groups, splits, me_ref, tok_ref, ghid_ref, w_ref, gain_ref, *refs):
    same, other = refs[: groups * splits], refs[groups * splits : groups * splits + splits]
    out_ref, mixed_ref = refs[groups * splits + splits :]
    width = tok_ref.shape[1]
    features = width // (2 * groups)
    wide = features // splits
    for d in range(2 * groups):
        owner = jnp.bitwise_xor(me_ref[0], d) * features
        for s in range(splits):
            for part in range(3):
                to = pl.ds(pl.multiple_of(part * width + owner + s * wide, wide), wide)
                at = slice(part * wide, (part + 1) * wide)
                if d % 2 == 0:
                    mixed_ref[:, to] = same[s * groups + d // 2][0, :, at]
                else:
                    mixed_ref[:, to] = other[s][d // 2, :, at]
    back = nt(mixed_ref[...], w_ref[...])
    unit, rstd = norm_parts(tok_ref[...].astype(f32))
    out_ref[0] = ghid_ref[...] + norm_back(back, unit, rstd, gain_ref[...])


def tokens_call(me, tok, ghid, w_qkv, gain, same, other, count):
    local_rows, width = tok.shape
    columns = same[0].shape[2]
    groups, splits = count // 2, len(other)
    block = 256
    by_rows = lambda n: pl.BlockSpec((block, n), lambda i, m: (i, 0))
    return pl.pallas_call(
        functools.partial(tokens_kernel, groups, splits),
        grid_spec=pltpu.PrefetchScalarGridSpec(
            num_scalar_prefetch=1,
            grid=(pl.cdiv(local_rows, block),),
            in_specs=[
                by_rows(width),
                by_rows(width),
                pl.BlockSpec(w_qkv.shape, lambda i, m: (0, 0), pipeline_mode=pl.Buffered(1)),
                pl.BlockSpec(gain.shape, lambda i, m: (0, 0)),
            ]
            + [pl.BlockSpec((1, block, columns), lambda i, m: (0, i, 0))] * len(same)
            + [pl.BlockSpec((groups, block, columns), lambda i, m: (0, i, 0))] * splits,
            out_specs=pl.BlockSpec((1, block, width), lambda i, m: (0, i, 0)),
            scratch_shapes=[pltpu.VMEM((block, 3 * width), bf16)],
        ),
        out_shape=jax.ShapeDtypeStruct((1, local_rows, width), f32),
        compiler_params=params(),
        cost_estimate=pl.CostEstimate(flops=1 << 20, bytes_accessed=1 << 10, transcendentals=0),
    )(me, tok, ghid, w_qkv, gain, *same, *other)


def flip(index, bit):
    return index + bit - 2 * bit * ((index // bit) % 2)


def vectors_kernel(count, row_bits, img_bits, vec_ref, slot_ref, out_ref, sum_ref, *scratch):
    recv, slot_recv, send_sem, recv_sem, slot_send, slot_got = scratch
    row, img = lax.axis_index("row"), lax.axis_index("img")

    def partner(row_mask, img_mask=0):
        r, g = row, img
        for bit in row_bits:
            r = flip(r, bit) if row_mask & bit else r
        for bit in img_bits:
            g = flip(g, bit) if img_mask & bit else g
        return (g, r)

    steps = [(bit, 0) for bit in row_bits] + [(0, bit) for bit in img_bits]
    everyone = sorted(set(steps) | {(d, 0) for d in range(1, count)})
    barrier = pltpu.get_barrier_semaphore()
    for masks in everyone:
        pl.semaphore_signal(
            barrier, inc=1, device_id=partner(*masks), device_id_type=pl.DeviceIdType.MESH
        )
    pl.semaphore_wait(barrier, len(everyone))
    slots = []
    for d in range(1, count):
        copy = pltpu.make_async_remote_copy(
            src_ref=slot_ref.at[d],
            dst_ref=slot_recv.at[d - 1],
            send_sem=slot_send.at[d - 1],
            recv_sem=slot_got.at[d - 1],
            device_id=partner(d),
            device_id_type=pl.DeviceIdType.MESH,
        )
        copy.start()
        slots.append(copy)
    out_ref[...] = vec_ref[...]
    for i, masks in enumerate(steps):
        copy = pltpu.make_async_remote_copy(
            src_ref=out_ref,
            dst_ref=recv.at[i],
            send_sem=send_sem.at[i],
            recv_sem=recv_sem.at[i],
            device_id=partner(*masks),
            device_id_type=pl.DeviceIdType.MESH,
        )
        copy.start()
        copy.wait()
        out_ref[...] = out_ref[...] + recv[i]
    for copy in slots:
        copy.wait()
    sum_ref[...] = tree(
        [slot_ref[0].astype(f32)] + [slot_recv[d - 1].astype(f32) for d in range(1, count)]
    )


def vectors_call(vec, slots):
    count = lax.axis_size("row")
    row_bits, img_bits = bits_of(count), bits_of(lax.axis_size("img"))
    steps = len(row_bits) + len(img_bits)
    whole = pl.BlockSpec(memory_space=pltpu.VMEM)
    return pl.pallas_call(
        functools.partial(vectors_kernel, count, row_bits, img_bits),
        in_specs=[whole, whole],
        out_specs=[whole, whole],
        out_shape=[
            jax.ShapeDtypeStruct(vec.shape, f32),
            jax.ShapeDtypeStruct(slots.shape[1:], f32),
        ],
        scratch_shapes=[
            pltpu.VMEM((steps,) + vec.shape, f32),
            pltpu.VMEM((count - 1,) + slots.shape[1:], bf16),
            pltpu.SemaphoreType.DMA((steps,)),
            pltpu.SemaphoreType.DMA((steps,)),
            pltpu.SemaphoreType.DMA((count - 1,)),
            pltpu.SemaphoreType.DMA((count - 1,)),
        ],
        compiler_params=pltpu.CompilerParams(
            collective_id=0, has_side_effects=True, vmem_limit_bytes=32 << 20
        ),
        cost_estimate=pl.CostEstimate(flops=1 << 20, bytes_accessed=1 << 10, transcendentals=0),
    )(vec, slots)


def rows_of(array, index, length):
    return lax.dynamic_slice_in_dim(array, index * length, length, 0)


def on_device(
    tokens,
    counts,
    owner,
    w_qkv,
    qv_bias,
    w_out,
    out_bias,
    w_up,
    up_bias,
    w_down,
    down_bias,
    norm_gain,
    norm_bias,
    learn_in,
    learn_in_bias,
    learn_out,
    learn_out_bias,
    cotangent,
):
    width = tokens.shape[2]
    local_rows = tokens.shape[1]
    row_count = lax.axis_size("row")
    images_count = lax.axis_size("img")
    device = lax.axis_index("row")
    image_device = lax.axis_index("img")
    features = width // row_count
    wide = min(features, 128)
    splits = features // wide
    slots_here = IMGS // row_count
    group_counts = counts[0]
    partners = [device ^ d for d in range(row_count)]
    row_bits, img_bits = stages()
    n_img = len(img_bits)

    piece_rows = BLK // row_count
    blocks = pl.cdiv(local_rows, piece_rows)
    images = jnp.stack([row_images(group_counts, p, local_rows, row_count) for p in partners])
    extra = blocks * piece_rows - local_rows
    images = jnp.pad(images, ((0, 0), (0, extra)), constant_values=IMGS + 1)
    image_here = images[0].reshape(-1, 1)
    images = images.reshape(row_count, blocks, piece_rows).transpose(1, 0, 2).reshape(blocks, BLK)
    least, most = jnp.min(images, axis=1), jnp.max(images, axis=1)
    lo = jnp.sum((most[None, :] < least[:, None]).astype(jnp.int32), axis=1)
    hi = jnp.sum((least[None, :] <= most[:, None]).astype(jnp.int32), axis=1)
    imgq, imgk = images.reshape(1, -1), images.reshape(-1, 1)

    me = device.reshape(1)
    w_out_here = jnp.concatenate([rows_of(w_out, p, features) for p in partners], axis=0)
    bias_here = lax.dynamic_slice_in_dim(qv_bias, device * features, features, 1)
    grads_in = gather_pieces(cotangent[0].reshape(slots_here, LT * width).astype(bf16))
    pieces = gather_pieces(
        tokens[0], [imgq, imgk, lo, hi, image_here, w_out_here, bias_here, grads_in[-1]]
    )

    unit, q, k, v, kt, vt = qkv_call(
        me, pieces, w_qkv, bias_here, norm_gain[0:1], norm_bias[0:1], splits
    )
    *attended, ot, lse = attend_call(q, k, vt, imgq, imgk, lo, hi, row_count)
    attended = send_pieces(attended)

    slot_rel = ((owner[0] // slots_here) ^ device) * slots_here + owner[0] % slots_here
    select = (slot_rel[:, None] == jnp.arange(IMGS, dtype=jnp.int32)[None, :]).astype(f32)
    scale = lax.rsqrt(group_counts.astype(f32))
    incoming = jnp.concatenate(grads_in, axis=0).astype(f32)
    grad_pooled = jnp.dot(select, incoming, precision=highest) * scale[:, None]
    grad_pooled_low = grad_pooled.reshape(IMGS * LT, width).astype(bf16)

    vecs = jnp.concatenate(
        [
            out_bias[None],
            down_bias[None],
            norm_gain[1:2],
            norm_bias[1:2],
            norm_gain[2:3],
            norm_bias[2:3],
            learn_in_bias[None],
            jnp.zeros((1, width), f32),
        ],
        axis=0,
    )
    out = rows_call(
        tokens[0],
        image_here,
        attended,
        w_out_here,
        w_up,
        w_down,
        learn_in,
        jnp.tile(learn_out, (1, IMGS)),
        vecs,
        up_bias[None],
        jnp.tile(learn_out_bias, IMGS)[None],
        grad_pooled_low,
        splits,
    )
    n2, gated, gup, gres, n3, glearn, inner, glogit, ghid, grad_hidden = out[:10]
    grad_attended = out[10 : 10 + row_count * splits]
    pooled, vec_sums, up_sums, logit_sums = out[10 + row_count * splits :]
    grad_attended = [send_pieces(grad_attended[s::splits]) for s in range(splits)]

    core, far_row = row_bits[:1], row_bits[1:]
    y_bits, z_bits = img_bits[:1], [[bit] for bit in img_bits[1:]]
    stage = lambda value, bits, after=(): reduce_stage(value, bits, n_img, after)
    stack_other = lambda groups: jump(jnp.stack([g[1] for g in groups]), 1)

    def core_sum(keep, send, after):
        arrived = behind(jump(send, 1), after)
        return spread_img((keep.astype(f32) + arrived.astype(f32)).astype(bf16))

    keep_small, send_small, grad_learn_out = small_grad_call(
        me, n3, glearn, ghid, inner, glogit, attended
    )
    keep_down, send_down = down_grad_call(me, gated, gres, [send_small])
    small = core_sum(keep_small, send_small, [send_down])
    keep_up, send_up = up_grad_call(me, n2, gup, [send_down, small])
    down = core_sum(keep_down, send_down, [send_up])

    def back_call(s, after):
        *parts, sums = attend_back_call(
            grad_attended[s], q, k, v, kt, ot, lse, imgq, imgk, lo, hi, s, after
        )
        return parts, sums

    def grad_qkv_call(s, parts, after):
        turned = [norm_gain[0].reshape(-1, 1), norm_bias[0].reshape(-1, 1)]
        return qkv_grad_call(me, unit, parts, w_qkv, *turned, s, splits, after)

    def far_sent(parts):
        return [parts[0]] + [jump(parts[g], 2 * g) for g in range(1, len(parts))]

    same, qkv_sums, norm_sums, grad_qkv = [], [], [], []
    after = [down, send_up]
    for s in range(splits):
        parts, sums = back_call(s, after)
        here = far_sent(parts)
        qkv_sums.append(sums[0:2])
        last = s == splits - 1
        if s == 0:
            small = stage(small, y_bits, [sums])
            ups = core_sum(keep_up, send_up, [sums])
            down = stage(down, far_row, [sums])
        if last:
            ups = stage(ups, y_bits, [sums])
            down = stage(down, z_bits[0], [sums])
            small = stage(small, z_bits[1], [sums])
            same = [behind(h, [sums]) for h in same]
        grad, norm_sum = grad_qkv_call(s, parts, [ups, down])
        norm_sums.append(norm_sum)
        grad_qkv.append(spread_img(grad))
        same += here
        if s == 0:
            small = stage(small, z_bits[0], [norm_sum])
            after = [small, grad]
    by_slot = jnp.dot(select.T, pooled.reshape(IMGS, LT * width), precision=highest)
    by_slot = by_slot.astype(bf16).reshape(row_count, -1, 128)
    late = lax.dynamic_update_slice(
        jnp.zeros((2, width), f32), jnp.concatenate(qkv_sums, axis=1), (0, device * features)
    )
    vectors = jnp.concatenate(
        [
            up_sums.reshape(-1),
            vec_sums.reshape(-1),
            jnp.sum(grad_learn_out.reshape(-1, IMGS, LT), axis=1).reshape(-1),
            late.reshape(-1),
            sum(norm_sums).T.reshape(-1),
            jnp.sum(logit_sums.reshape(IMGS, LT), axis=0),
        ]
    )
    vectors = jnp.pad(vectors, (0, -vectors.shape[0] % 1024)).reshape(-1, 128)
    vectors, learned = vectors_call(vectors, by_slot)

    here = [behind(h, [vectors]) for h in same[-row_count // 2 + 1 :]]
    same = same[: len(same) - len(here)] + here
    groups = row_count // 2
    others = jnp.stack([p[1] for p in same])
    others = jump(others, 1)
    other = [others[s * groups : (s + 1) * groups] for s in range(splits)]
    ups = stage(ups, z_bits[0], [vectors])
    down = stage(down, z_bits[1], [vectors])
    grad_qkv = stage(jnp.concatenate(grad_qkv, axis=-1), y_bits, [vectors])
    for bits in z_bits[2:]:
        down = stage(down, bits)
        small = stage(small, bits)
    grad_tokens = tokens_call(
        me,
        tokens[0],
        behind(grad_hidden, [ups, down, grad_qkv]),
        w_qkv,
        norm_gain[0:1],
        same,
        other,
        row_count,
    )
    small = exchange_sum(small, far_row, [grad_tokens])
    grad_qkv = stage(grad_qkv, z_bits[0], [grad_tokens])
    for bits in z_bits[1:]:
        ups = stage(ups, bits, [grad_tokens])
    down = stage(down, y_bits, [grad_tokens])
    ups = exchange_sum(ups, far_row)
    for bits in z_bits[1:]:
        grad_qkv = stage(grad_qkv, bits)
    vectors = vectors.reshape(-1)
    scale_here = jnp.dot(scale, select, precision=highest)[:slots_here]
    learned = learned.reshape(slots_here, LT * width) * scale_here[:, None]
    learned = learned.reshape(1, slots_here, LT, width)

    share_down = finish_weight(down, row_bits)
    share_small = finish_weight(small, core, [grad_tokens])
    share_up = finish_weight(ups, core)
    share_learn = share_small[:, : learn_in.shape[1]]
    share_out = share_small[:, learn_in.shape[1] :]
    shares = gather_columns(grad_qkv.reshape(grad_qkv.shape[-2:]), lambda c: c, row_bits)
    share_qkv = jnp.concatenate(
        [
            shares[c][:, (3 * s + part) * wide : (3 * s + part + 1) * wide]
            for part in range(3)
            for c in range(row_count)
            for s in range(splits)
        ],
        axis=1,
    ).astype(f32)

    at = up_bias.shape[0]
    up_sum, vec_sums = vectors[:at], vectors[at : at + 8 * width].reshape(8, width)
    at += 8 * width
    learn_out_sum = vectors[at : at + learn_out.size].reshape(learn_out.shape)
    at += learn_out.size
    late = vectors[at : at + 4 * width].reshape(4, width)
    at += 4 * width
    out_sum, down_sum, gain_two, shift_two, gain_three, shift_three, learn_in_sum = vec_sums[:7]
    share_learn_out = rows_of(learn_out_sum, image_device, learn_out.shape[0] // images_count)
    return (
        learned,
        grad_tokens,
        share_qkv,
        late[0:2],
        share_out,
        out_sum,
        share_up,
        up_sum,
        share_down,
        down_sum,
        jnp.stack([late[2], gain_two, gain_three]),
        jnp.stack([late[3], shift_two, shift_three]),
        share_learn,
        learn_in_sum,
        share_learn_out,
        vectors[at : at + learn_out.shape[1]],
    )


def solution(mesh):
    by_image = P("img", None)
    in_specs = (
        (P("img", "row", None), by_image, by_image) + (P(),) * 14 + (P("img", "row", None, None),)
    )
    out_specs = (
        P("img", "row", None, None),
        P("img", "row", None),
        by_image,
        P(),
        by_image,
        P(),
        by_image,
        P(),
        by_image,
        P(),
        P(),
        P(),
        by_image,
        P(),
        by_image,
        P(),
    )
    return jax.shard_map(
        on_device, mesh=mesh, in_specs=in_specs, out_specs=out_specs, check_vma=False
    )
```

```python
import functools

import jax
import jax.numpy as jnp
from jax import lax
from jax.experimental import pallas as pl
from jax.experimental.pallas import tpu as pltpu
from jax.sharding import PartitionSpec as P

HEADS = 16
HEAD = 64
LT = 8
IMGS = 8
BLK = 256
NEG = -1e30
VMEM = 60 << 20
ROW_BLOCK = 256
UP_BLOCK = 1024
GRAD_BLOCK = 1024

highest = lax.Precision.HIGHEST
epsilon = 1e-06
f32 = jnp.float32
bf16 = jnp.bfloat16


def smooth_both(v):
    half = jnp.abs(v) * 0.7071067811865476
    t = 1.0 / (1.0 + 0.3275911 * half)
    bell = jnp.exp(-half * half)
    poly = t * (
        0.127414796
        + t * (-0.142248368 + t * (0.7107068705 + t * (-0.7265760135 + t * 0.5307027145)))
    )
    tail = poly * bell
    cdf = jnp.where(v >= 0.0, 1.0 - tail, tail)
    return v * cdf, cdf + v * (bell * 0.3989422804014327)


def matmul(left, right):
    return jnp.dot(left, right, preferred_element_type=f32)


def nt(left, right):
    return lax.dot_general(left, right, (((1,), (1,)), ((), ())), preferred_element_type=f32)


def tn(left, right):
    return lax.dot_general(left, right, (((0,), (0,)), ((), ())), preferred_element_type=f32)


def row_images(counts, device, local_rows, row_count):
    upper_end = counts * (device + 1) // row_count
    lower_end = counts * device // row_count
    run_ends = jnp.cumsum(upper_end - lower_end)
    positions = jnp.arange(local_rows, dtype=jnp.int32)
    return jnp.sum((positions[:, None] >= run_ends[None, :]).astype(jnp.int32), axis=1)


def bits_of(size):
    return [1 << i for i in range(size.bit_length() - 1)]


def jump(value, row_mask, img_mask=0):
    rows, imgs = lax.axis_size("row"), lax.axis_size("img")
    if img_mask == 0:
        return lax.ppermute(value, "row", [(i, i ^ row_mask) for i in range(rows)])
    if row_mask == 0:
        return lax.ppermute(value, "img", [(i, i ^ img_mask) for i in range(imgs)])
    mask = img_mask * rows + row_mask
    return lax.ppermute(value, ("img", "row"), [(i, i ^ mask) for i in range(rows * imgs)])


def masks_of(bits):
    masks = []
    for e in range(1 << len(bits)):
        masks.append(
            tuple(
                sum(bit for j, (axis, bit) in enumerate(bits) if axis == name and e >> j & 1)
                for name in ("row", "img")
            )
        )
    return masks


def gather_pieces(value, after=()):
    pieces = {0: value}
    order = sorted(range(1, lax.axis_size("row")), key=lambda d: (d & 1, d))
    for d in order:
        low = d & -d
        pieces[d] = jump(pieces[d ^ low], low)
        if d % 2 == 0:
            pieces[d] = behind(pieces[d], after)
    return [pieces[d] for d in range(lax.axis_size("row"))]


def send_pieces(pieces):
    far_first = sorted(range(1, len(pieces)), reverse=True)
    arrived = {d: jump(pieces[d], d) for d in far_first}
    return [pieces[0]] + [arrived[d] for d in range(1, len(pieces))]


def stages():
    row_bits = [("row", b) for b in bits_of(lax.axis_size("row"))]
    img_bits = [("img", b) for b in bits_of(lax.axis_size("img"))]
    return row_bits, img_bits


def tree(values):
    while len(values) > 1:
        values = [values[i] + values[i + 1] for i in range(0, len(values), 2)]
    return values[0]


def behind(value, after):
    return lax.optimization_barrier((value, tuple(after)))[0] if after else value


class Halving:
    def __init__(self, value, bits, img_count):
        mine = {"row": lax.axis_index("row"), "img": lax.axis_index("img")}

        def part(e):
            piece = value
            for j, (axis, bit) in enumerate(bits):
                want = (mine[axis] // bit) % 2 ^ (e >> j & 1)
                dim = value.ndim - 1 if axis == "row" else img_count - bit.bit_length()
                length = piece.shape[dim] // 2
                piece = lax.dynamic_slice_in_dim(piece, want * length, length, dim)
            return piece

        masks = masks_of(bits)
        self.kept = part(0)
        self.moved = [jump(part(e), *masks[e]) for e in range(1, len(masks))]

    def finish(self):
        values = [self.kept, *self.moved]
        return tree([v.astype(f32) for v in values]).astype(bf16)


class Exchange(Halving):
    def __init__(self, value, bits):
        self.kept = value
        self.moved = [jump(value, *mask) for mask in masks_of(bits)[1:]]


class Moved(Halving):
    def __init__(self, values, masks):
        self.moved = [jump(v, *mask) for v, mask in zip(values, masks)]

    def finish(self):
        return self.moved


def arrive(flights, after=()):
    return arrive_with(flights, tuple(after))[0]


def arrive_with(flights, beside):
    flat = [m for flight in flights for m in flight.moved]
    flat, beside = lax.optimization_barrier((flat, beside))
    for flight in flights:
        flight.moved, flat = flat[: len(flight.moved)], flat[len(flight.moved) :]
    return [flight.finish() for flight in flights], beside


def spread_img(grad):
    rows, columns = grad.shape
    images = lax.axis_size("img")
    return grad.reshape((2,) * len(bits_of(images)) + (rows // images, columns))


def gather_columns(value, order, bits, after=()):
    masks = [row_mask for row_mask, _ in masks_of(bits)]
    device = lax.axis_index("row") % len(masks)
    stack = jnp.stack([value if m == 0 else behind(jump(value, m), after) for m in masks])
    return [
        lax.dynamic_index_in_dim(stack, order(c) ^ device, 0, False) for c in range(len(masks))
    ]


def reversed_bits(index, size):
    width = size.bit_length() - 1
    return int(format(index, f"0{width}b")[::-1], 2) if width else 0


def finish_weight(value, bits, after=()):
    value = value.reshape(value.shape[-2:])
    count = 1 << len(bits)
    blocks = gather_columns(value, lambda c: reversed_bits(c, count), bits, after)
    return jnp.concatenate(blocks, axis=1).astype(f32)


def params(flags=("arbitrary",)):
    return pltpu.CompilerParams(dimension_semantics=flags, vmem_limit_bytes=VMEM)


ANYWHERE = pl.BlockSpec(memory_space=pl.ANY)


def own_columns(w_qkv, features, splits, chosen):
    width = w_qkv.shape[0]
    wide = features // splits

    def spec(s, part):
        def index(b, me):
            return 0, part * (width // wide) + me[0] * splits + s

        return pl.BlockSpec((width, wide), index, pipeline_mode=pl.Buffered(1))

    return [spec(s, part) for s in chosen for part in range(3)], [w_qkv] * (3 * len(chosen))


def valid_rows(block, piece_rows, local_rows):
    position = lax.broadcasted_iota(jnp.int32, (BLK, 1), 0) % piece_rows + block * piece_rows
    return position < local_rows


def load_block(refs, block, piece_rows, local_rows):
    value = jnp.concatenate([ref[...] for ref in refs], axis=0).astype(f32)
    return jnp.where(valid_rows(block, piece_rows, local_rows), value, 0.0)


def norm_parts(value):
    centre = value - jnp.mean(value, axis=-1, keepdims=True)
    rstd = lax.rsqrt(jnp.mean(centre * centre, axis=-1, keepdims=True) + epsilon)
    return centre * rstd, rstd


def qkv_kernel(count, splits, local_rows, features, me_ref, *refs):
    n_w = 3 * splits
    pieces, columns = refs[:count], refs[count : count + n_w]
    bias_ref, gain_ref, shift_ref = refs[count + n_w : count + n_w + 3]
    n_ref, q_ref, k_ref, v_ref, kt_ref, vt_ref, w_ref = refs[count + n_w + 3 :]
    block = pl.program_id(0)
    wide = features // splits

    @pl.when(block == 0)
    def _():
        for i, ref in enumerate(columns):
            w_ref[:, i * wide : (i + 1) * wide] = ref[...]

    unit, _ = norm_parts(load_block(pieces, block, BLK // count, local_rows))
    normed = (unit * gain_ref[...] + shift_ref[...]).astype(bf16)
    n_ref[...] = unit.astype(bf16).reshape(n_ref.shape)
    mixed = matmul(normed, w_ref[...])
    for s in range(splits):
        at = slice(s * wide, (s + 1) * wide)
        part = mixed[:, 3 * s * wide : 3 * (s + 1) * wide]
        keys = part[:, wide : 2 * wide]
        values = part[:, 2 * wide :] + bias_ref[1:2, at]
        q_ref[:, at] = ((part[:, :wide] + bias_ref[0:1, at]) * 0.125).astype(bf16)
        k_ref[:, at] = keys.astype(bf16)
        v_ref[:, at] = values.astype(bf16)
        kt_ref[0, at] = keys.T.astype(bf16)
        vt_ref[0, at] = values.T.astype(bf16)


def qkv_call(me, pieces, w_qkv, bias, gain, shift, splits):
    count, (local_rows, width) = len(pieces), pieces[0].shape
    features = width // count
    piece_rows = BLK // count
    blocks = pl.cdiv(local_rows, piece_rows)
    whole = lambda a: pl.BlockSpec(a.shape, lambda b, m: (0,) * a.ndim)
    flat = pl.BlockSpec((BLK, features), lambda b, m: (b, 0))
    turned = pl.BlockSpec((1, features, BLK), lambda b, m: (b, 0, 0))
    specs, operands = own_columns(w_qkv, features, splits, range(splits))
    return pl.pallas_call(
        functools.partial(qkv_kernel, count, splits, local_rows, features),
        grid_spec=pltpu.PrefetchScalarGridSpec(
            num_scalar_prefetch=1,
            grid=(blocks,),
            in_specs=[pl.BlockSpec((piece_rows, width), lambda b, m: (b, 0))] * count
            + specs
            + [whole(bias), whole(gain), whole(shift)],
            out_specs=[
                pl.BlockSpec((count, piece_rows, width), lambda b, m: (0, b, 0)),
                flat,
                flat,
                flat,
                turned,
                turned,
            ],
            scratch_shapes=[pltpu.VMEM((width, 3 * features), bf16)],
        ),
        out_shape=[jax.ShapeDtypeStruct((count, blocks * piece_rows, width), bf16)]
        + [jax.ShapeDtypeStruct((blocks * BLK, features), bf16)] * 3
        + [jax.ShapeDtypeStruct((blocks, features, BLK), bf16)] * 2,
        compiler_params=params(),
        cost_estimate=pl.CostEstimate(
            flops=6 * blocks * BLK * width * 3 * features,
            bytes_accessed=2 * blocks * BLK * (2 * width + 5 * features),
            transcendentals=0,
        ),
    )(me, *pieces, *operands, bias, gain, shift)


def per_head(stack_ref, value, heads):
    lane = lax.broadcasted_iota(jnp.int32, value.shape, 1) // HEAD
    for h in range(heads):
        stack_ref[h * BLK : (h + 1) * BLK] = jnp.where(lane == h, value, jnp.zeros_like(value))


def in_pairs(lo, hi, step, carry):
    pairs = (hi - lo) // 2
    carry = lax.fori_loop(0, pairs, lambda i, c: step(lo + 2 * i, 2, c), carry)
    return lax.fori_loop(lo + 2 * pairs, hi, lambda kb, c: step(kb, 1, c), carry)


def attend_kernel(count, heads, lo_ref, hi_ref, *refs):
    q_ref, k_ref, vt_ref, imgq_ref, imgk_ref = refs[:5]
    outs, (ot_ref, lse_ref) = refs[5 : 5 + count], refs[5 + count : 7 + count]
    s_ref, qs_ref, acc_ref = refs[7 + count :]
    block = pl.program_id(0)
    lo, hi = lo_ref[block], hi_ref[block]
    per_head(qs_ref, q_ref[...], heads)
    imgq = imgq_ref[...]

    def first(kb, width, tops):
        rows = pl.ds(pl.multiple_of(kb * BLK, BLK), width * BLK)
        allowed = imgk_ref[rows, :] == imgq
        s = nt(k_ref[rows, :], qs_ref[...])
        new = []
        for h in range(heads):
            cols = slice(h * BLK, (h + 1) * BLK)
            part = jnp.where(allowed, s[:, cols], NEG)
            for j in range(width):
                s_ref[kb - lo + j, :, cols] = part[j * BLK : (j + 1) * BLK]
            high = jnp.max(part.reshape(width * BLK // 8, 8, BLK), axis=0)
            new.append(jnp.maximum(tops[h], high))
        return tuple(new)

    tops = in_pairs(lo, hi, first, (jnp.full((8, BLK), NEG, f32),) * heads)
    tops = [jnp.max(t, axis=0, keepdims=True) for t in tops]
    acc_ref[...] = jnp.zeros_like(acc_ref)

    def second(kb, width, sums):
        new = []
        for h in range(heads):
            rows, cols = slice(h * HEAD, (h + 1) * HEAD), slice(h * BLK, (h + 1) * BLK)
            part, weights = 0.0, sums[h]
            for j in range(width):
                p = jnp.exp(s_ref[kb - lo + j, :, cols] - tops[h])
                weights = weights + jnp.sum(p.reshape(BLK // 8, 8, BLK), axis=0)
                part = part + matmul(vt_ref[kb + j, rows, :], p.astype(bf16))
            new.append(weights)
            acc_ref[rows, :] += part
        return tuple(new)

    sums = in_pairs(lo, hi, second, (jnp.zeros((8, BLK), f32),) * heads)
    sums = [jnp.sum(t, axis=0, keepdims=True) for t in sums]
    for h in range(heads):
        rows = slice(h * HEAD, (h + 1) * HEAD)
        acc_ref[rows, :] = acc_ref[rows, :] / sums[h]
    lse_ref[...] = jnp.concatenate(
        [t + jnp.log(s) for t, s in zip(tops, sums)] + [jnp.zeros((8 - heads, BLK), f32)], axis=0
    )
    ot_ref[0] = acc_ref[...]
    out = acc_ref[...].T.astype(bf16)
    for d in range(count):
        outs[d][...] = out[d * (BLK // count) : (d + 1) * (BLK // count)]


def attend_call(q, k, vt, imgq, imgk, lo, hi, count):
    blocks, features = vt.shape[0], q.shape[1]
    heads = features // HEAD
    piece_rows = BLK // count
    whole = lambda a: pl.BlockSpec(
        a.shape, lambda b, *_: (0,) * a.ndim, pipeline_mode=pl.Buffered(1)
    )
    return pl.pallas_call(
        functools.partial(attend_kernel, count, heads),
        grid_spec=pltpu.PrefetchScalarGridSpec(
            num_scalar_prefetch=2,
            grid=(blocks,),
            in_specs=[
                pl.BlockSpec((BLK, features), lambda b, *_: (b, 0)),
                whole(k),
                whole(vt),
                pl.BlockSpec((1, BLK), lambda b, *_: (0, b)),
                whole(imgk),
            ],
            out_specs=[pl.BlockSpec((piece_rows, features), lambda b, *_: (b, 0))] * count
            + [
                pl.BlockSpec((1, features, BLK), lambda b, *_: (b, 0, 0)),
                pl.BlockSpec((8, BLK), lambda b, *_: (0, b)),
            ],
            scratch_shapes=[
                pltpu.VMEM((blocks, BLK, heads * BLK), f32),
                pltpu.VMEM((heads * BLK, features), bf16),
                pltpu.VMEM((features, BLK), f32),
            ],
        ),
        out_shape=[jax.ShapeDtypeStruct((blocks * piece_rows, features), bf16)] * count
        + [
            jax.ShapeDtypeStruct((blocks, features, BLK), f32),
            jax.ShapeDtypeStruct((8, blocks * BLK), f32),
        ],
        compiler_params=params(),
        cost_estimate=pl.CostEstimate(
            flops=10 * (blocks * BLK) ** 2 * features,
            bytes_accessed=2 * blocks * BLK * features * 8,
            transcendentals=0,
        ),
    )(lo, hi, q, k, vt, imgq, imgk)


def attend_back_kernel(count, heads, first, waits, lo_ref, hi_ref, *refs):
    pieces, refs = refs[:count], refs[:count] + refs[count + waits :]
    q_ref, k_ref, v_ref, kt_ref, ot_ref, lse_ref, imgq_ref, imgk_ref = refs[count : count + 8]
    groups = count // 2
    outs, sums_ref = refs[count + 8 : count + groups + 8], refs[count + groups + 8]
    qs_ref, dos_ref, p_ref, ds_ref, dqt_ref, dk_ref, dv_ref = refs[count + groups + 9 :]
    block = pl.program_id(0)
    lo, hi = lo_ref[block], hi_ref[block]
    piece_rows = BLK // count
    wide = heads * HEAD

    @pl.when(block == 0)
    def _():
        dk_ref[...] = jnp.zeros_like(dk_ref)
        dv_ref[...] = jnp.zeros_like(dv_ref)
        sums_ref[...] = jnp.zeros_like(sums_ref)

    grad = jnp.concatenate([ref[...] for ref in pieces], axis=0)
    query = q_ref[...]
    lane = lax.broadcasted_iota(jnp.int32, grad.shape, 1) // HEAD
    for h in range(heads):
        dos_ref[h * BLK : (h + 1) * BLK] = jnp.where(lane == h, grad, jnp.zeros_like(grad))
        qs_ref[h * BLK : (h + 1) * BLK] = jnp.where(lane == h, query, jnp.zeros_like(query))
    both = grad.astype(f32).T * ot_ref[0]
    delta = [
        jnp.sum(both[h * HEAD : (h + 1) * HEAD], axis=0, keepdims=True) for h in range(heads)
    ]
    logsum = [lse_ref[first + h : first + h + 1, :] for h in range(heads)]
    imgq = imgq_ref[...]
    dqt_ref[...] = jnp.zeros_like(dqt_ref)

    def step(kb, width):
        length = width * BLK
        rows = pl.ds(pl.multiple_of(kb * BLK, BLK), length)
        keys, values = k_ref[rows, :], v_ref[rows, :]
        allowed = imgk_ref[rows, :] == imgq
        s = nt(keys, qs_ref[...])
        dp = nt(values, dos_ref[...])
        for h in range(heads):
            cols = slice(h * BLK, (h + 1) * BLK)
            p = jnp.exp(jnp.where(allowed, s[:, cols] - logsum[h], NEG))
            p_ref[:length, cols] = p.astype(bf16)
            ds_ref[:length, cols] = (p * (dp[:, cols] - delta[h])).astype(bf16)
        dv_ref[rows, :] += matmul(p_ref[:length], dos_ref[...])
        dk_ref[rows, :] += matmul(ds_ref[:length], qs_ref[...])
        for h in range(heads):
            cols, feats = slice(h * BLK, (h + 1) * BLK), slice(h * HEAD, (h + 1) * HEAD)
            total = 0.0
            for j in range(width):
                ds = ds_ref[j * BLK : (j + 1) * BLK, cols]
                total = total + matmul(kt_ref[kb + j, feats, :], ds)
            dqt_ref[feats, :] += total

    def pair(i, _):
        step(lo + 2 * i, 2)
        return 0

    lax.fori_loop(0, (hi - lo) // 2, pair, 0)

    @pl.when((hi - lo) % 2 == 1)
    def _():
        step(hi - 1, 1)

    dq = dqt_ref[...].T * 0.125
    sums_ref[0:1, :] += jnp.sum(dq, axis=0, keepdims=True)
    here = pl.ds(pl.multiple_of(block * piece_rows, piece_rows), piece_rows)
    for d in range(count):
        outs[d // 2][d % 2, here, :wide] = dq[d * piece_rows : (d + 1) * piece_rows].astype(bf16)

    @pl.when(block == pl.num_programs(0) - 1)
    def _():
        sums_ref[1:2, :] = jnp.sum(dv_ref[...], axis=0, keepdims=True)

        def move(b, _):
            to = pl.ds(pl.multiple_of(b * piece_rows, piece_rows), piece_rows)
            for d in range(count):
                at = pl.ds(pl.multiple_of(b * BLK + d * piece_rows, piece_rows), piece_rows)
                outs[d // 2][d % 2, to, wide : 2 * wide] = dk_ref[at, :].astype(bf16)
                outs[d // 2][d % 2, to, 2 * wide :] = dv_ref[at, :].astype(bf16)
            return 0

        lax.fori_loop(0, pl.num_programs(0), move, 0)


def attend_back_call(pieces, q, k, v, kt, ot, lse, imgq, imgk, lo, hi, split, after):
    count, (rows, wide) = len(pieces), pieces[0].shape
    blocks = kt.shape[0]
    heads = wide // HEAD
    once = pl.Buffered(1)
    half = pl.BlockSpec((blocks * BLK, wide), lambda b, *_: (0, split), pipeline_mode=once)
    out = jax.ShapeDtypeStruct((2, rows, 3 * wide), bf16)
    return pl.pallas_call(
        functools.partial(attend_back_kernel, count, heads, split * heads, len(after)),
        grid_spec=pltpu.PrefetchScalarGridSpec(
            num_scalar_prefetch=2,
            grid=(blocks,),
            in_specs=[pl.BlockSpec((BLK // count, wide), lambda b, *_: (b, 0))] * count
            + [ANYWHERE] * len(after)
            + [
                pl.BlockSpec((BLK, wide), lambda b, *_: (b, split)),
                half,
                half,
                pl.BlockSpec((blocks, wide, BLK), lambda b, *_: (0, split, 0), pipeline_mode=once),
                pl.BlockSpec((1, wide, BLK), lambda b, *_: (b, split, 0)),
                pl.BlockSpec((8, BLK), lambda b, *_: (0, b)),
                pl.BlockSpec((1, BLK), lambda b, *_: (0, b)),
                pl.BlockSpec(imgk.shape, lambda b, *_: (0, 0), pipeline_mode=once),
            ],
            out_specs=[pl.BlockSpec(out.shape, lambda b, *_: (0, 0, 0), pipeline_mode=once)] * (count // 2)
            + [pl.BlockSpec((8, wide), lambda b, *_: (0, 0))],
            scratch_shapes=[
                pltpu.VMEM((heads * BLK, wide), bf16),
                pltpu.VMEM((heads * BLK, wide), bf16),
                pltpu.VMEM((2 * BLK, heads * BLK), bf16),
                pltpu.VMEM((2 * BLK, heads * BLK), bf16),
                pltpu.VMEM((wide, BLK), f32),
                pltpu.VMEM((blocks * BLK, wide), f32),
                pltpu.VMEM((blocks * BLK, wide), f32),
            ],
        ),
        out_shape=[out] * (count // 2) + [jax.ShapeDtypeStruct((8, wide), f32)],
        compiler_params=params(),
        cost_estimate=pl.CostEstimate(
            flops=16 * (blocks * BLK) ** 2 * wide,
            bytes_accessed=2 * blocks * BLK * wide * 12,
            transcendentals=0,
        ),
    )(lo, hi, *pieces, *after, q, k, v, kt, ot, lse, imgq, imgk)


def norm_back(grad, unit, rstd, gain):
    e = grad * gain
    mean = jnp.mean(e, axis=-1, keepdims=True)
    return (e - mean - unit * jnp.mean(e * unit, axis=-1, keepdims=True)) * rstd


def total(value):
    return jnp.sum(value, axis=0, keepdims=True)


def rows_kernel(count, splits, local_rows, *refs):
    (
        tok_ref,
        img_ref,
        w_out_ref,
        w_up_ref,
        w_down_ref,
        learn_in_ref,
        learn_out_ref,
        vec_ref,
        up_bias_ref,
        out_bias_ref,
        pooled_grad_ref,
    ) = refs[:11]
    attended = refs[11 : 11 + count]
    at = 11 + count
    (
        n2_ref,
        gated_ref,
        gup_ref,
        gres_ref,
        n3_ref,
        glearn_ref,
        inner_ref,
        glogit_ref,
        ghid_ref,
        ghid_f32_ref,
    ) = refs[at : at + 10]
    gatt = refs[at + 10 : at + 10 + count * splits]
    at += 10 + count * splits
    pooled_ref, vsum_ref, usum_ref, lsum_ref = refs[at : at + 4]
    hid_ref, res_ref, dgate_ref, up0_ref, up1_ref = refs[at + 4 :]
    step = pl.program_id(0)
    rows, width = tok_ref.shape
    hidden_units = w_up_ref.shape[1]
    chunk = up0_ref.shape[1]
    chunks = hidden_units // chunk

    @pl.when(step == 0)
    def _():
        for ref in (pooled_ref, vsum_ref, usum_ref, lsum_ref):
            ref[...] = jnp.zeros_like(ref)

    def vec(i):
        return vec_ref[i : i + 1, :]

    position = lax.broadcasted_iota(jnp.int32, (rows, 1), 0) + step * rows
    tok = jnp.where(position < local_rows, tok_ref[...].astype(f32), 0.0)
    low = jnp.concatenate([ref[...] for ref in attended], axis=1)
    hidden = tok + matmul(low, w_out_ref[...]) + vec(0)
    hid_ref[...] = hidden
    unit, _ = norm_parts(hidden)
    n2_ref[...] = (unit * vec(2) + vec(3)).astype(bf16)

    def columns(j):
        return pl.ds(pl.multiple_of(j * chunk, chunk), chunk)

    def up(ref, j):
        ref[...] = matmul(n2_ref[...], w_up_ref[:, columns(j)])

    def gate(ref, j):
        value, slope = smooth_both(ref[...] + up_bias_ref[:, columns(j)])
        gated_ref[:, columns(j)] = value.astype(bf16)
        dgate_ref[:, columns(j)] = slope

    up(up0_ref, 0)

    def pair(i, _):
        up(up1_ref, 2 * i + 1)
        gate(up0_ref, 2 * i)
        up(up0_ref, jnp.minimum(2 * i + 2, chunks - 1))
        gate(up1_ref, 2 * i + 1)
        return 0

    lax.fori_loop(0, chunks // 2, pair, 0)
    result = hid_ref[...] + matmul(gated_ref[...], w_down_ref[...]) + vec(1)
    res_ref[...] = result
    unit, rstd = norm_parts(result)
    n3_ref[...] = (unit * vec(4) + vec(5)).astype(bf16)
    inner, slope = smooth_both(matmul(n3_ref[...], learn_in_ref[...]) + vec(6))
    inner_ref[...] = inner.astype(bf16)
    maps = jax.nn.sigmoid(matmul(inner_ref[...], learn_out_ref[...]) + out_bias_ref[...])
    member = lax.broadcasted_iota(jnp.int32, maps.shape, 1) // LT == img_ref[...]
    spread = jnp.where(member, maps, 0.0).astype(bf16)
    result_low = res_ref[...].astype(bf16)
    pooled_ref[...] += tn(spread, result_low)
    grad_spread = nt(result_low, pooled_grad_ref[...])
    grad_logit = jnp.where(member, grad_spread * maps * (1.0 - maps), 0.0)
    lsum_ref[...] += total(grad_logit)
    glogit_ref[...] = grad_logit.astype(bf16)
    grad_pre = nt(glogit_ref[...], learn_out_ref[...]) * slope
    vsum_ref[6:7, :] += total(grad_pre)
    glearn_ref[...] = grad_pre.astype(bf16)
    back = nt(glearn_ref[...], learn_in_ref[...])
    unit, rstd = norm_parts(res_ref[...])
    vsum_ref[4:5, :] += total(back * unit)
    vsum_ref[5:6, :] += total(back)
    grad_result = matmul(spread, pooled_grad_ref[...]) + norm_back(back, unit, rstd, vec(4))
    vsum_ref[1:2, :] += total(grad_result)
    res_ref[...] = grad_result
    gres_ref[...] = grad_result.astype(bf16)

    def down_back(j, _):
        grad = nt(gres_ref[...], w_down_ref[columns(j), :]) * dgate_ref[:, columns(j)]
        usum_ref[:, columns(j)] += total(grad)
        gup_ref[:, columns(j)] = grad.astype(bf16)
        return 0

    lax.fori_loop(0, chunks, down_back, 0)
    back = nt(gup_ref[...], w_up_ref[...])
    unit, rstd = norm_parts(hid_ref[...])
    vsum_ref[2:3, :] += total(back * unit)
    vsum_ref[3:4, :] += total(back)
    grad_hidden = res_ref[...] + norm_back(back, unit, rstd, vec(2))
    vsum_ref[0:1, :] += total(grad_hidden)
    ghid_f32_ref[...] = grad_hidden
    ghid_ref[...] = grad_hidden.astype(bf16)
    grad = nt(ghid_ref[...], w_out_ref[...]).astype(bf16)
    wide = width // (count * splits)
    for i in range(count * splits):
        gatt[i][...] = grad[:, i * wide : (i + 1) * wide]


def rows_call(tok, img, attended, w_out, w_up, w_down, learn_in, learn_out, vecs, up_bias, out_bias, pooled_grad, splits):
    count, (rows, features) = len(attended), attended[0].shape
    local_rows, width = tok.shape
    hidden_units = w_up.shape[1]
    inner = learn_in.shape[1]
    spread = learn_out.shape[1]
    block = min(ROW_BLOCK, rows)
    chunk = UP_BLOCK
    wide = features // splits
    once = lambda a: pl.BlockSpec(a.shape, lambda i: (0,) * a.ndim, pipeline_mode=pl.Buffered(1))
    by_rows = lambda n: pl.BlockSpec((block, n), lambda i: (i, 0))
    kept = lambda a: pl.BlockSpec(a.shape, lambda i: (0, 0))
    low = lambda n: jax.ShapeDtypeStruct((rows, n), bf16)
    lows = [width, hidden_units, hidden_units, width, width, inner, inner, spread, width]
    sums = [
        jax.ShapeDtypeStruct((spread, width), f32),
        jax.ShapeDtypeStruct((8, width), f32),
        jax.ShapeDtypeStruct((1, hidden_units), f32),
        jax.ShapeDtypeStruct((1, spread), f32),
    ]
    resident = [w_out, w_up, w_down, learn_in, learn_out, vecs, up_bias, out_bias, pooled_grad]
    return pl.pallas_call(
        functools.partial(rows_kernel, count, splits, local_rows),
        grid=(rows // block,),
        in_specs=[by_rows(width), by_rows(1)]
        + [once(a) for a in resident]
        + [by_rows(features)] * count,
        out_specs=[by_rows(n) for n in lows]
        + [by_rows(width)]
        + [by_rows(wide)] * (count * splits)
        + [kept(a) for a in sums],
        out_shape=[low(n) for n in lows]
        + [jax.ShapeDtypeStruct((rows, width), f32)]
        + [low(wide)] * (count * splits)
        + sums,
        scratch_shapes=[
            pltpu.VMEM((block, width), f32),
            pltpu.VMEM((block, width), f32),
            pltpu.VMEM((block, hidden_units), f32),
            pltpu.VMEM((block, chunk), f32),
            pltpu.VMEM((block, chunk), f32),
        ],
        compiler_params=params(),
        cost_estimate=pl.CostEstimate(
            flops=4 * rows * width * (width + 2 * hidden_units + inner),
            bytes_accessed=2 * (rows * 20 * width + 2 * width * hidden_units),
            transcendentals=0,
        ),
    )(tok, img, *resident, *attended)


def part_halves(me_ref, value, keep_ref, send_ref, whole_ref):
    half = value.shape[1] // 2
    core = me_ref[0] % 2
    whole_ref[...] = value
    keep_ref[...] = whole_ref[:, pl.ds(pl.multiple_of(core * half, half), half)]
    send_ref[...] = whole_ref[:, pl.ds(pl.multiple_of((1 - core) * half, half), half)]


def down_grad_kernel(waits, me_ref, left_ref, right_ref, *refs):
    part_halves(me_ref, tn(left_ref[...], right_ref[...]).astype(bf16), *refs[waits:])


def down_grad_call(me, left, right, after=()):
    rows, m = left.shape
    n = right.shape[1]
    out = pl.BlockSpec((GRAD_BLOCK, n // 2), lambda j, m: (j, 0))
    return pl.pallas_call(
        functools.partial(down_grad_kernel, len(after)),
        grid_spec=pltpu.PrefetchScalarGridSpec(
            num_scalar_prefetch=1,
            grid=(m // GRAD_BLOCK,),
            in_specs=[
                pl.BlockSpec((rows, GRAD_BLOCK), lambda j, m: (0, j)),
                pl.BlockSpec((rows, n), lambda j, m: (0, 0), pipeline_mode=pl.Buffered(1)),
            ]
            + [ANYWHERE] * len(after),
            out_specs=[out, out],
            scratch_shapes=[pltpu.VMEM((GRAD_BLOCK, n), bf16)],
        ),
        out_shape=[jax.ShapeDtypeStruct((m, n // 2), bf16)] * 2,
        compiler_params=params(),
        cost_estimate=pl.CostEstimate(
            flops=3 * rows * m * n, bytes_accessed=4 * m * n, transcendentals=0
        ),
    )(me, left, right, *after)


def up_grad_kernel(half, waits, me_ref, left_ref, right_ref, *refs):
    keep_ref, send_ref = refs[waits:]
    value = tn(left_ref[...], right_ref[...]).astype(bf16)

    @pl.when(pl.program_id(0) < half)
    def _():
        send_ref[...] = value

    @pl.when(pl.program_id(0) >= half)
    def _():
        keep_ref[...] = value


def up_grad_call(me, left, right, after=()):
    rows, m = left.shape
    n = right.shape[1]
    half = n // GRAD_BLOCK // 2

    def column(j, core):
        return jnp.where(j < half, (1 - core) * half + j, core * half + j - half)

    return pl.pallas_call(
        functools.partial(up_grad_kernel, half, len(after)),
        grid_spec=pltpu.PrefetchScalarGridSpec(
            num_scalar_prefetch=1,
            grid=(2 * half,),
            in_specs=[
                pl.BlockSpec((rows, m), lambda j, me: (0, 0), pipeline_mode=pl.Buffered(1)),
                pl.BlockSpec((rows, GRAD_BLOCK), lambda j, me: (0, column(j, me[0] % 2))),
            ]
            + [ANYWHERE] * len(after),
            out_specs=[
                pl.BlockSpec((m, GRAD_BLOCK), lambda j, me: (0, jnp.maximum(j - half, 0))),
                pl.BlockSpec((m, GRAD_BLOCK), lambda j, me: (0, jnp.minimum(j, half - 1))),
            ],
        ),
        out_shape=[jax.ShapeDtypeStruct((m, n // 2), bf16)] * 2,
        compiler_params=params(),
        cost_estimate=pl.CostEstimate(
            flops=3 * rows * m * n, bytes_accessed=4 * m * n, transcendentals=0
        ),
    )(me, left, right, *after)


def small_grad_kernel(count, me_ref, *refs):
    n3_ref, glearn_ref, ghid_ref, inner_ref, glogit_ref = refs[:5]
    attended = refs[5 : 5 + count]
    keep_ref, send_ref, lout_ref, learn_ref, wout_ref = refs[5 + count :]
    learn_ref[...] = tn(n3_ref[...], glearn_ref[...]).astype(bf16)
    lout_ref[...] = tn(inner_ref[...], glogit_ref[...])
    features = attended[0].shape[1]
    for d in range(count):
        owner = jnp.bitwise_xor(me_ref[0], d)
        to = pl.ds(pl.multiple_of(owner * features, features), features)
        wout_ref[to, :] = tn(attended[d][...], ghid_ref[...]).astype(bf16)
    first = me_ref[0] % 2 == 0

    @pl.when(first)
    def _():
        keep_ref[...] = learn_ref[...]
        send_ref[...] = wout_ref[...]

    @pl.when(jnp.logical_not(first))
    def _():
        keep_ref[...] = wout_ref[...]
        send_ref[...] = learn_ref[...]


def small_grad_call(me, n3, glearn, ghid, inner, glogit, attended):
    rows, width = n3.shape
    operands = [n3, glearn, ghid, inner, glogit, *attended]
    out = jax.ShapeDtypeStruct((width, ghid.shape[1]), bf16)
    lout = jax.ShapeDtypeStruct((inner.shape[1], glogit.shape[1]), f32)
    once = lambda a: pl.BlockSpec(a.shape, lambda j, m: (0, 0), pipeline_mode=pl.Buffered(1))
    return pl.pallas_call(
        functools.partial(small_grad_kernel, len(attended)),
        grid_spec=pltpu.PrefetchScalarGridSpec(
            num_scalar_prefetch=1,
            grid=(1,),
            in_specs=[once(a) for a in operands],
            out_specs=[once(out), once(out), once(lout)],
            scratch_shapes=[pltpu.VMEM(out.shape, bf16), pltpu.VMEM(out.shape, bf16)],
        ),
        out_shape=[out, out, lout],
        compiler_params=params(),
        cost_estimate=pl.CostEstimate(
            flops=6 * rows * width * width, bytes_accessed=20 * width * width, transcendentals=0
        ),
    )(me, *operands)


def qkv_grad_kernel(groups, waits, me_ref, n_ref, gain_ref, shift_ref, *refs):
    parts, weights = refs[:groups], refs[groups : groups + 3]
    out_ref, sums_ref, acc_ref, sum_ref = refs[groups + 3 + waits :]
    step = pl.program_id(0)
    wide = weights[0].shape[1]
    for d in range(2 * groups):

        @pl.when(step == d)
        def _():
            mixed = parts[d // 2][d % 2]
            part = tn(n_ref[0], mixed)
            column = total(mixed.astype(f32))
            acc_ref[...] = part if d == 0 else acc_ref[...] + part
            sum_ref[...] = column if d == 0 else sum_ref[...] + column

    @pl.when(step == 2 * groups - 1)
    def _():
        by_unit, column = acc_ref[...], sum_ref[...]
        out_ref[...] = (by_unit * gain_ref[...] + shift_ref[...] * column).astype(bf16)
        weight = jnp.concatenate([ref[...].astype(f32) for ref in weights], axis=1)
        sums_ref[:, 0:1] = jnp.sum(by_unit * weight, axis=1, keepdims=True)
        sums_ref[:, 1:2] = jnp.sum(weight * column, axis=1, keepdims=True)


def qkv_grad_call(me, unit, parts, w_qkv, gain, shift, split, splits, after=()):
    count, rows, width = unit.shape
    columns = parts[0].shape[2]
    once = lambda a: pl.BlockSpec(
        a.shape, lambda d, m: (0,) * len(a.shape), pipeline_mode=pl.Buffered(1)
    )
    specs, operands = own_columns(w_qkv, width // count, splits, [split])
    return pl.pallas_call(
        functools.partial(qkv_grad_kernel, count // 2, len(after)),
        grid_spec=pltpu.PrefetchScalarGridSpec(
            num_scalar_prefetch=1,
            grid=(count,),
            in_specs=[pl.BlockSpec((1, rows, width), lambda d, m: (d, 0, 0)), once(gain), once(shift)]
            + [once(a) for a in parts]
            + specs
            + [ANYWHERE] * len(after),
            out_specs=[
                pl.BlockSpec((width, columns), lambda d, m: (0, 0)),
                pl.BlockSpec((width, 2), lambda d, m: (0, 0)),
            ],
            scratch_shapes=[pltpu.VMEM((width, columns), f32), pltpu.VMEM((1, columns), f32)],
        ),
        out_shape=[
            jax.ShapeDtypeStruct((width, columns), bf16),
            jax.ShapeDtypeStruct((width, 2), f32),
        ],
        compiler_params=params(),
        cost_estimate=pl.CostEstimate(flops=1 << 34, bytes_accessed=1 << 10, transcendentals=0),
    )(me, unit, gain, shift, *parts, *operands, *after)


def tokens_kernel(groups, splits, me_ref, tok_ref, ghid_ref, w_ref, gain_ref, *refs):
    same, other = refs[: groups * splits], refs[groups * splits : groups * splits + splits]
    out_ref, mixed_ref = refs[groups * splits + splits :]
    width = tok_ref.shape[1]
    features = width // (2 * groups)
    wide = features // splits
    for d in range(2 * groups):
        owner = jnp.bitwise_xor(me_ref[0], d) * features
        for s in range(splits):
            for part in range(3):
                to = pl.ds(pl.multiple_of(part * width + owner + s * wide, wide), wide)
                at = slice(part * wide, (part + 1) * wide)
                if d % 2 == 0:
                    mixed_ref[:, to] = same[s * groups + d // 2][0, :, at]
                else:
                    mixed_ref[:, to] = other[s][d // 2, :, at]
    back = nt(mixed_ref[...], w_ref[...])
    unit, rstd = norm_parts(tok_ref[...].astype(f32))
    out_ref[0] = ghid_ref[...] + norm_back(back, unit, rstd, gain_ref[...])


def tokens_call(me, tok, ghid, w_qkv, gain, same, other, count):
    local_rows, width = tok.shape
    columns = same[0].shape[2]
    groups, splits = count // 2, len(other)
    block = 256
    by_rows = lambda n: pl.BlockSpec((block, n), lambda i, m: (i, 0))
    return pl.pallas_call(
        functools.partial(tokens_kernel, groups, splits),
        grid_spec=pltpu.PrefetchScalarGridSpec(
            num_scalar_prefetch=1,
            grid=(pl.cdiv(local_rows, block),),
            in_specs=[
                by_rows(width),
                by_rows(width),
                pl.BlockSpec(w_qkv.shape, lambda i, m: (0, 0), pipeline_mode=pl.Buffered(1)),
                pl.BlockSpec(gain.shape, lambda i, m: (0, 0)),
            ]
            + [pl.BlockSpec((1, block, columns), lambda i, m: (0, i, 0))] * len(same)
            + [pl.BlockSpec((groups, block, columns), lambda i, m: (0, i, 0))] * splits,
            out_specs=pl.BlockSpec((1, block, width), lambda i, m: (0, i, 0)),
            scratch_shapes=[pltpu.VMEM((block, 3 * width), bf16)],
        ),
        out_shape=jax.ShapeDtypeStruct((1, local_rows, width), f32),
        compiler_params=params(),
        cost_estimate=pl.CostEstimate(flops=1 << 34, bytes_accessed=1 << 10, transcendentals=0),
    )(me, tok, ghid, w_qkv, gain, *same, *other)


def flip(index, bit):
    return index + bit - 2 * bit * ((index // bit) % 2)


def vectors_kernel(count, row_bits, img_bits, vec_ref, slot_ref, out_ref, sum_ref, *scratch):
    recv, slot_recv, send_sem, recv_sem, slot_send, slot_got = scratch
    row, img = lax.axis_index("row"), lax.axis_index("img")

    def partner(row_mask, img_mask=0):
        r, g = row, img
        for bit in row_bits:
            r = flip(r, bit) if row_mask & bit else r
        for bit in img_bits:
            g = flip(g, bit) if img_mask & bit else g
        return (g, r)

    steps = [(bit, 0) for bit in row_bits] + [(0, bit) for bit in img_bits]
    everyone = sorted(set(steps) | {(d, 0) for d in range(1, count)})
    barrier = pltpu.get_barrier_semaphore()
    for masks in everyone:
        pl.semaphore_signal(
            barrier, inc=1, device_id=partner(*masks), device_id_type=pl.DeviceIdType.MESH
        )
    pl.semaphore_wait(barrier, len(everyone))
    slots = []
    for d in range(1, count):
        copy = pltpu.make_async_remote_copy(
            src_ref=slot_ref.at[d],
            dst_ref=slot_recv.at[d - 1],
            send_sem=slot_send.at[d - 1],
            recv_sem=slot_got.at[d - 1],
            device_id=partner(d),
            device_id_type=pl.DeviceIdType.MESH,
        )
        copy.start()
        slots.append(copy)
    out_ref[...] = vec_ref[...]
    for i, masks in enumerate(steps):
        copy = pltpu.make_async_remote_copy(
            src_ref=out_ref,
            dst_ref=recv.at[i],
            send_sem=send_sem.at[i],
            recv_sem=recv_sem.at[i],
            device_id=partner(*masks),
            device_id_type=pl.DeviceIdType.MESH,
        )
        copy.start()
        copy.wait()
        out_ref[...] = out_ref[...] + recv[i]
    for copy in slots:
        copy.wait()
    sum_ref[...] = tree(
        [slot_ref[0].astype(f32)] + [slot_recv[d - 1].astype(f32) for d in range(1, count)]
    )


def vectors_call(vec, slots):
    count = lax.axis_size("row")
    row_bits, img_bits = bits_of(count), bits_of(lax.axis_size("img"))
    steps = len(row_bits) + len(img_bits)
    whole = pl.BlockSpec(memory_space=pltpu.VMEM)
    return pl.pallas_call(
        functools.partial(vectors_kernel, count, row_bits, img_bits),
        in_specs=[whole, whole],
        out_specs=[whole, whole],
        out_shape=[
            jax.ShapeDtypeStruct(vec.shape, f32),
            jax.ShapeDtypeStruct(slots.shape[1:], f32),
        ],
        scratch_shapes=[
            pltpu.VMEM((steps,) + vec.shape, f32),
            pltpu.VMEM((count - 1,) + slots.shape[1:], bf16),
            pltpu.SemaphoreType.DMA((steps,)),
            pltpu.SemaphoreType.DMA((steps,)),
            pltpu.SemaphoreType.DMA((count - 1,)),
            pltpu.SemaphoreType.DMA((count - 1,)),
        ],
        compiler_params=pltpu.CompilerParams(
            collective_id=0, has_side_effects=True, vmem_limit_bytes=32 << 20
        ),
        cost_estimate=pl.CostEstimate(flops=1 << 34, bytes_accessed=1 << 10, transcendentals=0),
    )(vec, slots)


def rows_of(array, index, length):
    return lax.dynamic_slice_in_dim(array, index * length, length, 0)


def on_device(
    tokens,
    counts,
    owner,
    w_qkv,
    qv_bias,
    w_out,
    out_bias,
    w_up,
    up_bias,
    w_down,
    down_bias,
    norm_gain,
    norm_bias,
    learn_in,
    learn_in_bias,
    learn_out,
    learn_out_bias,
    cotangent,
):
    width = tokens.shape[2]
    local_rows = tokens.shape[1]
    row_count = lax.axis_size("row")
    images_count = lax.axis_size("img")
    device = lax.axis_index("row")
    image_device = lax.axis_index("img")
    features = width // row_count
    wide = min(features, 128)
    splits = features // wide
    slots_here = IMGS // row_count
    group_counts = counts[0]
    partners = [device ^ d for d in range(row_count)]
    row_bits, img_bits = stages()
    n_img = len(img_bits)

    piece_rows = BLK // row_count
    blocks = pl.cdiv(local_rows, piece_rows)
    images = jnp.stack([row_images(group_counts, p, local_rows, row_count) for p in partners])
    extra = blocks * piece_rows - local_rows
    images = jnp.pad(images, ((0, 0), (0, extra)), constant_values=IMGS + 1)
    image_here = images[0].reshape(-1, 1)
    images = images.reshape(row_count, blocks, piece_rows).transpose(1, 0, 2).reshape(blocks, BLK)
    least, most = jnp.min(images, axis=1), jnp.max(images, axis=1)
    lo = jnp.sum((most[None, :] < least[:, None]).astype(jnp.int32), axis=1)
    hi = jnp.sum((least[None, :] <= most[:, None]).astype(jnp.int32), axis=1)
    imgq, imgk = images.reshape(1, -1), images.reshape(-1, 1)

    me = device.reshape(1)
    w_out_here = jnp.concatenate([rows_of(w_out, p, features) for p in partners], axis=0)
    bias_here = lax.dynamic_slice_in_dim(qv_bias, device * features, features, 1)
    grads_in = gather_pieces(cotangent[0].reshape(slots_here, LT * width).astype(bf16))
    pieces = gather_pieces(
        tokens[0], [imgq, imgk, lo, hi, image_here, w_out_here, bias_here, grads_in[-1]]
    )

    unit, q, k, v, kt, vt = qkv_call(
        me, pieces, w_qkv, bias_here, norm_gain[0:1], norm_bias[0:1], splits
    )
    *attended, ot, lse = attend_call(q, k, vt, imgq, imgk, lo, hi, row_count)
    attended = send_pieces(attended)

    slot_rel = ((owner[0] // slots_here) ^ device) * slots_here + owner[0] % slots_here
    select = (slot_rel[:, None] == jnp.arange(IMGS, dtype=jnp.int32)[None, :]).astype(f32)
    scale = lax.rsqrt(group_counts.astype(f32))
    incoming = jnp.concatenate(grads_in, axis=0).astype(f32)
    grad_pooled = jnp.dot(select, incoming, precision=highest) * scale[:, None]
    grad_pooled_low = grad_pooled.reshape(IMGS * LT, width).astype(bf16)

    vecs = jnp.concatenate(
        [
            out_bias[None],
            down_bias[None],
            norm_gain[1:2],
            norm_bias[1:2],
            norm_gain[2:3],
            norm_bias[2:3],
            learn_in_bias[None],
            jnp.zeros((1, width), f32),
        ],
        axis=0,
    )
    out = rows_call(
        tokens[0],
        image_here,
        attended,
        w_out_here,
        w_up,
        w_down,
        learn_in,
        jnp.tile(learn_out, (1, IMGS)),
        vecs,
        up_bias[None],
        jnp.tile(learn_out_bias, IMGS)[None],
        grad_pooled_low,
        splits,
    )
    n2, gated, gup, gres, n3, glearn, inner, glogit, ghid, grad_hidden = out[:10]
    grad_attended = out[10 : 10 + row_count * splits]
    pooled, vec_sums, up_sums, logit_sums = out[10 + row_count * splits :]
    grad_attended = [send_pieces(grad_attended[s::splits]) for s in range(splits)]

    core, far_row = row_bits[:1], row_bits[1:]
    y_bits, z_bits = img_bits[:1], [[bit] for bit in img_bits[1:]]
    half = lambda value, bits: Halving(value, bits, n_img)

    def core_flight(keep, send):
        flight = Exchange(keep, [])
        flight.moved = [jump(send, 1)]
        return flight

    keep_small, send_small, grad_learn_out = small_grad_call(
        me, n3, glearn, ghid, inner, glogit, attended
    )
    keep_down, send_down = down_grad_call(me, gated, gres, [send_small])
    keep_up, send_up = up_grad_call(me, n2, gup, [send_down])
    small, down = arrive(
        [core_flight(keep_small, send_small), core_flight(keep_down, send_down)], [send_up]
    )
    small, down = spread_img(small), spread_img(down)

    def back_call(s, after):
        *parts, sums = attend_back_call(
            grad_attended[s], q, k, v, kt, ot, lse, imgq, imgk, lo, hi, s, after
        )
        return parts, sums

    def grad_qkv_call(s, parts, after):
        turned = [norm_gain[0].reshape(-1, 1), norm_bias[0].reshape(-1, 1)]
        return qkv_grad_call(me, unit, parts, w_qkv, *turned, s, splits, after)

    groups = row_count // 2
    far_masks = [(2 * g, 0) for g in range(1, groups)]
    same, qkv_sums, norm_sums, grad_qkv = [], [], [], []
    after, far = [small, down, send_up], None
    for s in range(splits):
        parts, sums = back_call(s, after)
        qkv_sums.append(sums[0:2])
        if s == 0:
            small, down, ups = arrive(
                [half(small, y_bits), half(down, z_bits[0]), core_flight(keep_up, send_up)], [sums]
            )
            ups = spread_img(ups)
        if s == splits - 1:
            flights = [half(ups, y_bits), half(down, z_bits[1]), half(small, z_bits[0])]
            if far is not None:
                flights.append(far)
            ups, down, small, *arrived = arrive(flights, [sums])
            for pieces_far in arrived:
                same += pieces_far
        same.append(parts[0])
        far = Moved(parts[1:], far_masks)
        grad, norm_sum = grad_qkv_call(s, parts, [ups, down])
        if s == splits - 1:
            (ups, arrived, down, small), (grad, norm_sum) = arrive_with(
                [half(ups, z_bits[0]), far, half(down, y_bits), half(small, z_bits[1])],
                (grad, norm_sum),
            )
            same += arrived
        norm_sums.append(norm_sum)
        grad_qkv.append(spread_img(grad))
        after = [grad]
    grad_qkv = jnp.concatenate(grad_qkv, axis=-1)
    near = Moved([jnp.stack([p[1] for p in same])], [(1, 0)])

    by_slot = jnp.dot(select.T, pooled.reshape(IMGS, LT * width), precision=highest)
    by_slot = by_slot.astype(bf16).reshape(row_count, -1, 128)
    late = lax.dynamic_update_slice(
        jnp.zeros((2, width), f32), jnp.concatenate(qkv_sums, axis=1), (0, device * features)
    )
    vectors = jnp.concatenate(
        [
            up_sums.reshape(-1),
            vec_sums.reshape(-1),
            jnp.sum(grad_learn_out.reshape(-1, IMGS, LT), axis=1).reshape(-1),
            late.reshape(-1),
            sum(norm_sums).T.reshape(-1),
            jnp.sum(logit_sums.reshape(IMGS, LT), axis=0),
        ]
    )
    vectors = jnp.pad(vectors, (0, -vectors.shape[0] % 1024)).reshape(-1, 128)
    made = vectors_call(vectors, by_slot)

    for bits in z_bits[2:]:
        down, small = arrive([half(down, bits), half(small, bits)])
    ((others,), grad_qkv, ups, down, small), (vectors, learned) = arrive_with(
        [
            near,
            half(grad_qkv, y_bits),
            half(ups, z_bits[1]),
            half(down, far_row),
            Exchange(small, far_row),
        ],
        tuple(made),
    )
    for bits in z_bits[2:]:
        ups, grad_qkv = arrive([half(ups, bits), half(grad_qkv, bits)])
    other = [others[s * groups : (s + 1) * groups] for s in range(splits)]
    grad_tokens = tokens_call(
        me,
        tokens[0],
        behind(grad_hidden, [ups, grad_qkv, down, small]),
        w_qkv,
        norm_gain[0:1],
        same,
        other,
        row_count,
    )
    (grad_qkv, ups), grad_tokens = arrive_with(
        [half(grad_qkv, z_bits[0]), Exchange(ups, far_row)], grad_tokens
    )
    (grad_qkv,) = arrive([half(grad_qkv, z_bits[1])])
    vectors, learned = behind((vectors, learned), [grad_tokens])
    vectors = vectors.reshape(-1)
    scale_here = jnp.dot(scale, select, precision=highest)[:slots_here]
    learned = learned.reshape(slots_here, LT * width) * scale_here[:, None]
    learned = learned.reshape(1, slots_here, LT, width)

    share_down = finish_weight(down, row_bits)
    share_small = finish_weight(small, core, [grad_tokens])
    share_up = finish_weight(ups, core)
    share_learn = share_small[:, : learn_in.shape[1]]
    share_out = share_small[:, learn_in.shape[1] :]
    shares = gather_columns(grad_qkv.reshape(grad_qkv.shape[-2:]), lambda c: c, row_bits)
    share_qkv = jnp.concatenate(
        [
            shares[c][:, (3 * s + part) * wide : (3 * s + part + 1) * wide]
            for part in range(3)
            for c in range(row_count)
            for s in range(splits)
        ],
        axis=1,
    ).astype(f32)

    at = up_bias.shape[0]
    up_sum, vec_sums = vectors[:at], vectors[at : at + 8 * width].reshape(8, width)
    at += 8 * width
    learn_out_sum = vectors[at : at + learn_out.size].reshape(learn_out.shape)
    at += learn_out.size
    late = vectors[at : at + 4 * width].reshape(4, width)
    at += 4 * width
    out_sum, down_sum, gain_two, shift_two, gain_three, shift_three, learn_in_sum = vec_sums[:7]
    share_learn_out = rows_of(learn_out_sum, image_device, learn_out.shape[0] // images_count)
    return (
        learned,
        grad_tokens,
        share_qkv,
        late[0:2],
        share_out,
        out_sum,
        share_up,
        up_sum,
        share_down,
        down_sum,
        jnp.stack([late[2], gain_two, gain_three]),
        jnp.stack([late[3], shift_two, shift_three]),
        share_learn,
        learn_in_sum,
        share_learn_out,
        vectors[at : at + learn_out.shape[1]],
    )


def solution(mesh):
    by_image = P("img", None)
    in_specs = (
        (P("img", "row", None), by_image, by_image) + (P(),) * 14 + (P("img", "row", None, None),)
    )
    out_specs = (
        P("img", "row", None, None),
        P("img", "row", None),
        by_image,
        P(),
        by_image,
        P(),
        by_image,
        P(),
        by_image,
        P(),
        P(),
        P(),
        by_image,
        P(),
        by_image,
        P(),
    )
    return jax.shard_map(
        on_device, mesh=mesh, in_specs=in_specs, out_specs=out_specs, check_vma=False
    )
```

```python
import functools

import jax
import jax.numpy as jnp
from jax import lax
from jax.experimental import pallas as pl
from jax.experimental.pallas import tpu as pltpu
from jax.sharding import PartitionSpec as P

HEADS = 16
HEAD = 64
LT = 8
IMGS = 8
BLK = 256
NEG = -1e30
VMEM = 60 << 20
ROW_BLOCK = 256
UP_BLOCK = 1024
GRAD_BLOCK = 1024

highest = lax.Precision.HIGHEST
epsilon = 1e-06
f32 = jnp.float32
bf16 = jnp.bfloat16


def smooth_both(v):
    half = jnp.abs(v) * 0.7071067811865476
    t = 1.0 / (1.0 + 0.3275911 * half)
    bell = jnp.exp(-half * half)
    poly = t * (
        0.127414796
        + t * (-0.142248368 + t * (0.7107068705 + t * (-0.7265760135 + t * 0.5307027145)))
    )
    tail = poly * bell
    cdf = jnp.where(v >= 0.0, 1.0 - tail, tail)
    return v * cdf, cdf + v * (bell * 0.3989422804014327)


def matmul(left, right):
    return jnp.dot(left, right, preferred_element_type=f32)


def nt(left, right):
    return lax.dot_general(left, right, (((1,), (1,)), ((), ())), preferred_element_type=f32)


def tn(left, right):
    return lax.dot_general(left, right, (((0,), (0,)), ((), ())), preferred_element_type=f32)


def row_images(counts, device, local_rows, row_count):
    upper_end = counts * (device + 1) // row_count
    lower_end = counts * device // row_count
    run_ends = jnp.cumsum(upper_end - lower_end)
    positions = jnp.arange(local_rows, dtype=jnp.int32)
    return jnp.sum((positions[:, None] >= run_ends[None, :]).astype(jnp.int32), axis=1)


def bits_of(size):
    return [1 << i for i in range(size.bit_length() - 1)]


def jump(value, row_mask, img_mask=0):
    rows, imgs = lax.axis_size("row"), lax.axis_size("img")
    if img_mask == 0:
        return lax.ppermute(value, "row", [(i, i ^ row_mask) for i in range(rows)])
    if row_mask == 0:
        return lax.ppermute(value, "img", [(i, i ^ img_mask) for i in range(imgs)])
    mask = img_mask * rows + row_mask
    return lax.ppermute(value, ("img", "row"), [(i, i ^ mask) for i in range(rows * imgs)])


def masks_of(bits):
    masks = []
    for e in range(1 << len(bits)):
        masks.append(
            tuple(
                sum(bit for j, (axis, bit) in enumerate(bits) if axis == name and e >> j & 1)
                for name in ("row", "img")
            )
        )
    return masks


def gather_pieces(value, count):
    pieces = {0: value}
    order = sorted(range(1, count), key=lambda d: (d & 1, d))
    for d in order:
        low = d & -d
        pieces[d] = jump(pieces[d ^ low], low)
    return [pieces[d] for d in range(count)]


def send_pieces(pieces):
    far_first = sorted(range(1, len(pieces)), reverse=True)
    arrived = {d: jump(pieces[d], d) for d in far_first}
    return [pieces[0]] + [arrived[d] for d in range(1, len(pieces))]


def stages():
    row_bits = [("row", b) for b in bits_of(lax.axis_size("row"))]
    img_bits = [("img", b) for b in bits_of(lax.axis_size("img"))]
    return row_bits, img_bits


def tree(values):
    while len(values) > 1:
        values = [values[i] + values[i + 1] for i in range(0, len(values), 2)]
    return values[0]


def behind(value, after):
    return lax.optimization_barrier((value, tuple(after)))[0] if after else value


class Halving:
    def __init__(self, value, bits, img_count):
        mine = {"row": lax.axis_index("row"), "img": lax.axis_index("img")}

        def part(e):
            piece = value
            for j, (axis, bit) in enumerate(bits):
                want = (mine[axis] // bit) % 2 ^ (e >> j & 1)
                dim = value.ndim - 1 if axis == "row" else img_count - bit.bit_length()
                length = piece.shape[dim] // 2
                piece = lax.dynamic_slice_in_dim(piece, want * length, length, dim)
            return piece

        masks = masks_of(bits)
        self.kept = part(0)
        self.moved = [jump(part(e), *masks[e]) for e in range(1, len(masks))]

    def finish(self):
        values = [self.kept, *self.moved]
        return tree([v.astype(f32) for v in values]).astype(bf16)


class Exchange(Halving):
    def __init__(self, value, bits):
        self.kept = value
        self.moved = [jump(value, *mask) for mask in masks_of(bits)[1:]]


class Moved(Halving):
    def __init__(self, values, masks):
        self.moved = [jump(v, *mask) for v, mask in zip(values, masks)]

    def finish(self):
        return self.moved


def arrive(flights, after=()):
    return arrive_with(flights, tuple(after))[0]


def arrive_with(flights, beside):
    flat = [m for flight in flights for m in flight.moved]
    flat, beside = lax.optimization_barrier((flat, beside))
    for flight in flights:
        flight.moved, flat = flat[: len(flight.moved)], flat[len(flight.moved) :]
    return [flight.finish() for flight in flights], beside


def spread_img(grad):
    rows, columns = grad.shape
    images = lax.axis_size("img")
    return grad.reshape((2,) * len(bits_of(images)) + (rows // images, columns))


def gather_columns(value, order, bits, after=()):
    masks = [row_mask for row_mask, _ in masks_of(bits)]
    device = lax.axis_index("row") % len(masks)
    stack = jnp.stack([value if m == 0 else behind(jump(value, m), after) for m in masks])
    return [
        lax.dynamic_index_in_dim(stack, order(c) ^ device, 0, False) for c in range(len(masks))
    ]


def reversed_bits(index, size):
    width = size.bit_length() - 1
    return int(format(index, f"0{width}b")[::-1], 2) if width else 0


def finish_weight(value, bits, after=()):
    value = value.reshape(value.shape[-2:])
    count = 1 << len(bits)
    blocks = gather_columns(value, lambda c: reversed_bits(c, count), bits, after)
    return jnp.concatenate(blocks, axis=1).astype(f32)


def params(flags=("arbitrary",)):
    return pltpu.CompilerParams(dimension_semantics=flags, vmem_limit_bytes=VMEM)


ANYWHERE = pl.BlockSpec(memory_space=pl.ANY)


def own_columns(w_qkv, features, splits, chosen):
    width = w_qkv.shape[0]
    wide = features // splits

    def spec(s, part):
        def index(b, me):
            return 0, part * (width // wide) + me[0] * splits + s

        return pl.BlockSpec((width, wide), index, pipeline_mode=pl.Buffered(1))

    return [spec(s, part) for s in chosen for part in range(3)], [w_qkv] * (3 * len(chosen))


def valid_rows(block, piece_rows, local_rows):
    position = lax.broadcasted_iota(jnp.int32, (BLK, 1), 0) % piece_rows + block * piece_rows
    return position < local_rows


def load_block(refs, block, piece_rows, local_rows):
    value = jnp.concatenate([ref[...] for ref in refs], axis=0).astype(f32)
    return jnp.where(valid_rows(block, piece_rows, local_rows), value, 0.0)


def norm_parts(value):
    centre = value - jnp.mean(value, axis=-1, keepdims=True)
    rstd = lax.rsqrt(jnp.mean(centre * centre, axis=-1, keepdims=True) + epsilon)
    return centre * rstd, rstd


def qkv_kernel(count, splits, local_rows, features, held, me_ref, *refs):
    n_w = 3 * splits
    pieces, columns = refs[:count], refs[count : count + n_w]
    bias_ref, gain_ref, shift_ref = refs[count + n_w : count + n_w + 3]
    n_ref, q_ref, k_ref, v_ref, kt_ref, vt_ref, w_ref = refs[count + n_w + 3 + held :]
    step = pl.program_id(0)
    wide = features // splits
    half = BLK // 2
    rows = half // count

    @pl.when(step == 0)
    def _():
        for i, ref in enumerate(columns):
            w_ref[:, i * wide : (i + 1) * wide] = ref[...]

    places = [(b, d) for b in range(2) for d in range(count)]
    value = jnp.concatenate(
        [pieces[d][b * rows : (b + 1) * rows, :] for b, d in places], axis=0
    ).astype(f32)
    row = lax.broadcasted_iota(jnp.int32, (BLK, 1), 0)
    position = (2 * step + row // half) * rows + row % rows
    unit, _ = norm_parts(jnp.where(position < local_rows, value, 0.0))
    normed = (unit * gain_ref[...] + shift_ref[...]).astype(bf16)
    low = unit.astype(bf16)
    for i, (b, d) in enumerate(places):
        n_ref[d, b * rows : (b + 1) * rows, :] = low[i * rows : (i + 1) * rows]
    mixed = matmul(normed, w_ref[...])
    for s in range(splits):
        at = slice(s * wide, (s + 1) * wide)
        part = mixed[:, 3 * s * wide : 3 * (s + 1) * wide]
        queries = ((part[:, :wide] + bias_ref[0:1, at]) * 0.125).astype(bf16)
        keys = part[:, wide : 2 * wide]
        values = part[:, 2 * wide :] + bias_ref[1:2, at]
        keys_low, values_low = keys.astype(bf16), values.astype(bf16)
        keys_turned, values_turned = keys.T.astype(bf16), values.T.astype(bf16)
        for b in range(2):
            here = slice(b * half, (b + 1) * half)
            q_ref[b, 0, :, at] = queries[here]
            k_ref[b, 0, :, at] = keys_low[here]
            v_ref[b, 0, :, at] = values_low[here]
            kt_ref[b, at, :] = keys_turned[:, here]
            vt_ref[b, at, :] = values_turned[:, here]


def qkv_call(me, pieces, part, w_qkv, bias, gain, shift, splits, held=()):
    count, (local_rows, width) = len(pieces), pieces[0].shape
    features = width // (2 * count)
    rows = BLK // 2 // count
    blocks = pl.cdiv(local_rows, rows)
    whole = lambda a: pl.BlockSpec(a.shape, lambda b, m: (0,) * a.ndim)
    flat = pl.BlockSpec((2, 1, BLK // 2, features), lambda b, m: (b, part, 0, 0))
    turned = pl.BlockSpec((2, features, BLK // 2), lambda b, m: (b, 0, part))
    specs, operands = own_columns(w_qkv, features, splits, range(splits))
    at = 1 + count + 3 * splits + 3
    return pl.pallas_call(
        functools.partial(qkv_kernel, count, splits, local_rows, features, len(held)),
        grid_spec=pltpu.PrefetchScalarGridSpec(
            num_scalar_prefetch=1,
            grid=(blocks // 2,),
            in_specs=[pl.BlockSpec((2 * rows, width), lambda b, m: (b, 0))] * count
            + specs
            + [whole(bias), whole(gain), whole(shift)]
            + [ANYWHERE] * len(held),
            out_specs=[
                pl.BlockSpec((count, 2 * rows, width), lambda b, m: (part, b, 0)),
                flat,
                flat,
                flat,
                turned,
                turned,
            ],
            scratch_shapes=[pltpu.VMEM((width, 3 * features), bf16)],
        ),
        out_shape=[jax.ShapeDtypeStruct((2 * count, blocks * rows, width), bf16)]
        + [jax.ShapeDtypeStruct((blocks, 2, BLK // 2, features), bf16)] * 3
        + [jax.ShapeDtypeStruct((blocks, features, BLK), bf16)] * 2,
        input_output_aliases={at + i: i for i in range(len(held))},
        compiler_params=params(),
        cost_estimate=pl.CostEstimate(
            flops=6 * blocks * BLK * width * 3 * features,
            bytes_accessed=blocks * BLK * (2 * width + 5 * features),
            transcendentals=0,
        ),
    )(me, *pieces, *operands, bias, gain, shift, *held)


def per_head(stack_ref, value, heads):
    lane = lax.broadcasted_iota(jnp.int32, value.shape, 1) // HEAD
    for h in range(heads):
        stack_ref[h * BLK : (h + 1) * BLK] = jnp.where(lane == h, value, jnp.zeros_like(value))


def in_pairs(lo, hi, step, carry):
    pairs = (hi - lo) // 2
    carry = lax.fori_loop(0, pairs, lambda i, c: step(lo + 2 * i, 2, c), carry)
    return lax.fori_loop(lo + 2 * pairs, hi, lambda kb, c: step(kb, 1, c), carry)


def attend_kernel(count, heads, lo_ref, hi_ref, *refs):
    q_ref, k_ref, vt_ref, imgq_ref, imgk_ref = refs[:5]
    outs, (ot_ref, lse_ref) = refs[5 : 5 + count], refs[5 + count : 7 + count]
    s_ref, qs_ref, acc_ref = refs[7 + count :]
    block = pl.program_id(0)
    lo, hi = lo_ref[block], hi_ref[block]
    per_head(qs_ref, q_ref[...], heads)
    imgq = imgq_ref[...]

    def first(kb, width, tops):
        rows = pl.ds(pl.multiple_of(kb * BLK, BLK), width * BLK)
        allowed = imgk_ref[rows, :] == imgq
        s = nt(k_ref[rows, :], qs_ref[...])
        new = []
        for h in range(heads):
            cols = slice(h * BLK, (h + 1) * BLK)
            part = jnp.where(allowed, s[:, cols], NEG)
            for j in range(width):
                s_ref[kb - lo + j, :, cols] = part[j * BLK : (j + 1) * BLK]
            high = jnp.max(part.reshape(width * BLK // 8, 8, BLK), axis=0)
            new.append(jnp.maximum(tops[h], high))
        return tuple(new)

    tops = in_pairs(lo, hi, first, (jnp.full((8, BLK), NEG, f32),) * heads)
    tops = [jnp.max(t, axis=0, keepdims=True) for t in tops]
    acc_ref[...] = jnp.zeros_like(acc_ref)

    def second(kb, width, sums):
        new = []
        for h in range(heads):
            rows, cols = slice(h * HEAD, (h + 1) * HEAD), slice(h * BLK, (h + 1) * BLK)
            part, weights = 0.0, sums[h]
            for j in range(width):
                p = jnp.exp(s_ref[kb - lo + j, :, cols] - tops[h])
                weights = weights + jnp.sum(p.reshape(BLK // 8, 8, BLK), axis=0)
                part = part + matmul(vt_ref[kb + j, rows, :], p.astype(bf16))
            new.append(weights)
            acc_ref[rows, :] += part
        return tuple(new)

    sums = in_pairs(lo, hi, second, (jnp.zeros((8, BLK), f32),) * heads)
    sums = [jnp.sum(t, axis=0, keepdims=True) for t in sums]
    for h in range(heads):
        rows = slice(h * HEAD, (h + 1) * HEAD)
        acc_ref[rows, :] = acc_ref[rows, :] / sums[h]
    lse_ref[...] = jnp.concatenate(
        [t + jnp.log(s) for t, s in zip(tops, sums)] + [jnp.zeros((8 - heads, BLK), f32)], axis=0
    )
    ot_ref[0] = acc_ref[...]
    out = acc_ref[...].T.astype(bf16)
    for d in range(count):
        outs[d][...] = out[d * (BLK // count) : (d + 1) * (BLK // count)]


def attend_call(q, k, vt, imgq, imgk, lo, hi, count):
    blocks, features = vt.shape[0], q.shape[1]
    heads = features // HEAD
    piece_rows = BLK // count
    whole = lambda a: pl.BlockSpec(
        a.shape, lambda b, *_: (0,) * a.ndim, pipeline_mode=pl.Buffered(1)
    )
    return pl.pallas_call(
        functools.partial(attend_kernel, count, heads),
        grid_spec=pltpu.PrefetchScalarGridSpec(
            num_scalar_prefetch=2,
            grid=(blocks,),
            in_specs=[
                pl.BlockSpec((BLK, features), lambda b, *_: (b, 0)),
                whole(k),
                whole(vt),
                pl.BlockSpec((1, BLK), lambda b, *_: (0, b)),
                whole(imgk),
            ],
            out_specs=[pl.BlockSpec((piece_rows, features), lambda b, *_: (b, 0))] * count
            + [
                pl.BlockSpec((1, features, BLK), lambda b, *_: (b, 0, 0)),
                pl.BlockSpec((8, BLK), lambda b, *_: (0, b)),
            ],
            scratch_shapes=[
                pltpu.VMEM((blocks, BLK, heads * BLK), f32),
                pltpu.VMEM((heads * BLK, features), bf16),
                pltpu.VMEM((features, BLK), f32),
            ],
        ),
        out_shape=[jax.ShapeDtypeStruct((blocks * piece_rows, features), bf16)] * count
        + [
            jax.ShapeDtypeStruct((blocks, features, BLK), f32),
            jax.ShapeDtypeStruct((8, blocks * BLK), f32),
        ],
        compiler_params=params(),
        cost_estimate=pl.CostEstimate(
            flops=10 * (blocks * BLK) ** 2 * features,
            bytes_accessed=2 * blocks * BLK * features * 8,
            transcendentals=0,
        ),
    )(lo, hi, q, k, vt, imgq, imgk)


def attend_back_kernel(count, heads, first, waits, lo_ref, hi_ref, *refs):
    pieces, refs = refs[:count], refs[:count] + refs[count + waits :]
    q_ref, k_ref, v_ref, kt_ref, ot_ref, lse_ref, imgq_ref, imgk_ref = refs[count : count + 8]
    groups = count // 2
    outs, sums_ref = refs[count + 8 : count + groups + 8], refs[count + groups + 8]
    qs_ref, dos_ref, p_ref, ds_ref, dqt_ref, dk_ref, dv_ref = refs[count + groups + 9 :]
    block = pl.program_id(0)
    lo, hi = lo_ref[block], hi_ref[block]
    piece_rows = BLK // count
    wide = heads * HEAD

    @pl.when(block == 0)
    def _():
        dk_ref[...] = jnp.zeros_like(dk_ref)
        dv_ref[...] = jnp.zeros_like(dv_ref)
        sums_ref[...] = jnp.zeros_like(sums_ref)

    grad = jnp.concatenate([ref[...] for ref in pieces], axis=0)
    query = q_ref[...]
    lane = lax.broadcasted_iota(jnp.int32, grad.shape, 1) // HEAD
    for h in range(heads):
        dos_ref[h * BLK : (h + 1) * BLK] = jnp.where(lane == h, grad, jnp.zeros_like(grad))
        qs_ref[h * BLK : (h + 1) * BLK] = jnp.where(lane == h, query, jnp.zeros_like(query))
    both = grad.astype(f32).T * ot_ref[0]
    delta = [
        jnp.sum(both[h * HEAD : (h + 1) * HEAD], axis=0, keepdims=True) for h in range(heads)
    ]
    logsum = [lse_ref[first + h : first + h + 1, :] for h in range(heads)]
    imgq = imgq_ref[...]
    dqt_ref[...] = jnp.zeros_like(dqt_ref)

    def step(kb, width):
        length = width * BLK
        rows = pl.ds(pl.multiple_of(kb * BLK, BLK), length)
        keys, values = k_ref[rows, :], v_ref[rows, :]
        allowed = imgk_ref[rows, :] == imgq
        s = nt(keys, qs_ref[...])
        dp = nt(values, dos_ref[...])
        for h in range(heads):
            cols = slice(h * BLK, (h + 1) * BLK)
            p = jnp.exp(jnp.where(allowed, s[:, cols] - logsum[h], NEG))
            p_ref[:length, cols] = p.astype(bf16)
            ds_ref[:length, cols] = (p * (dp[:, cols] - delta[h])).astype(bf16)
        dv_ref[rows, :] += matmul(p_ref[:length], dos_ref[...])
        dk_ref[rows, :] += matmul(ds_ref[:length], qs_ref[...])
        for h in range(heads):
            cols, feats = slice(h * BLK, (h + 1) * BLK), slice(h * HEAD, (h + 1) * HEAD)
            total = 0.0
            for j in range(width):
                ds = ds_ref[j * BLK : (j + 1) * BLK, cols]
                total = total + matmul(kt_ref[kb + j, feats, :], ds)
            dqt_ref[feats, :] += total

    def pair(i, _):
        step(lo + 2 * i, 2)
        return 0

    lax.fori_loop(0, (hi - lo) // 2, pair, 0)

    @pl.when((hi - lo) % 2 == 1)
    def _():
        step(hi - 1, 1)

    dq = dqt_ref[...].T * 0.125
    sums_ref[0:1, :] += jnp.sum(dq, axis=0, keepdims=True)
    here = pl.ds(pl.multiple_of(block * piece_rows, piece_rows), piece_rows)
    for d in range(count):
        outs[d // 2][d % 2, here, :wide] = dq[d * piece_rows : (d + 1) * piece_rows].astype(bf16)

    @pl.when(block == pl.num_programs(0) - 1)
    def _():
        sums_ref[1:2, :] = jnp.sum(dv_ref[...], axis=0, keepdims=True)

        def move(b, _):
            to = pl.ds(pl.multiple_of(b * piece_rows, piece_rows), piece_rows)
            for d in range(count):
                at = pl.ds(pl.multiple_of(b * BLK + d * piece_rows, piece_rows), piece_rows)
                outs[d // 2][d % 2, to, wide : 2 * wide] = dk_ref[at, :].astype(bf16)
                outs[d // 2][d % 2, to, 2 * wide :] = dv_ref[at, :].astype(bf16)
            return 0

        lax.fori_loop(0, pl.num_programs(0), move, 0)


def attend_back_call(pieces, q, k, v, kt, ot, lse, imgq, imgk, lo, hi, split, after):
    count, (rows, wide) = len(pieces), pieces[0].shape
    blocks = kt.shape[0]
    heads = wide // HEAD
    once = pl.Buffered(1)
    half = pl.BlockSpec((blocks * BLK, wide), lambda b, *_: (0, split), pipeline_mode=once)
    out = jax.ShapeDtypeStruct((2, rows, 3 * wide), bf16)
    return pl.pallas_call(
        functools.partial(attend_back_kernel, count, heads, split * heads, len(after)),
        grid_spec=pltpu.PrefetchScalarGridSpec(
            num_scalar_prefetch=2,
            grid=(blocks,),
            in_specs=[pl.BlockSpec((BLK // count, wide), lambda b, *_: (b, 0))] * count
            + [ANYWHERE] * len(after)
            + [
                pl.BlockSpec((BLK, wide), lambda b, *_: (b, split)),
                half,
                half,
                pl.BlockSpec((blocks, wide, BLK), lambda b, *_: (0, split, 0), pipeline_mode=once),
                pl.BlockSpec((1, wide, BLK), lambda b, *_: (b, split, 0)),
                pl.BlockSpec((8, BLK), lambda b, *_: (0, b)),
                pl.BlockSpec((1, BLK), lambda b, *_: (0, b)),
                pl.BlockSpec(imgk.shape, lambda b, *_: (0, 0), pipeline_mode=once),
            ],
            out_specs=[pl.BlockSpec(out.shape, lambda b, *_: (0, 0, 0), pipeline_mode=once)] * (count // 2)
            + [pl.BlockSpec((8, wide), lambda b, *_: (0, 0))],
            scratch_shapes=[
                pltpu.VMEM((heads * BLK, wide), bf16),
                pltpu.VMEM((heads * BLK, wide), bf16),
                pltpu.VMEM((2 * BLK, heads * BLK), bf16),
                pltpu.VMEM((2 * BLK, heads * BLK), bf16),
                pltpu.VMEM((wide, BLK), f32),
                pltpu.VMEM((blocks * BLK, wide), f32),
                pltpu.VMEM((blocks * BLK, wide), f32),
            ],
        ),
        out_shape=[out] * (count // 2) + [jax.ShapeDtypeStruct((8, wide), f32)],
        compiler_params=params(),
        cost_estimate=pl.CostEstimate(
            flops=16 * (blocks * BLK) ** 2 * wide,
            bytes_accessed=2 * blocks * BLK * wide * 12,
            transcendentals=0,
        ),
    )(lo, hi, *pieces, *after, q, k, v, kt, ot, lse, imgq, imgk)


def norm_back(grad, unit, rstd, gain):
    e = grad * gain
    mean = jnp.mean(e, axis=-1, keepdims=True)
    return (e - mean - unit * jnp.mean(e * unit, axis=-1, keepdims=True)) * rstd


def total(value):
    return jnp.sum(value, axis=0, keepdims=True)


def rows_kernel(count, splits, local_rows, *refs):
    (
        tok_ref,
        img_ref,
        w_out_ref,
        w_up_ref,
        w_down_ref,
        learn_in_ref,
        learn_out_ref,
        vec_ref,
        up_bias_ref,
        out_bias_ref,
        pooled_grad_ref,
    ) = refs[:11]
    attended = refs[11 : 11 + count]
    at = 11 + count
    (
        n2_ref,
        gated_ref,
        gup_ref,
        gres_ref,
        n3_ref,
        glearn_ref,
        inner_ref,
        glogit_ref,
        ghid_ref,
        ghid_f32_ref,
    ) = refs[at : at + 10]
    gatt = refs[at + 10 : at + 10 + count * splits]
    at += 10 + count * splits
    pooled_ref, vsum_ref, usum_ref, lsum_ref = refs[at : at + 4]
    hid_ref, res_ref, dgate_ref, up0_ref, up1_ref = refs[at + 4 :]
    step = pl.program_id(0)
    rows, width = tok_ref.shape
    hidden_units = w_up_ref.shape[1]
    chunk = up0_ref.shape[1]
    chunks = hidden_units // chunk

    @pl.when(step == 0)
    def _():
        for ref in (pooled_ref, vsum_ref, usum_ref, lsum_ref):
            ref[...] = jnp.zeros_like(ref)

    def vec(i):
        return vec_ref[i : i + 1, :]

    position = lax.broadcasted_iota(jnp.int32, (rows, 1), 0) + step * rows
    tok = jnp.where(position < local_rows, tok_ref[...].astype(f32), 0.0)
    low = jnp.concatenate([ref[...] for ref in attended], axis=1)
    hidden = tok + matmul(low, w_out_ref[...]) + vec(0)
    hid_ref[...] = hidden
    unit, _ = norm_parts(hidden)
    n2_ref[...] = (unit * vec(2) + vec(3)).astype(bf16)

    def columns(j):
        return pl.ds(pl.multiple_of(j * chunk, chunk), chunk)

    def up(ref, j):
        ref[...] = matmul(n2_ref[...], w_up_ref[:, columns(j)])

    def gate(ref, j):
        value, slope = smooth_both(ref[...] + up_bias_ref[:, columns(j)])
        gated_ref[:, columns(j)] = value.astype(bf16)
        dgate_ref[:, columns(j)] = slope

    up(up0_ref, 0)

    def pair(i, _):
        up(up1_ref, 2 * i + 1)
        gate(up0_ref, 2 * i)
        up(up0_ref, jnp.minimum(2 * i + 2, chunks - 1))
        gate(up1_ref, 2 * i + 1)
        return 0

    lax.fori_loop(0, chunks // 2, pair, 0)
    result = hid_ref[...] + matmul(gated_ref[...], w_down_ref[...]) + vec(1)
    res_ref[...] = result
    unit, rstd = norm_parts(result)
    n3_ref[...] = (unit * vec(4) + vec(5)).astype(bf16)
    inner, slope = smooth_both(matmul(n3_ref[...], learn_in_ref[...]) + vec(6))
    inner_ref[...] = inner.astype(bf16)
    maps = jax.nn.sigmoid(matmul(inner_ref[...], learn_out_ref[...]) + out_bias_ref[...])
    member = lax.broadcasted_iota(jnp.int32, maps.shape, 1) // LT == img_ref[...]
    spread = jnp.where(member, maps, 0.0).astype(bf16)
    result_low = res_ref[...].astype(bf16)
    pooled_ref[...] += tn(spread, result_low)
    grad_spread = nt(result_low, pooled_grad_ref[...])
    grad_logit = jnp.where(member, grad_spread * maps * (1.0 - maps), 0.0)
    lsum_ref[...] += total(grad_logit)
    glogit_ref[...] = grad_logit.astype(bf16)
    grad_pre = nt(glogit_ref[...], learn_out_ref[...]) * slope
    vsum_ref[6:7, :] += total(grad_pre)
    glearn_ref[...] = grad_pre.astype(bf16)
    back = nt(glearn_ref[...], learn_in_ref[...])
    unit, rstd = norm_parts(res_ref[...])
    vsum_ref[4:5, :] += total(back * unit)
    vsum_ref[5:6, :] += total(back)
    grad_result = matmul(spread, pooled_grad_ref[...]) + norm_back(back, unit, rstd, vec(4))
    vsum_ref[1:2, :] += total(grad_result)
    res_ref[...] = grad_result
    gres_ref[...] = grad_result.astype(bf16)

    def down_back(j, _):
        grad = nt(gres_ref[...], w_down_ref[columns(j), :]) * dgate_ref[:, columns(j)]
        usum_ref[:, columns(j)] += total(grad)
        gup_ref[:, columns(j)] = grad.astype(bf16)
        return 0

    lax.fori_loop(0, chunks, down_back, 0)
    back = nt(gup_ref[...], w_up_ref[...])
    unit, rstd = norm_parts(hid_ref[...])
    vsum_ref[2:3, :] += total(back * unit)
    vsum_ref[3:4, :] += total(back)
    grad_hidden = res_ref[...] + norm_back(back, unit, rstd, vec(2))
    vsum_ref[0:1, :] += total(grad_hidden)
    ghid_f32_ref[...] = grad_hidden
    ghid_ref[...] = grad_hidden.astype(bf16)
    grad = nt(ghid_ref[...], w_out_ref[...]).astype(bf16)
    wide = width // (count * splits)
    for i in range(count * splits):
        gatt[i][...] = grad[:, i * wide : (i + 1) * wide]


def rows_call(tok, img, attended, w_out, w_up, w_down, learn_in, learn_out, vecs, up_bias, out_bias, pooled_grad, splits):
    count, (rows, features) = len(attended), attended[0].shape
    local_rows, width = tok.shape
    hidden_units = w_up.shape[1]
    inner = learn_in.shape[1]
    spread = learn_out.shape[1]
    block = min(ROW_BLOCK, rows)
    chunk = UP_BLOCK
    wide = features // splits
    once = lambda a: pl.BlockSpec(a.shape, lambda i: (0,) * a.ndim, pipeline_mode=pl.Buffered(1))
    by_rows = lambda n: pl.BlockSpec((block, n), lambda i: (i, 0))
    kept = lambda a: pl.BlockSpec(a.shape, lambda i: (0, 0))
    low = lambda n: jax.ShapeDtypeStruct((rows, n), bf16)
    lows = [width, hidden_units, hidden_units, width, width, inner, inner, spread, width]
    sums = [
        jax.ShapeDtypeStruct((spread, width), f32),
        jax.ShapeDtypeStruct((8, width), f32),
        jax.ShapeDtypeStruct((1, hidden_units), f32),
        jax.ShapeDtypeStruct((1, spread), f32),
    ]
    resident = [w_out, w_up, w_down, learn_in, learn_out, vecs, up_bias, out_bias, pooled_grad]
    return pl.pallas_call(
        functools.partial(rows_kernel, count, splits, local_rows),
        grid=(rows // block,),
        in_specs=[by_rows(width), by_rows(1)]
        + [once(a) for a in resident]
        + [by_rows(features)] * count,
        out_specs=[by_rows(n) for n in lows]
        + [by_rows(width)]
        + [by_rows(wide)] * (count * splits)
        + [kept(a) for a in sums],
        out_shape=[low(n) for n in lows]
        + [jax.ShapeDtypeStruct((rows, width), f32)]
        + [low(wide)] * (count * splits)
        + sums,
        scratch_shapes=[
            pltpu.VMEM((block, width), f32),
            pltpu.VMEM((block, width), f32),
            pltpu.VMEM((block, hidden_units), f32),
            pltpu.VMEM((block, chunk), f32),
            pltpu.VMEM((block, chunk), f32),
        ],
        compiler_params=params(),
        cost_estimate=pl.CostEstimate(
            flops=4 * rows * width * (width + 2 * hidden_units + inner),
            bytes_accessed=2 * (rows * 20 * width + 2 * width * hidden_units),
            transcendentals=0,
        ),
    )(tok, img, *resident, *attended)


def part_halves(me_ref, value, keep_ref, send_ref, whole_ref):
    half = value.shape[1] // 2
    core = me_ref[0] % 2
    whole_ref[...] = value
    keep_ref[...] = whole_ref[:, pl.ds(pl.multiple_of(core * half, half), half)]
    send_ref[...] = whole_ref[:, pl.ds(pl.multiple_of((1 - core) * half, half), half)]


def down_grad_kernel(waits, me_ref, left_ref, right_ref, *refs):
    part_halves(me_ref, tn(left_ref[...], right_ref[...]).astype(bf16), *refs[waits:])


def down_grad_call(me, left, right, after=()):
    rows, m = left.shape
    n = right.shape[1]
    out = pl.BlockSpec((GRAD_BLOCK, n // 2), lambda j, m: (j, 0))
    return pl.pallas_call(
        functools.partial(down_grad_kernel, len(after)),
        grid_spec=pltpu.PrefetchScalarGridSpec(
            num_scalar_prefetch=1,
            grid=(m // GRAD_BLOCK,),
            in_specs=[
                pl.BlockSpec((rows, GRAD_BLOCK), lambda j, m: (0, j)),
                pl.BlockSpec((rows, n), lambda j, m: (0, 0), pipeline_mode=pl.Buffered(1)),
            ]
            + [ANYWHERE] * len(after),
            out_specs=[out, out],
            scratch_shapes=[pltpu.VMEM((GRAD_BLOCK, n), bf16)],
        ),
        out_shape=[jax.ShapeDtypeStruct((m, n // 2), bf16)] * 2,
        compiler_params=params(),
        cost_estimate=pl.CostEstimate(
            flops=3 * rows * m * n, bytes_accessed=4 * m * n, transcendentals=0
        ),
    )(me, left, right, *after)


def up_grad_kernel(half, waits, me_ref, left_ref, right_ref, *refs):
    keep_ref, send_ref = refs[waits:]
    value = tn(left_ref[...], right_ref[...]).astype(bf16)

    @pl.when(pl.program_id(0) < half)
    def _():
        send_ref[...] = value

    @pl.when(pl.program_id(0) >= half)
    def _():
        keep_ref[...] = value


def up_grad_call(me, left, right, after=()):
    rows, m = left.shape
    n = right.shape[1]
    half = n // GRAD_BLOCK // 2

    def column(j, core):
        return jnp.where(j < half, (1 - core) * half + j, core * half + j - half)

    return pl.pallas_call(
        functools.partial(up_grad_kernel, half, len(after)),
        grid_spec=pltpu.PrefetchScalarGridSpec(
            num_scalar_prefetch=1,
            grid=(2 * half,),
            in_specs=[
                pl.BlockSpec((rows, m), lambda j, me: (0, 0), pipeline_mode=pl.Buffered(1)),
                pl.BlockSpec((rows, GRAD_BLOCK), lambda j, me: (0, column(j, me[0] % 2))),
            ]
            + [ANYWHERE] * len(after),
            out_specs=[
                pl.BlockSpec((m, GRAD_BLOCK), lambda j, me: (0, jnp.maximum(j - half, 0))),
                pl.BlockSpec((m, GRAD_BLOCK), lambda j, me: (0, jnp.minimum(j, half - 1))),
            ],
        ),
        out_shape=[jax.ShapeDtypeStruct((m, n // 2), bf16)] * 2,
        compiler_params=params(),
        cost_estimate=pl.CostEstimate(
            flops=3 * rows * m * n, bytes_accessed=4 * m * n, transcendentals=0
        ),
    )(me, left, right, *after)


def small_grad_kernel(count, me_ref, *refs):
    n3_ref, glearn_ref, ghid_ref, inner_ref, glogit_ref = refs[:5]
    attended = refs[5 : 5 + count]
    keep_ref, send_ref, lout_ref, learn_ref, wout_ref = refs[5 + count :]
    learn_ref[...] = tn(n3_ref[...], glearn_ref[...]).astype(bf16)
    lout_ref[...] = tn(inner_ref[...], glogit_ref[...])
    features = attended[0].shape[1]
    for d in range(count):
        owner = jnp.bitwise_xor(me_ref[0], d)
        to = pl.ds(pl.multiple_of(owner * features, features), features)
        wout_ref[to, :] = tn(attended[d][...], ghid_ref[...]).astype(bf16)
    first = me_ref[0] % 2 == 0

    @pl.when(first)
    def _():
        keep_ref[...] = learn_ref[...]
        send_ref[...] = wout_ref[...]

    @pl.when(jnp.logical_not(first))
    def _():
        keep_ref[...] = wout_ref[...]
        send_ref[...] = learn_ref[...]


def small_grad_call(me, n3, glearn, ghid, inner, glogit, attended):
    rows, width = n3.shape
    operands = [n3, glearn, ghid, inner, glogit, *attended]
    out = jax.ShapeDtypeStruct((width, ghid.shape[1]), bf16)
    lout = jax.ShapeDtypeStruct((inner.shape[1], glogit.shape[1]), f32)
    once = lambda a: pl.BlockSpec(a.shape, lambda j, m: (0, 0), pipeline_mode=pl.Buffered(1))
    return pl.pallas_call(
        functools.partial(small_grad_kernel, len(attended)),
        grid_spec=pltpu.PrefetchScalarGridSpec(
            num_scalar_prefetch=1,
            grid=(1,),
            in_specs=[once(a) for a in operands],
            out_specs=[once(out), once(out), once(lout)],
            scratch_shapes=[pltpu.VMEM(out.shape, bf16), pltpu.VMEM(out.shape, bf16)],
        ),
        out_shape=[out, out, lout],
        compiler_params=params(),
        cost_estimate=pl.CostEstimate(
            flops=6 * rows * width * width, bytes_accessed=20 * width * width, transcendentals=0
        ),
    )(me, *operands)


def qkv_grad_kernel(groups, waits, me_ref, n_ref, gain_ref, shift_ref, *refs):
    parts, weights = refs[:groups], refs[groups : groups + 3]
    out_ref, sums_ref, acc_ref, sum_ref = refs[groups + 3 + waits :]
    step = pl.program_id(0)
    wide = weights[0].shape[1]
    for d in range(2 * groups):

        @pl.when(step == d)
        def _():
            mixed = parts[d // 2][d % 2]
            part = tn(n_ref[0], mixed)
            column = total(mixed.astype(f32))
            acc_ref[...] = part if d == 0 else acc_ref[...] + part
            sum_ref[...] = column if d == 0 else sum_ref[...] + column

    @pl.when(step == 2 * groups - 1)
    def _():
        by_unit, column = acc_ref[...], sum_ref[...]
        out_ref[...] = (by_unit * gain_ref[...] + shift_ref[...] * column).astype(bf16)
        weight = jnp.concatenate([ref[...].astype(f32) for ref in weights], axis=1)
        sums_ref[:, 0:1] = jnp.sum(by_unit * weight, axis=1, keepdims=True)
        sums_ref[:, 1:2] = jnp.sum(weight * column, axis=1, keepdims=True)


def qkv_grad_call(me, unit, parts, w_qkv, gain, shift, split, splits, after=()):
    count, rows, width = unit.shape
    columns = parts[0].shape[2]
    once = lambda a: pl.BlockSpec(
        a.shape, lambda d, m: (0,) * len(a.shape), pipeline_mode=pl.Buffered(1)
    )
    specs, operands = own_columns(w_qkv, width // count, splits, [split])
    return pl.pallas_call(
        functools.partial(qkv_grad_kernel, count // 2, len(after)),
        grid_spec=pltpu.PrefetchScalarGridSpec(
            num_scalar_prefetch=1,
            grid=(count,),
            in_specs=[pl.BlockSpec((1, rows, width), lambda d, m: (d, 0, 0)), once(gain), once(shift)]
            + [once(a) for a in parts]
            + specs
            + [ANYWHERE] * len(after),
            out_specs=[
                pl.BlockSpec((width, columns), lambda d, m: (0, 0)),
                pl.BlockSpec((width, 2), lambda d, m: (0, 0)),
            ],
            scratch_shapes=[pltpu.VMEM((width, columns), f32), pltpu.VMEM((1, columns), f32)],
        ),
        out_shape=[
            jax.ShapeDtypeStruct((width, columns), bf16),
            jax.ShapeDtypeStruct((width, 2), f32),
        ],
        compiler_params=params(),
        cost_estimate=pl.CostEstimate(flops=1 << 34, bytes_accessed=1 << 10, transcendentals=0),
    )(me, unit, gain, shift, *parts, *operands, *after)


def tokens_kernel(groups, splits, me_ref, tok_ref, ghid_ref, w_ref, gain_ref, *refs):
    same, other = refs[: groups * splits], refs[groups * splits : groups * splits + splits]
    out_ref, mixed_ref = refs[groups * splits + splits :]
    width = tok_ref.shape[1]
    features = width // (2 * groups)
    wide = features // splits
    for d in range(2 * groups):
        owner = jnp.bitwise_xor(me_ref[0], d) * features
        for s in range(splits):
            for part in range(3):
                to = pl.ds(pl.multiple_of(part * width + owner + s * wide, wide), wide)
                at = slice(part * wide, (part + 1) * wide)
                if d % 2 == 0:
                    mixed_ref[:, to] = same[s * groups + d // 2][0, :, at]
                else:
                    mixed_ref[:, to] = other[s][d // 2, :, at]
    back = nt(mixed_ref[...], w_ref[...])
    unit, rstd = norm_parts(tok_ref[...].astype(f32))
    out_ref[0] = ghid_ref[...] + norm_back(back, unit, rstd, gain_ref[...])


def tokens_call(me, tok, ghid, w_qkv, gain, same, other, count):
    local_rows, width = tok.shape
    columns = same[0].shape[2]
    groups, splits = count // 2, len(other)
    block = 256
    by_rows = lambda n: pl.BlockSpec((block, n), lambda i, m: (i, 0))
    return pl.pallas_call(
        functools.partial(tokens_kernel, groups, splits),
        grid_spec=pltpu.PrefetchScalarGridSpec(
            num_scalar_prefetch=1,
            grid=(pl.cdiv(local_rows, block),),
            in_specs=[
                by_rows(width),
                by_rows(width),
                pl.BlockSpec(w_qkv.shape, lambda i, m: (0, 0), pipeline_mode=pl.Buffered(1)),
                pl.BlockSpec(gain.shape, lambda i, m: (0, 0)),
            ]
            + [pl.BlockSpec((1, block, columns), lambda i, m: (0, i, 0))] * len(same)
            + [pl.BlockSpec((groups, block, columns), lambda i, m: (0, i, 0))] * splits,
            out_specs=pl.BlockSpec((1, block, width), lambda i, m: (0, i, 0)),
            scratch_shapes=[pltpu.VMEM((block, 3 * width), bf16)],
        ),
        out_shape=jax.ShapeDtypeStruct((1, local_rows, width), f32),
        compiler_params=params(),
        cost_estimate=pl.CostEstimate(flops=1 << 34, bytes_accessed=1 << 10, transcendentals=0),
    )(me, tok, ghid, w_qkv, gain, *same, *other)


def flip(index, bit):
    return index + bit - 2 * bit * ((index // bit) % 2)


def vectors_kernel(count, row_bits, img_bits, vec_ref, slot_ref, out_ref, sum_ref, *scratch):
    recv, slot_recv, send_sem, recv_sem, slot_send, slot_got = scratch
    row, img = lax.axis_index("row"), lax.axis_index("img")

    def partner(row_mask, img_mask=0):
        r, g = row, img
        for bit in row_bits:
            r = flip(r, bit) if row_mask & bit else r
        for bit in img_bits:
            g = flip(g, bit) if img_mask & bit else g
        return (g, r)

    steps = [(bit, 0) for bit in row_bits] + [(0, bit) for bit in img_bits]
    everyone = sorted(set(steps) | {(d, 0) for d in range(1, count)})
    barrier = pltpu.get_barrier_semaphore()
    for masks in everyone:
        pl.semaphore_signal(
            barrier, inc=1, device_id=partner(*masks), device_id_type=pl.DeviceIdType.MESH
        )
    pl.semaphore_wait(barrier, len(everyone))
    slots = []
    for d in range(1, count):
        copy = pltpu.make_async_remote_copy(
            src_ref=slot_ref.at[d],
            dst_ref=slot_recv.at[d - 1],
            send_sem=slot_send.at[d - 1],
            recv_sem=slot_got.at[d - 1],
            device_id=partner(d),
            device_id_type=pl.DeviceIdType.MESH,
        )
        copy.start()
        slots.append(copy)
    out_ref[...] = vec_ref[...]
    for i, masks in enumerate(steps):
        copy = pltpu.make_async_remote_copy(
            src_ref=out_ref,
            dst_ref=recv.at[i],
            send_sem=send_sem.at[i],
            recv_sem=recv_sem.at[i],
            device_id=partner(*masks),
            device_id_type=pl.DeviceIdType.MESH,
        )
        copy.start()
        copy.wait()
        out_ref[...] = out_ref[...] + recv[i]
    for copy in slots:
        copy.wait()
    sum_ref[...] = tree(
        [slot_ref[0].astype(f32)] + [slot_recv[d - 1].astype(f32) for d in range(1, count)]
    )


def vectors_call(vec, slots):
    count = lax.axis_size("row")
    row_bits, img_bits = bits_of(count), bits_of(lax.axis_size("img"))
    steps = len(row_bits) + len(img_bits)
    whole = pl.BlockSpec(memory_space=pltpu.VMEM)
    return pl.pallas_call(
        functools.partial(vectors_kernel, count, row_bits, img_bits),
        in_specs=[whole, whole],
        out_specs=[whole, whole],
        out_shape=[
            jax.ShapeDtypeStruct(vec.shape, f32),
            jax.ShapeDtypeStruct(slots.shape[1:], f32),
        ],
        scratch_shapes=[
            pltpu.VMEM((steps,) + vec.shape, f32),
            pltpu.VMEM((count - 1,) + slots.shape[1:], bf16),
            pltpu.SemaphoreType.DMA((steps,)),
            pltpu.SemaphoreType.DMA((steps,)),
            pltpu.SemaphoreType.DMA((count - 1,)),
            pltpu.SemaphoreType.DMA((count - 1,)),
        ],
        compiler_params=pltpu.CompilerParams(
            collective_id=0, has_side_effects=True, vmem_limit_bytes=32 << 20
        ),
        cost_estimate=pl.CostEstimate(flops=1 << 34, bytes_accessed=1 << 10, transcendentals=0),
    )(vec, slots)


def rows_of(array, index, length):
    return lax.dynamic_slice_in_dim(array, index * length, length, 0)


def on_device(
    tokens,
    counts,
    owner,
    w_qkv,
    qv_bias,
    w_out,
    out_bias,
    w_up,
    up_bias,
    w_down,
    down_bias,
    norm_gain,
    norm_bias,
    learn_in,
    learn_in_bias,
    learn_out,
    learn_out_bias,
    cotangent,
):
    width = tokens.shape[2]
    local_rows = tokens.shape[1]
    row_count = lax.axis_size("row")
    images_count = lax.axis_size("img")
    device = lax.axis_index("row")
    image_device = lax.axis_index("img")
    features = width // row_count
    wide = min(features, 128)
    splits = features // wide
    slots_here = IMGS // row_count
    group_counts = counts[0]
    partners = [device ^ d for d in range(row_count)]
    row_bits, img_bits = stages()
    n_img = len(img_bits)

    piece_rows = BLK // row_count
    blocks = pl.cdiv(local_rows, piece_rows)
    images = jnp.stack([row_images(group_counts, p, local_rows, row_count) for p in partners])
    extra = blocks * piece_rows - local_rows
    images = jnp.pad(images, ((0, 0), (0, extra)), constant_values=IMGS + 1)
    image_here = images[0].reshape(-1, 1)
    images = images.reshape(row_count, blocks, piece_rows).transpose(1, 0, 2).reshape(blocks, BLK)
    least, most = jnp.min(images, axis=1), jnp.max(images, axis=1)
    lo = jnp.sum((most[None, :] < least[:, None]).astype(jnp.int32), axis=1)
    hi = jnp.sum((least[None, :] <= most[:, None]).astype(jnp.int32), axis=1)
    imgq, imgk = images.reshape(1, -1), images.reshape(-1, 1)

    me = device.reshape(1)
    w_out_here = jnp.concatenate([rows_of(w_out, p, features) for p in partners], axis=0)
    bias_here = lax.dynamic_slice_in_dim(qv_bias, device * features, features, 1)
    half_count = row_count // 2
    first_norm = (w_qkv, bias_here, norm_gain[0:1], norm_bias[0:1], splits)
    far_tokens = jump(tokens[0], half_count)
    pieces = gather_pieces(tokens[0], half_count)
    filled = qkv_call(me, pieces, 0, *first_norm)
    tables = (imgq, imgk, lo, hi, image_here, w_out_here)
    far_tokens, filled, tables = lax.optimization_barrier((far_tokens, filled, tables))
    imgq, imgk, lo, hi, image_here, w_out_here = tables
    pieces = gather_pieces(far_tokens, half_count)
    unit, q, k, v, kt, vt = qkv_call(me, pieces, 1, *first_norm, filled)
    q, k, v = (a.reshape(-1, features) for a in (q, k, v))
    slot_grads = behind(cotangent[0].reshape(slots_here, LT * width).astype(bf16), [lo, unit])
    grads_in = gather_pieces(slot_grads, row_count)
    *attended, ot, lse = attend_call(q, k, vt, imgq, imgk, lo, hi, row_count)
    attended = send_pieces(attended)

    slot_rel = ((owner[0] // slots_here) ^ device) * slots_here + owner[0] % slots_here
    select = (slot_rel[:, None] == jnp.arange(IMGS, dtype=jnp.int32)[None, :]).astype(f32)
    scale = lax.rsqrt(group_counts.astype(f32))
    incoming = jnp.concatenate(grads_in, axis=0).astype(f32)
    grad_pooled = jnp.dot(select, incoming, precision=highest) * scale[:, None]
    grad_pooled_low = grad_pooled.reshape(IMGS * LT, width).astype(bf16)

    vecs = jnp.concatenate(
        [
            out_bias[None],
            down_bias[None],
            norm_gain[1:2],
            norm_bias[1:2],
            norm_gain[2:3],
            norm_bias[2:3],
            learn_in_bias[None],
            jnp.zeros((1, width), f32),
        ],
        axis=0,
    )
    out = rows_call(
        tokens[0],
        image_here,
        attended,
        w_out_here,
        w_up,
        w_down,
        learn_in,
        jnp.tile(learn_out, (1, IMGS)),
        vecs,
        up_bias[None],
        jnp.tile(learn_out_bias, IMGS)[None],
        grad_pooled_low,
        splits,
    )
    n2, gated, gup, gres, n3, glearn, inner, glogit, ghid, grad_hidden = out[:10]
    grad_attended = out[10 : 10 + row_count * splits]
    pooled, vec_sums, up_sums, logit_sums = out[10 + row_count * splits :]
    grad_attended = [send_pieces(grad_attended[s::splits]) for s in range(splits)]

    core, far_row = row_bits[:1], row_bits[1:]
    y_bits, z_bits = img_bits[:1], [[bit] for bit in img_bits[1:]]
    half = lambda value, bits: Halving(value, bits, n_img)

    def core_flight(keep, send):
        flight = Exchange(keep, [])
        flight.moved = [jump(send, 1)]
        return flight

    keep_small, send_small, grad_learn_out = small_grad_call(
        me, n3, glearn, ghid, inner, glogit, attended
    )
    keep_down, send_down = down_grad_call(me, gated, gres, [send_small])
    keep_up, send_up = up_grad_call(me, n2, gup, [send_down])
    small, down = arrive(
        [core_flight(keep_small, send_small), core_flight(keep_down, send_down)], [send_up]
    )
    small, down = spread_img(small), spread_img(down)

    def back_call(s, after):
        *parts, sums = attend_back_call(
            grad_attended[s], q, k, v, kt, ot, lse, imgq, imgk, lo, hi, s, after
        )
        return parts, sums

    def grad_qkv_call(s, parts, after):
        turned = [norm_gain[0].reshape(-1, 1), norm_bias[0].reshape(-1, 1)]
        return qkv_grad_call(me, unit, parts, w_qkv, *turned, s, splits, after)

    groups = row_count // 2
    far_masks = [(2 * g, 0) for g in range(1, groups)]
    same, qkv_sums, norm_sums, grad_qkv = [], [], [], []
    after, far = [small, down, send_up], None
    for s in range(splits):
        parts, sums = back_call(s, after)
        qkv_sums.append(sums[0:2])
        if s == 0:
            small, down, ups = arrive(
                [half(small, y_bits), half(down, z_bits[0]), core_flight(keep_up, send_up)], [sums]
            )
            ups = spread_img(ups)
        if s == splits - 1:
            flights = [half(ups, y_bits), half(down, z_bits[1]), half(small, z_bits[0])]
            if far is not None:
                flights.append(far)
            ups, down, small, *arrived = arrive(flights, [sums])
            for pieces_far in arrived:
                same += pieces_far
        same.append(parts[0])
        far = Moved(parts[1:], far_masks)
        grad, norm_sum = grad_qkv_call(s, parts, [ups, down])
        if s == splits - 1:
            (ups, arrived, down, small), (grad, norm_sum) = arrive_with(
                [half(ups, z_bits[0]), far, half(down, y_bits), half(small, z_bits[1])],
                (grad, norm_sum),
            )
            same += arrived
        norm_sums.append(norm_sum)
        grad_qkv.append(spread_img(grad))
        after = [grad]
    grad_qkv = jnp.concatenate(grad_qkv, axis=-1)
    near = Moved([jnp.stack([p[1] for p in same])], [(1, 0)])

    by_slot = jnp.dot(select.T, pooled.reshape(IMGS, LT * width), precision=highest)
    by_slot = by_slot.astype(bf16).reshape(row_count, -1, 128)
    late = lax.dynamic_update_slice(
        jnp.zeros((2, width), f32), jnp.concatenate(qkv_sums, axis=1), (0, device * features)
    )
    vectors = jnp.concatenate(
        [
            up_sums.reshape(-1),
            vec_sums.reshape(-1),
            jnp.sum(grad_learn_out.reshape(-1, IMGS, LT), axis=1).reshape(-1),
            late.reshape(-1),
            sum(norm_sums).T.reshape(-1),
            jnp.sum(logit_sums.reshape(IMGS, LT), axis=0),
        ]
    )
    vectors = jnp.pad(vectors, (0, -vectors.shape[0] % 1024)).reshape(-1, 128)
    made = vectors_call(vectors, by_slot)

    for bits in z_bits[2:]:
        down, small = arrive([half(down, bits), half(small, bits)])
    ((others,), grad_qkv, ups, down, small), (vectors, learned) = arrive_with(
        [
            near,
            half(grad_qkv, y_bits),
            half(ups, z_bits[1]),
            half(down, far_row),
            Exchange(small, far_row),
        ],
        tuple(made),
    )
    for bits in z_bits[2:]:
        ups, grad_qkv = arrive([half(ups, bits), half(grad_qkv, bits)])
    other = [others[s * groups : (s + 1) * groups] for s in range(splits)]
    grad_tokens = tokens_call(
        me,
        tokens[0],
        behind(grad_hidden, [ups, grad_qkv, down, small]),
        w_qkv,
        norm_gain[0:1],
        same,
        other,
        row_count,
    )
    (grad_qkv, ups), grad_tokens = arrive_with(
        [half(grad_qkv, z_bits[0]), Exchange(ups, far_row)], grad_tokens
    )
    (grad_qkv,) = arrive([half(grad_qkv, z_bits[1])])
    vectors, learned = behind((vectors, learned), [grad_tokens])
    vectors = vectors.reshape(-1)
    scale_here = jnp.dot(scale, select, precision=highest)[:slots_here]
    learned = learned.reshape(slots_here, LT * width) * scale_here[:, None]
    learned = learned.reshape(1, slots_here, LT, width)

    share_down = finish_weight(down, row_bits)
    share_small = finish_weight(small, core, [grad_tokens])
    share_up = finish_weight(ups, core)
    share_learn = share_small[:, : learn_in.shape[1]]
    share_out = share_small[:, learn_in.shape[1] :]
    shares = gather_columns(grad_qkv.reshape(grad_qkv.shape[-2:]), lambda c: c, row_bits)
    share_qkv = jnp.concatenate(
        [
            shares[c][:, (3 * s + part) * wide : (3 * s + part + 1) * wide]
            for part in range(3)
            for c in range(row_count)
            for s in range(splits)
        ],
        axis=1,
    ).astype(f32)

    at = up_bias.shape[0]
    up_sum, vec_sums = vectors[:at], vectors[at : at + 8 * width].reshape(8, width)
    at += 8 * width
    learn_out_sum = vectors[at : at + learn_out.size].reshape(learn_out.shape)
    at += learn_out.size
    late = vectors[at : at + 4 * width].reshape(4, width)
    at += 4 * width
    out_sum, down_sum, gain_two, shift_two, gain_three, shift_three, learn_in_sum = vec_sums[:7]
    share_learn_out = rows_of(learn_out_sum, image_device, learn_out.shape[0] // images_count)
    return (
        learned,
        grad_tokens,
        share_qkv,
        late[0:2],
        share_out,
        out_sum,
        share_up,
        up_sum,
        share_down,
        down_sum,
        jnp.stack([late[2], gain_two, gain_three]),
        jnp.stack([late[3], shift_two, shift_three]),
        share_learn,
        learn_in_sum,
        share_learn_out,
        vectors[at : at + learn_out.shape[1]],
    )


def solution(mesh):
    by_image = P("img", None)
    in_specs = (
        (P("img", "row", None), by_image, by_image) + (P(),) * 14 + (P("img", "row", None, None),)
    )
    out_specs = (
        P("img", "row", None, None),
        P("img", "row", None),
        by_image,
        P(),
        by_image,
        P(),
        by_image,
        P(),
        by_image,
        P(),
        P(),
        P(),
        by_image,
        P(),
        by_image,
        P(),
    )
    return jax.shard_map(
        on_device, mesh=mesh, in_specs=in_specs, out_specs=out_specs, check_vma=False
    )
```

```python
import functools

import jax
import jax.numpy as jnp
from jax import lax
from jax.experimental import pallas as pl
from jax.experimental.pallas import tpu as pltpu
from jax.sharding import PartitionSpec as P

HEADS = 16
HEAD = 64
LT = 8
IMGS = 8
BLK = 256
NEG = -1e30
VMEM = 60 << 20
ROW_BLOCK = 256
UP_BLOCK = 1024
GRAD_BLOCK = 1024

highest = lax.Precision.HIGHEST
epsilon = 1e-06
f32 = jnp.float32
bf16 = jnp.bfloat16


def smooth_both(v):
    half = jnp.abs(v) * 0.7071067811865476
    t = 1.0 / (1.0 + 0.3275911 * half)
    bell = jnp.exp(-half * half)
    poly = t * (
        0.127414796
        + t * (-0.142248368 + t * (0.7107068705 + t * (-0.7265760135 + t * 0.5307027145)))
    )
    tail = poly * bell
    cdf = jnp.where(v >= 0.0, 1.0 - tail, tail)
    return v * cdf, cdf + v * (bell * 0.3989422804014327)


def matmul(left, right):
    return jnp.dot(left, right, preferred_element_type=f32)


def nt(left, right):
    return lax.dot_general(left, right, (((1,), (1,)), ((), ())), preferred_element_type=f32)


def tn(left, right):
    return lax.dot_general(left, right, (((0,), (0,)), ((), ())), preferred_element_type=f32)


def row_images(counts, device, local_rows, row_count):
    upper_end = counts * (device + 1) // row_count
    lower_end = counts * device // row_count
    run_ends = jnp.cumsum(upper_end - lower_end)
    positions = jnp.arange(local_rows, dtype=jnp.int32)
    return jnp.sum((positions[:, None] >= run_ends[None, :]).astype(jnp.int32), axis=1)


def bits_of(size):
    return [1 << i for i in range(size.bit_length() - 1)]


def jump(value, row_mask, img_mask=0):
    rows, imgs = lax.axis_size("row"), lax.axis_size("img")
    if img_mask == 0:
        return lax.ppermute(value, "row", [(i, i ^ row_mask) for i in range(rows)])
    if row_mask == 0:
        return lax.ppermute(value, "img", [(i, i ^ img_mask) for i in range(imgs)])
    mask = img_mask * rows + row_mask
    return lax.ppermute(value, ("img", "row"), [(i, i ^ mask) for i in range(rows * imgs)])


def masks_of(bits):
    masks = []
    for e in range(1 << len(bits)):
        masks.append(
            tuple(
                sum(bit for j, (axis, bit) in enumerate(bits) if axis == name and e >> j & 1)
                for name in ("row", "img")
            )
        )
    return masks


def gather_pieces(value, count):
    pieces = {0: value}
    order = sorted(range(1, count), key=lambda d: (d & 1, d))
    for d in order:
        low = d & -d
        pieces[d] = jump(pieces[d ^ low], low)
    return [pieces[d] for d in range(count)]


def send_pieces(pieces):
    far_first = sorted(range(1, len(pieces)), reverse=True)
    arrived = {d: jump(pieces[d], d) for d in far_first}
    return [pieces[0]] + [arrived[d] for d in range(1, len(pieces))]


def stages():
    row_bits = [("row", b) for b in bits_of(lax.axis_size("row"))]
    img_bits = [("img", b) for b in bits_of(lax.axis_size("img"))]
    return row_bits, img_bits


def tree(values):
    while len(values) > 1:
        values = [values[i] + values[i + 1] for i in range(0, len(values), 2)]
    return values[0]


def behind(value, after):
    return lax.optimization_barrier((value, tuple(after)))[0] if after else value


class Halving:
    def __init__(self, value, bits, img_count):
        mine = {"row": lax.axis_index("row"), "img": lax.axis_index("img")}

        def part(e):
            piece = value
            for j, (axis, bit) in enumerate(bits):
                want = (mine[axis] // bit) % 2 ^ (e >> j & 1)
                dim = value.ndim - 1 if axis == "row" else img_count - bit.bit_length()
                length = piece.shape[dim] // 2
                piece = lax.dynamic_slice_in_dim(piece, want * length, length, dim)
            return piece

        masks = masks_of(bits)
        self.kept = part(0)
        self.moved = [jump(part(e), *masks[e]) for e in range(1, len(masks))]

    def finish(self):
        values = [self.kept, *self.moved]
        return tree([v.astype(f32) for v in values]).astype(bf16)


class Exchange(Halving):
    def __init__(self, value, bits):
        self.kept = value
        self.moved = [jump(value, *mask) for mask in masks_of(bits)[1:]]


class Moved(Halving):
    def __init__(self, values, masks):
        self.moved = [jump(v, *mask) for v, mask in zip(values, masks)]

    def finish(self):
        return self.moved


def arrive(flights, after=()):
    return arrive_with(flights, tuple(after))[0]


def arrive_with(flights, beside):
    flat = [m for flight in flights for m in flight.moved]
    flat, beside = lax.optimization_barrier((flat, beside))
    for flight in flights:
        flight.moved, flat = flat[: len(flight.moved)], flat[len(flight.moved) :]
    return [flight.finish() for flight in flights], beside


def spread_img(grad):
    rows, columns = grad.shape
    images = lax.axis_size("img")
    return grad.reshape((2,) * len(bits_of(images)) + (rows // images, columns))


def gather_columns(value, order, bits, after=()):
    masks = [row_mask for row_mask, _ in masks_of(bits)]
    device = lax.axis_index("row") % len(masks)
    stack = jnp.stack([value if m == 0 else behind(jump(value, m), after) for m in masks])
    return [
        lax.dynamic_index_in_dim(stack, order(c) ^ device, 0, False) for c in range(len(masks))
    ]


def reversed_bits(index, size):
    width = size.bit_length() - 1
    return int(format(index, f"0{width}b")[::-1], 2) if width else 0


def finish_weight(value, bits, after=()):
    value = value.reshape(value.shape[-2:])
    count = 1 << len(bits)
    blocks = gather_columns(value, lambda c: reversed_bits(c, count), bits, after)
    return jnp.concatenate(blocks, axis=1).astype(f32)


def params(flags=("arbitrary",)):
    return pltpu.CompilerParams(dimension_semantics=flags, vmem_limit_bytes=VMEM)


ANYWHERE = pl.BlockSpec(memory_space=pl.ANY)


def own_columns(w_qkv, features, splits, chosen):
    width = w_qkv.shape[0]
    wide = features // splits

    def spec(s, part):
        def index(b, me):
            return 0, part * (width // wide) + me[0] * splits + s

        return pl.BlockSpec((width, wide), index, pipeline_mode=pl.Buffered(1))

    return [spec(s, part) for s in chosen for part in range(3)], [w_qkv] * (3 * len(chosen))


def valid_rows(block, piece_rows, local_rows):
    position = lax.broadcasted_iota(jnp.int32, (BLK, 1), 0) % piece_rows + block * piece_rows
    return position < local_rows


def load_block(refs, block, piece_rows, local_rows):
    value = jnp.concatenate([ref[...] for ref in refs], axis=0).astype(f32)
    return jnp.where(valid_rows(block, piece_rows, local_rows), value, 0.0)


def norm_parts(value):
    centre = value - jnp.mean(value, axis=-1, keepdims=True)
    rstd = lax.rsqrt(jnp.mean(centre * centre, axis=-1, keepdims=True) + epsilon)
    return centre * rstd, rstd


def qkv_kernel(count, splits, local_rows, features, held, me_ref, *refs):
    n_w = 3 * splits
    pieces, columns = refs[:count], refs[count : count + n_w]
    bias_ref, gain_ref, shift_ref = refs[count + n_w : count + n_w + 3]
    n_ref, q_ref, k_ref, v_ref, kt_ref, vt_ref, w_ref = refs[count + n_w + 3 + held :]
    step = pl.program_id(0)
    wide = features // splits
    half = BLK // 2
    rows = half // count

    @pl.when(step == 0)
    def _():
        for i, ref in enumerate(columns):
            w_ref[:, i * wide : (i + 1) * wide] = ref[...]

    places = [(b, d) for b in range(2) for d in range(count)]
    value = jnp.concatenate(
        [pieces[d][b * rows : (b + 1) * rows, :] for b, d in places], axis=0
    ).astype(f32)
    row = lax.broadcasted_iota(jnp.int32, (BLK, 1), 0)
    position = (2 * step + row // half) * rows + row % rows
    unit, _ = norm_parts(jnp.where(position < local_rows, value, 0.0))
    normed = (unit * gain_ref[...] + shift_ref[...]).astype(bf16)
    low = unit.astype(bf16)
    for i, (b, d) in enumerate(places):
        n_ref[d, b * rows : (b + 1) * rows, :] = low[i * rows : (i + 1) * rows]
    mixed = matmul(normed, w_ref[...])
    for s in range(splits):
        at = slice(s * wide, (s + 1) * wide)
        part = mixed[:, 3 * s * wide : 3 * (s + 1) * wide]
        queries = ((part[:, :wide] + bias_ref[0:1, at]) * 0.125).astype(bf16)
        keys = part[:, wide : 2 * wide]
        values = part[:, 2 * wide :] + bias_ref[1:2, at]
        keys_low, values_low = keys.astype(bf16), values.astype(bf16)
        keys_turned, values_turned = keys.T.astype(bf16), values.T.astype(bf16)
        for b in range(2):
            here = slice(b * half, (b + 1) * half)
            q_ref[b, 0, :, at] = queries[here]
            k_ref[b, 0, :, at] = keys_low[here]
            v_ref[b, 0, :, at] = values_low[here]
            kt_ref[b, at, :] = keys_turned[:, here]
            vt_ref[b, at, :] = values_turned[:, here]


def qkv_call(me, pieces, part, w_qkv, bias, gain, shift, splits, held=()):
    count, (local_rows, width) = len(pieces), pieces[0].shape
    features = width // (2 * count)
    rows = BLK // 2 // count
    blocks = pl.cdiv(local_rows, rows)
    whole = lambda a: pl.BlockSpec(a.shape, lambda b, m: (0,) * a.ndim)
    flat = pl.BlockSpec((2, 1, BLK // 2, features), lambda b, m: (b, part, 0, 0))
    turned = pl.BlockSpec((2, features, BLK // 2), lambda b, m: (b, 0, part))
    specs, operands = own_columns(w_qkv, features, splits, range(splits))
    at = 1 + count + 3 * splits + 3
    return pl.pallas_call(
        functools.partial(qkv_kernel, count, splits, local_rows, features, len(held)),
        grid_spec=pltpu.PrefetchScalarGridSpec(
            num_scalar_prefetch=1,
            grid=(blocks // 2,),
            in_specs=[pl.BlockSpec((2 * rows, width), lambda b, m: (b, 0))] * count
            + specs
            + [whole(bias), whole(gain), whole(shift)]
            + [ANYWHERE] * len(held),
            out_specs=[
                pl.BlockSpec((count, 2 * rows, width), lambda b, m: (part, b, 0)),
                flat,
                flat,
                flat,
                turned,
                turned,
            ],
            scratch_shapes=[pltpu.VMEM((width, 3 * features), bf16)],
        ),
        out_shape=[jax.ShapeDtypeStruct((2 * count, blocks * rows, width), bf16)]
        + [jax.ShapeDtypeStruct((blocks, 2, BLK // 2, features), bf16)] * 3
        + [jax.ShapeDtypeStruct((blocks, features, BLK), bf16)] * 2,
        input_output_aliases={at + i: i for i in range(len(held))},
        compiler_params=params(),
        cost_estimate=pl.CostEstimate(
            flops=6 * blocks * BLK * width * 3 * features,
            bytes_accessed=blocks * BLK * (2 * width + 5 * features),
            transcendentals=0,
        ),
    )(me, *pieces, *operands, bias, gain, shift, *held)


def per_head(stack_ref, value, heads):
    lane = lax.broadcasted_iota(jnp.int32, value.shape, 1) // HEAD
    for h in range(heads):
        stack_ref[h * BLK : (h + 1) * BLK] = jnp.where(lane == h, value, jnp.zeros_like(value))


def in_pairs(lo, hi, step, carry):
    pairs = (hi - lo) // 2
    carry = lax.fori_loop(0, pairs, lambda i, c: step(lo + 2 * i, 2, c), carry)
    return lax.fori_loop(lo + 2 * pairs, hi, lambda kb, c: step(kb, 1, c), carry)


def attend_kernel(count, heads, start, held, lo_ref, hi_ref, *refs):
    q_ref, k_ref, vt_ref, imgq_ref, imgk_ref = refs[:5]
    refs = refs[5 + held :]
    outs, (ot_ref, lse_ref), (s_ref, qs_ref, acc_ref) = refs[:count], refs[count : count + 2], refs[count + 2 :]
    block = pl.program_id(0) + start
    lo, hi = lo_ref[block], hi_ref[block]
    per_head(qs_ref, q_ref[...], heads)
    imgq = imgq_ref[...]

    def first(kb, width, tops):
        rows = pl.ds(pl.multiple_of(kb * BLK, BLK), width * BLK)
        allowed = imgk_ref[rows, :] == imgq
        s = nt(k_ref[rows, :], qs_ref[...])
        new = []
        for h in range(heads):
            cols = slice(h * BLK, (h + 1) * BLK)
            part = jnp.where(allowed, s[:, cols], NEG)
            for j in range(width):
                s_ref[kb - lo + j, :, cols] = part[j * BLK : (j + 1) * BLK]
            high = jnp.max(part.reshape(width * BLK // 8, 8, BLK), axis=0)
            new.append(jnp.maximum(tops[h], high))
        return tuple(new)

    tops = in_pairs(lo, hi, first, (jnp.full((8, BLK), NEG, f32),) * heads)
    tops = [jnp.max(t, axis=0, keepdims=True) for t in tops]
    acc_ref[...] = jnp.zeros_like(acc_ref)

    def second(kb, width, sums):
        new = []
        for h in range(heads):
            rows, cols = slice(h * HEAD, (h + 1) * HEAD), slice(h * BLK, (h + 1) * BLK)
            part, weights = 0.0, sums[h]
            for j in range(width):
                p = jnp.exp(s_ref[kb - lo + j, :, cols] - tops[h])
                weights = weights + jnp.sum(p.reshape(BLK // 8, 8, BLK), axis=0)
                part = part + matmul(vt_ref[kb + j, rows, :], p.astype(bf16))
            new.append(weights)
            acc_ref[rows, :] += part
        return tuple(new)

    sums = in_pairs(lo, hi, second, (jnp.zeros((8, BLK), f32),) * heads)
    sums = [jnp.sum(t, axis=0, keepdims=True) for t in sums]
    for h in range(heads):
        rows = slice(h * HEAD, (h + 1) * HEAD)
        acc_ref[rows, :] = acc_ref[rows, :] / sums[h]
    lse_ref[...] = jnp.concatenate(
        [t + jnp.log(s) for t, s in zip(tops, sums)] + [jnp.zeros((8 - heads, BLK), f32)], axis=0
    )
    ot_ref[0] = acc_ref[...]
    out = acc_ref[...].T.astype(bf16)
    for d in range(count):
        outs[d][...] = out[d * (BLK // count) : (d + 1) * (BLK // count)]


def attend_call(q, k, vt, imgq, imgk, lo, hi, count, part, held=()):
    blocks, features = vt.shape[0], q.shape[1]
    heads = features // HEAD
    piece_rows = BLK // count
    steps = blocks // 2
    start = part * steps
    whole = lambda a: pl.BlockSpec(
        a.shape, lambda b, *_: (0,) * a.ndim, pipeline_mode=pl.Buffered(1)
    )
    return pl.pallas_call(
        functools.partial(attend_kernel, count, heads, start, len(held)),
        grid_spec=pltpu.PrefetchScalarGridSpec(
            num_scalar_prefetch=2,
            grid=(steps,),
            in_specs=[
                pl.BlockSpec((BLK, features), lambda b, *_: (b + start, 0)),
                whole(k),
                whole(vt),
                pl.BlockSpec((1, BLK), lambda b, *_: (0, b + start)),
                whole(imgk),
            ]
            + [ANYWHERE] * len(held),
            out_specs=[pl.BlockSpec((piece_rows, features), lambda b, *_: (b, 0))] * count
            + [
                pl.BlockSpec((1, features, BLK), lambda b, *_: (b + start, 0, 0)),
                pl.BlockSpec((8, BLK), lambda b, *_: (0, b + start)),
            ],
            scratch_shapes=[
                pltpu.VMEM((blocks, BLK, heads * BLK), f32),
                pltpu.VMEM((heads * BLK, features), bf16),
                pltpu.VMEM((features, BLK), f32),
            ],
        ),
        out_shape=[jax.ShapeDtypeStruct((steps * piece_rows, features), bf16)] * count
        + [
            jax.ShapeDtypeStruct((blocks, features, BLK), f32),
            jax.ShapeDtypeStruct((8, blocks * BLK), f32),
        ],
        input_output_aliases={7 + i: count + i for i in range(len(held))},
        compiler_params=params(),
        cost_estimate=pl.CostEstimate(
            flops=5 * (blocks * BLK) ** 2 * features,
            bytes_accessed=2 * blocks * BLK * features * 6,
            transcendentals=0,
        ),
    )(lo, hi, q, k, vt, imgq, imgk, *held)


def attend_back_kernel(count, heads, first, waits, lo_ref, hi_ref, *refs):
    pieces, refs = refs[:count], refs[:count] + refs[count + waits :]
    q_ref, k_ref, v_ref, kt_ref, ot_ref, lse_ref, imgq_ref, imgk_ref = refs[count : count + 8]
    groups = count // 2
    outs, sums_ref = refs[count + 8 : count + groups + 8], refs[count + groups + 8]
    qs_ref, dos_ref, p_ref, ds_ref, dqt_ref, dk_ref, dv_ref = refs[count + groups + 9 :]
    block = pl.program_id(0)
    lo, hi = lo_ref[block], hi_ref[block]
    piece_rows = BLK // count
    wide = heads * HEAD

    @pl.when(block == 0)
    def _():
        dk_ref[...] = jnp.zeros_like(dk_ref)
        dv_ref[...] = jnp.zeros_like(dv_ref)
        sums_ref[...] = jnp.zeros_like(sums_ref)

    grad = jnp.concatenate([ref[...] for ref in pieces], axis=0)
    query = q_ref[...]
    lane = lax.broadcasted_iota(jnp.int32, grad.shape, 1) // HEAD
    for h in range(heads):
        dos_ref[h * BLK : (h + 1) * BLK] = jnp.where(lane == h, grad, jnp.zeros_like(grad))
        qs_ref[h * BLK : (h + 1) * BLK] = jnp.where(lane == h, query, jnp.zeros_like(query))
    both = grad.astype(f32).T * ot_ref[0]
    delta = [
        jnp.sum(both[h * HEAD : (h + 1) * HEAD], axis=0, keepdims=True) for h in range(heads)
    ]
    logsum = [lse_ref[first + h : first + h + 1, :] for h in range(heads)]
    imgq = imgq_ref[...]
    dqt_ref[...] = jnp.zeros_like(dqt_ref)

    def step(kb, width):
        length = width * BLK
        rows = pl.ds(pl.multiple_of(kb * BLK, BLK), length)
        keys, values = k_ref[rows, :], v_ref[rows, :]
        allowed = imgk_ref[rows, :] == imgq
        s = nt(keys, qs_ref[...])
        dp = nt(values, dos_ref[...])
        for h in range(heads):
            cols = slice(h * BLK, (h + 1) * BLK)
            p = jnp.exp(jnp.where(allowed, s[:, cols] - logsum[h], NEG))
            p_ref[:length, cols] = p.astype(bf16)
            ds_ref[:length, cols] = (p * (dp[:, cols] - delta[h])).astype(bf16)
        dv_ref[rows, :] += matmul(p_ref[:length], dos_ref[...])
        dk_ref[rows, :] += matmul(ds_ref[:length], qs_ref[...])
        for h in range(heads):
            cols, feats = slice(h * BLK, (h + 1) * BLK), slice(h * HEAD, (h + 1) * HEAD)
            total = 0.0
            for j in range(width):
                ds = ds_ref[j * BLK : (j + 1) * BLK, cols]
                total = total + matmul(kt_ref[kb + j, feats, :], ds)
            dqt_ref[feats, :] += total

    def pair(i, _):
        step(lo + 2 * i, 2)
        return 0

    lax.fori_loop(0, (hi - lo) // 2, pair, 0)

    @pl.when((hi - lo) % 2 == 1)
    def _():
        step(hi - 1, 1)

    dq = dqt_ref[...].T * 0.125
    sums_ref[0:1, :] += jnp.sum(dq, axis=0, keepdims=True)
    here = pl.ds(pl.multiple_of(block * piece_rows, piece_rows), piece_rows)
    for d in range(count):
        outs[d // 2][d % 2, here, :wide] = dq[d * piece_rows : (d + 1) * piece_rows].astype(bf16)

    @pl.when(block == pl.num_programs(0) - 1)
    def _():
        sums_ref[1:2, :] = jnp.sum(dv_ref[...], axis=0, keepdims=True)

        def move(b, _):
            to = pl.ds(pl.multiple_of(b * piece_rows, piece_rows), piece_rows)
            for d in range(count):
                at = pl.ds(pl.multiple_of(b * BLK + d * piece_rows, piece_rows), piece_rows)
                outs[d // 2][d % 2, to, wide : 2 * wide] = dk_ref[at, :].astype(bf16)
                outs[d // 2][d % 2, to, 2 * wide :] = dv_ref[at, :].astype(bf16)
            return 0

        lax.fori_loop(0, pl.num_programs(0), move, 0)


def attend_back_call(pieces, q, k, v, kt, ot, lse, imgq, imgk, lo, hi, split, after):
    count, (rows, wide) = len(pieces), pieces[0].shape
    blocks = kt.shape[0]
    heads = wide // HEAD
    once = pl.Buffered(1)
    half = pl.BlockSpec((blocks * BLK, wide), lambda b, *_: (0, split), pipeline_mode=once)
    out = jax.ShapeDtypeStruct((2, rows, 3 * wide), bf16)
    return pl.pallas_call(
        functools.partial(attend_back_kernel, count, heads, split * heads, len(after)),
        grid_spec=pltpu.PrefetchScalarGridSpec(
            num_scalar_prefetch=2,
            grid=(blocks,),
            in_specs=[pl.BlockSpec((BLK // count, wide), lambda b, *_: (b, 0))] * count
            + [ANYWHERE] * len(after)
            + [
                pl.BlockSpec((BLK, wide), lambda b, *_: (b, split)),
                half,
                half,
                pl.BlockSpec((blocks, wide, BLK), lambda b, *_: (0, split, 0), pipeline_mode=once),
                pl.BlockSpec((1, wide, BLK), lambda b, *_: (b, split, 0)),
                pl.BlockSpec((8, BLK), lambda b, *_: (0, b)),
                pl.BlockSpec((1, BLK), lambda b, *_: (0, b)),
                pl.BlockSpec(imgk.shape, lambda b, *_: (0, 0), pipeline_mode=once),
            ],
            out_specs=[pl.BlockSpec(out.shape, lambda b, *_: (0, 0, 0), pipeline_mode=once)] * (count // 2)
            + [pl.BlockSpec((8, wide), lambda b, *_: (0, 0))],
            scratch_shapes=[
                pltpu.VMEM((heads * BLK, wide), bf16),
                pltpu.VMEM((heads * BLK, wide), bf16),
                pltpu.VMEM((2 * BLK, heads * BLK), bf16),
                pltpu.VMEM((2 * BLK, heads * BLK), bf16),
                pltpu.VMEM((wide, BLK), f32),
                pltpu.VMEM((blocks * BLK, wide), f32),
                pltpu.VMEM((blocks * BLK, wide), f32),
            ],
        ),
        out_shape=[out] * (count // 2) + [jax.ShapeDtypeStruct((8, wide), f32)],
        compiler_params=params(),
        cost_estimate=pl.CostEstimate(
            flops=16 * (blocks * BLK) ** 2 * wide,
            bytes_accessed=2 * blocks * BLK * wide * 12,
            transcendentals=0,
        ),
    )(lo, hi, *pieces, *after, q, k, v, kt, ot, lse, imgq, imgk)


def norm_back(grad, unit, rstd, gain):
    e = grad * gain
    mean = jnp.mean(e, axis=-1, keepdims=True)
    return (e - mean - unit * jnp.mean(e * unit, axis=-1, keepdims=True)) * rstd


def total(value):
    return jnp.sum(value, axis=0, keepdims=True)


def rows_kernel(count, splits, local_rows, *refs):
    (
        tok_ref,
        img_ref,
        w_out_ref,
        w_up_ref,
        w_down_ref,
        learn_in_ref,
        learn_out_ref,
        vec_ref,
        up_bias_ref,
        out_bias_ref,
        pooled_grad_ref,
    ) = refs[:11]
    upper, lower = refs[11 : 11 + count], refs[11 + count : 11 + 2 * count]
    at = 11 + 2 * count
    (
        n2_ref,
        gated_ref,
        gup_ref,
        gres_ref,
        n3_ref,
        glearn_ref,
        inner_ref,
        glogit_ref,
        ghid_ref,
        ghid_f32_ref,
    ) = refs[at : at + 10]
    gatt = refs[at + 10 : at + 10 + count * splits]
    at += 10 + count * splits
    pooled_ref, vsum_ref, usum_ref, lsum_ref = refs[at : at + 4]
    hid_ref, res_ref, dgate_ref, up0_ref, up1_ref = refs[at + 4 :]
    step = pl.program_id(0)
    rows, width = tok_ref.shape
    hidden_units = w_up_ref.shape[1]
    chunk = up0_ref.shape[1]
    chunks = hidden_units // chunk

    @pl.when(step == 0)
    def _():
        for ref in (pooled_ref, vsum_ref, usum_ref, lsum_ref):
            ref[...] = jnp.zeros_like(ref)

    def vec(i):
        return vec_ref[i : i + 1, :]

    position = lax.broadcasted_iota(jnp.int32, (rows, 1), 0) + step * rows
    tok = jnp.where(position < local_rows, tok_ref[...].astype(f32), 0.0)
    early = step < pl.num_programs(0) // 2
    low = jnp.concatenate(
        [jnp.where(early, a[...], b[...]) for a, b in zip(upper, lower)], axis=1
    )
    hidden = tok + matmul(low, w_out_ref[...]) + vec(0)
    hid_ref[...] = hidden
    unit, _ = norm_parts(hidden)
    n2_ref[...] = (unit * vec(2) + vec(3)).astype(bf16)

    def columns(j):
        return pl.ds(pl.multiple_of(j * chunk, chunk), chunk)

    def up(ref, j):
        ref[...] = matmul(n2_ref[...], w_up_ref[:, columns(j)])

    def gate(ref, j):
        value, slope = smooth_both(ref[...] + up_bias_ref[:, columns(j)])
        gated_ref[:, columns(j)] = value.astype(bf16)
        dgate_ref[:, columns(j)] = slope

    up(up0_ref, 0)

    def pair(i, _):
        up(up1_ref, 2 * i + 1)
        gate(up0_ref, 2 * i)
        up(up0_ref, jnp.minimum(2 * i + 2, chunks - 1))
        gate(up1_ref, 2 * i + 1)
        return 0

    lax.fori_loop(0, chunks // 2, pair, 0)
    result = hid_ref[...] + matmul(gated_ref[...], w_down_ref[...]) + vec(1)
    res_ref[...] = result
    unit, rstd = norm_parts(result)
    n3_ref[...] = (unit * vec(4) + vec(5)).astype(bf16)
    inner, slope = smooth_both(matmul(n3_ref[...], learn_in_ref[...]) + vec(6))
    inner_ref[...] = inner.astype(bf16)
    maps = jax.nn.sigmoid(matmul(inner_ref[...], learn_out_ref[...]) + out_bias_ref[...])
    member = lax.broadcasted_iota(jnp.int32, maps.shape, 1) // LT == img_ref[...]
    spread = jnp.where(member, maps, 0.0).astype(bf16)
    result_low = res_ref[...].astype(bf16)
    pooled_ref[...] += tn(spread, result_low)
    grad_spread = nt(result_low, pooled_grad_ref[...])
    grad_logit = jnp.where(member, grad_spread * maps * (1.0 - maps), 0.0)
    lsum_ref[...] += total(grad_logit)
    glogit_ref[...] = grad_logit.astype(bf16)
    grad_pre = nt(glogit_ref[...], learn_out_ref[...]) * slope
    vsum_ref[6:7, :] += total(grad_pre)
    glearn_ref[...] = grad_pre.astype(bf16)
    back = nt(glearn_ref[...], learn_in_ref[...])
    unit, rstd = norm_parts(res_ref[...])
    vsum_ref[4:5, :] += total(back * unit)
    vsum_ref[5:6, :] += total(back)
    grad_result = matmul(spread, pooled_grad_ref[...]) + norm_back(back, unit, rstd, vec(4))
    vsum_ref[1:2, :] += total(grad_result)
    res_ref[...] = grad_result
    gres_ref[...] = grad_result.astype(bf16)

    def down_back(j, _):
        grad = nt(gres_ref[...], w_down_ref[columns(j), :]) * dgate_ref[:, columns(j)]
        usum_ref[:, columns(j)] += total(grad)
        gup_ref[:, columns(j)] = grad.astype(bf16)
        return 0

    lax.fori_loop(0, chunks, down_back, 0)
    back = nt(gup_ref[...], w_up_ref[...])
    unit, rstd = norm_parts(hid_ref[...])
    vsum_ref[2:3, :] += total(back * unit)
    vsum_ref[3:4, :] += total(back)
    grad_hidden = res_ref[...] + norm_back(back, unit, rstd, vec(2))
    vsum_ref[0:1, :] += total(grad_hidden)
    ghid_f32_ref[...] = grad_hidden
    ghid_ref[...] = grad_hidden.astype(bf16)
    grad = nt(ghid_ref[...], w_out_ref[...]).astype(bf16)
    wide = width // (count * splits)
    for i in range(count * splits):
        gatt[i][...] = grad[:, i * wide : (i + 1) * wide]


def rows_call(tok, img, attended, w_out, w_up, w_down, learn_in, learn_out, vecs, up_bias, out_bias, pooled_grad, splits):
    count, (rows, features) = len(attended) // 2, attended[0].shape
    rows *= 2
    local_rows, width = tok.shape
    hidden_units = w_up.shape[1]
    inner = learn_in.shape[1]
    spread = learn_out.shape[1]
    block = min(ROW_BLOCK, rows // 2)
    half = rows // block // 2
    chunk = UP_BLOCK
    wide = features // splits
    once = lambda a: pl.BlockSpec(a.shape, lambda i: (0,) * a.ndim, pipeline_mode=pl.Buffered(1))
    by_rows = lambda n: pl.BlockSpec((block, n), lambda i: (i, 0))
    kept = lambda a: pl.BlockSpec(a.shape, lambda i: (0, 0))
    low = lambda n: jax.ShapeDtypeStruct((rows, n), bf16)
    lows = [width, hidden_units, hidden_units, width, width, inner, inner, spread, width]
    sums = [
        jax.ShapeDtypeStruct((spread, width), f32),
        jax.ShapeDtypeStruct((8, width), f32),
        jax.ShapeDtypeStruct((1, hidden_units), f32),
        jax.ShapeDtypeStruct((1, spread), f32),
    ]
    resident = [w_out, w_up, w_down, learn_in, learn_out, vecs, up_bias, out_bias, pooled_grad]
    return pl.pallas_call(
        functools.partial(rows_kernel, count, splits, local_rows),
        grid=(rows // block,),
        in_specs=[by_rows(width), by_rows(1)]
        + [once(a) for a in resident]
        + [pl.BlockSpec((block, features), lambda i: (jnp.minimum(i, half - 1), 0))] * count
        + [pl.BlockSpec((block, features), lambda i: (jnp.maximum(i - half, 0), 0))] * count,
        out_specs=[by_rows(n) for n in lows]
        + [by_rows(width)]
        + [by_rows(wide)] * (count * splits)
        + [kept(a) for a in sums],
        out_shape=[low(n) for n in lows]
        + [jax.ShapeDtypeStruct((rows, width), f32)]
        + [low(wide)] * (count * splits)
        + sums,
        scratch_shapes=[
            pltpu.VMEM((block, width), f32),
            pltpu.VMEM((block, width), f32),
            pltpu.VMEM((block, hidden_units), f32),
            pltpu.VMEM((block, chunk), f32),
            pltpu.VMEM((block, chunk), f32),
        ],
        compiler_params=params(),
        cost_estimate=pl.CostEstimate(
            flops=4 * rows * width * (width + 2 * hidden_units + inner),
            bytes_accessed=2 * (rows * 20 * width + 2 * width * hidden_units),
            transcendentals=0,
        ),
    )(tok, img, *resident, *attended)


def part_halves(me_ref, value, keep_ref, send_ref, whole_ref):
    half = value.shape[1] // 2
    core = me_ref[0] % 2
    whole_ref[...] = value
    keep_ref[...] = whole_ref[:, pl.ds(pl.multiple_of(core * half, half), half)]
    send_ref[...] = whole_ref[:, pl.ds(pl.multiple_of((1 - core) * half, half), half)]


def down_grad_kernel(waits, me_ref, left_ref, right_ref, *refs):
    part_halves(me_ref, tn(left_ref[...], right_ref[...]).astype(bf16), *refs[waits:])


def down_grad_call(me, left, right, after=()):
    rows, m = left.shape
    n = right.shape[1]
    out = pl.BlockSpec((GRAD_BLOCK, n // 2), lambda j, m: (j, 0))
    return pl.pallas_call(
        functools.partial(down_grad_kernel, len(after)),
        grid_spec=pltpu.PrefetchScalarGridSpec(
            num_scalar_prefetch=1,
            grid=(m // GRAD_BLOCK,),
            in_specs=[
                pl.BlockSpec((rows, GRAD_BLOCK), lambda j, m: (0, j)),
                pl.BlockSpec((rows, n), lambda j, m: (0, 0), pipeline_mode=pl.Buffered(1)),
            ]
            + [ANYWHERE] * len(after),
            out_specs=[out, out],
            scratch_shapes=[pltpu.VMEM((GRAD_BLOCK, n), bf16)],
        ),
        out_shape=[jax.ShapeDtypeStruct((m, n // 2), bf16)] * 2,
        compiler_params=params(),
        cost_estimate=pl.CostEstimate(
            flops=3 * rows * m * n, bytes_accessed=4 * m * n, transcendentals=0
        ),
    )(me, left, right, *after)


def up_grad_kernel(half, waits, me_ref, left_ref, right_ref, *refs):
    keep_ref, send_ref = refs[waits:]
    value = tn(left_ref[...], right_ref[...]).astype(bf16)

    @pl.when(pl.program_id(0) < half)
    def _():
        send_ref[...] = value

    @pl.when(pl.program_id(0) >= half)
    def _():
        keep_ref[...] = value


def up_grad_call(me, left, right, after=()):
    rows, m = left.shape
    n = right.shape[1]
    half = n // GRAD_BLOCK // 2

    def column(j, core):
        return jnp.where(j < half, (1 - core) * half + j, core * half + j - half)

    return pl.pallas_call(
        functools.partial(up_grad_kernel, half, len(after)),
        grid_spec=pltpu.PrefetchScalarGridSpec(
            num_scalar_prefetch=1,
            grid=(2 * half,),
            in_specs=[
                pl.BlockSpec((rows, m), lambda j, me: (0, 0), pipeline_mode=pl.Buffered(1)),
                pl.BlockSpec((rows, GRAD_BLOCK), lambda j, me: (0, column(j, me[0] % 2))),
            ]
            + [ANYWHERE] * len(after),
            out_specs=[
                pl.BlockSpec((m, GRAD_BLOCK), lambda j, me: (0, jnp.maximum(j - half, 0))),
                pl.BlockSpec((m, GRAD_BLOCK), lambda j, me: (0, jnp.minimum(j, half - 1))),
            ],
        ),
        out_shape=[jax.ShapeDtypeStruct((m, n // 2), bf16)] * 2,
        compiler_params=params(),
        cost_estimate=pl.CostEstimate(
            flops=3 * rows * m * n, bytes_accessed=4 * m * n, transcendentals=0
        ),
    )(me, left, right, *after)


def small_grad_kernel(count, me_ref, *refs):
    n3_ref, glearn_ref, ghid_ref, inner_ref, glogit_ref = refs[:5]
    attended = refs[5 : 5 + 2 * count]
    keep_ref, send_ref, lout_ref, learn_ref, wout_ref = refs[5 + 2 * count :]
    half = attended[0].shape[0]
    learn_ref[...] = tn(n3_ref[...], glearn_ref[...]).astype(bf16)
    lout_ref[...] = tn(inner_ref[...], glogit_ref[...])
    features = attended[0].shape[1]
    for d in range(count):
        owner = jnp.bitwise_xor(me_ref[0], d)
        to = pl.ds(pl.multiple_of(owner * features, features), features)
        part = tn(attended[d][...], ghid_ref[:half])
        part = part + tn(attended[count + d][...], ghid_ref[half:])
        wout_ref[to, :] = part.astype(bf16)
    first = me_ref[0] % 2 == 0

    @pl.when(first)
    def _():
        keep_ref[...] = learn_ref[...]
        send_ref[...] = wout_ref[...]

    @pl.when(jnp.logical_not(first))
    def _():
        keep_ref[...] = wout_ref[...]
        send_ref[...] = learn_ref[...]


def small_grad_call(me, n3, glearn, ghid, inner, glogit, attended):
    rows, width = n3.shape
    operands = [n3, glearn, ghid, inner, glogit, *attended]
    out = jax.ShapeDtypeStruct((width, ghid.shape[1]), bf16)
    lout = jax.ShapeDtypeStruct((inner.shape[1], glogit.shape[1]), f32)
    once = lambda a: pl.BlockSpec(a.shape, lambda j, m: (0, 0), pipeline_mode=pl.Buffered(1))
    return pl.pallas_call(
        functools.partial(small_grad_kernel, len(attended) // 2),
        grid_spec=pltpu.PrefetchScalarGridSpec(
            num_scalar_prefetch=1,
            grid=(1,),
            in_specs=[once(a) for a in operands],
            out_specs=[once(out), once(out), once(lout)],
            scratch_shapes=[pltpu.VMEM(out.shape, bf16), pltpu.VMEM(out.shape, bf16)],
        ),
        out_shape=[out, out, lout],
        compiler_params=params(),
        cost_estimate=pl.CostEstimate(
            flops=6 * rows * width * width, bytes_accessed=20 * width * width, transcendentals=0
        ),
    )(me, *operands)


def qkv_grad_kernel(groups, waits, me_ref, n_ref, gain_ref, shift_ref, *refs):
    parts, weights = refs[:groups], refs[groups : groups + 3]
    out_ref, sums_ref, acc_ref, sum_ref = refs[groups + 3 + waits :]
    step = pl.program_id(0)
    wide = weights[0].shape[1]
    for d in range(2 * groups):

        @pl.when(step == d)
        def _():
            mixed = parts[d // 2][d % 2]
            part = tn(n_ref[0], mixed)
            column = total(mixed.astype(f32))
            acc_ref[...] = part if d == 0 else acc_ref[...] + part
            sum_ref[...] = column if d == 0 else sum_ref[...] + column

    @pl.when(step == 2 * groups - 1)
    def _():
        by_unit, column = acc_ref[...], sum_ref[...]
        out_ref[...] = (by_unit * gain_ref[...] + shift_ref[...] * column).astype(bf16)
        weight = jnp.concatenate([ref[...].astype(f32) for ref in weights], axis=1)
        sums_ref[:, 0:1] = jnp.sum(by_unit * weight, axis=1, keepdims=True)
        sums_ref[:, 1:2] = jnp.sum(weight * column, axis=1, keepdims=True)


def qkv_grad_call(me, unit, parts, w_qkv, gain, shift, split, splits, after=()):
    count, rows, width = unit.shape
    columns = parts[0].shape[2]
    once = lambda a: pl.BlockSpec(
        a.shape, lambda d, m: (0,) * len(a.shape), pipeline_mode=pl.Buffered(1)
    )
    specs, operands = own_columns(w_qkv, width // count, splits, [split])
    return pl.pallas_call(
        functools.partial(qkv_grad_kernel, count // 2, len(after)),
        grid_spec=pltpu.PrefetchScalarGridSpec(
            num_scalar_prefetch=1,
            grid=(count,),
            in_specs=[pl.BlockSpec((1, rows, width), lambda d, m: (d, 0, 0)), once(gain), once(shift)]
            + [once(a) for a in parts]
            + specs
            + [ANYWHERE] * len(after),
            out_specs=[
                pl.BlockSpec((width, columns), lambda d, m: (0, 0)),
                pl.BlockSpec((width, 2), lambda d, m: (0, 0)),
            ],
            scratch_shapes=[pltpu.VMEM((width, columns), f32), pltpu.VMEM((1, columns), f32)],
        ),
        out_shape=[
            jax.ShapeDtypeStruct((width, columns), bf16),
            jax.ShapeDtypeStruct((width, 2), f32),
        ],
        compiler_params=params(),
        cost_estimate=pl.CostEstimate(flops=1 << 34, bytes_accessed=1 << 10, transcendentals=0),
    )(me, unit, gain, shift, *parts, *operands, *after)


def tokens_kernel(groups, splits, me_ref, tok_ref, ghid_ref, w_ref, gain_ref, *refs):
    same, other = refs[: groups * splits], refs[groups * splits : groups * splits + splits]
    out_ref, mixed_ref = refs[groups * splits + splits :]
    width = tok_ref.shape[1]
    features = width // (2 * groups)
    wide = features // splits
    for d in range(2 * groups):
        owner = jnp.bitwise_xor(me_ref[0], d) * features
        for s in range(splits):
            for part in range(3):
                to = pl.ds(pl.multiple_of(part * width + owner + s * wide, wide), wide)
                at = slice(part * wide, (part + 1) * wide)
                if d % 2 == 0:
                    mixed_ref[:, to] = same[s * groups + d // 2][0, :, at]
                else:
                    mixed_ref[:, to] = other[s][d // 2, :, at]
    back = nt(mixed_ref[...], w_ref[...])
    unit, rstd = norm_parts(tok_ref[...].astype(f32))
    out_ref[0] = ghid_ref[...] + norm_back(back, unit, rstd, gain_ref[...])


def tokens_call(me, tok, ghid, w_qkv, gain, same, other, count):
    local_rows, width = tok.shape
    columns = same[0].shape[2]
    groups, splits = count // 2, len(other)
    block = 256
    by_rows = lambda n: pl.BlockSpec((block, n), lambda i, m: (i, 0))
    return pl.pallas_call(
        functools.partial(tokens_kernel, groups, splits),
        grid_spec=pltpu.PrefetchScalarGridSpec(
            num_scalar_prefetch=1,
            grid=(pl.cdiv(local_rows, block),),
            in_specs=[
                by_rows(width),
                by_rows(width),
                pl.BlockSpec(w_qkv.shape, lambda i, m: (0, 0), pipeline_mode=pl.Buffered(1)),
                pl.BlockSpec(gain.shape, lambda i, m: (0, 0)),
            ]
            + [pl.BlockSpec((1, block, columns), lambda i, m: (0, i, 0))] * len(same)
            + [pl.BlockSpec((groups, block, columns), lambda i, m: (0, i, 0))] * splits,
            out_specs=pl.BlockSpec((1, block, width), lambda i, m: (0, i, 0)),
            scratch_shapes=[pltpu.VMEM((block, 3 * width), bf16)],
        ),
        out_shape=jax.ShapeDtypeStruct((1, local_rows, width), f32),
        compiler_params=params(),
        cost_estimate=pl.CostEstimate(flops=1 << 34, bytes_accessed=1 << 10, transcendentals=0),
    )(me, tok, ghid, w_qkv, gain, *same, *other)


def flip(index, bit):
    return index + bit - 2 * bit * ((index // bit) % 2)


def vectors_kernel(count, row_bits, img_bits, vec_ref, slot_ref, out_ref, sum_ref, *scratch):
    recv, slot_recv, send_sem, recv_sem, slot_send, slot_got = scratch
    row, img = lax.axis_index("row"), lax.axis_index("img")

    def partner(row_mask, img_mask=0):
        r, g = row, img
        for bit in row_bits:
            r = flip(r, bit) if row_mask & bit else r
        for bit in img_bits:
            g = flip(g, bit) if img_mask & bit else g
        return (g, r)

    steps = [(bit, 0) for bit in row_bits] + [(0, bit) for bit in img_bits]
    everyone = sorted(set(steps) | {(d, 0) for d in range(1, count)})
    barrier = pltpu.get_barrier_semaphore()
    for masks in everyone:
        pl.semaphore_signal(
            barrier, inc=1, device_id=partner(*masks), device_id_type=pl.DeviceIdType.MESH
        )
    pl.semaphore_wait(barrier, len(everyone))
    slots = []
    for d in range(1, count):
        copy = pltpu.make_async_remote_copy(
            src_ref=slot_ref.at[d],
            dst_ref=slot_recv.at[d - 1],
            send_sem=slot_send.at[d - 1],
            recv_sem=slot_got.at[d - 1],
            device_id=partner(d),
            device_id_type=pl.DeviceIdType.MESH,
        )
        copy.start()
        slots.append(copy)
    out_ref[...] = vec_ref[...]
    for i, masks in enumerate(steps):
        copy = pltpu.make_async_remote_copy(
            src_ref=out_ref,
            dst_ref=recv.at[i],
            send_sem=send_sem.at[i],
            recv_sem=recv_sem.at[i],
            device_id=partner(*masks),
            device_id_type=pl.DeviceIdType.MESH,
        )
        copy.start()
        copy.wait()
        out_ref[...] = out_ref[...] + recv[i]
    for copy in slots:
        copy.wait()
    sum_ref[...] = tree(
        [slot_ref[0].astype(f32)] + [slot_recv[d - 1].astype(f32) for d in range(1, count)]
    )


def vectors_call(vec, slots):
    count = lax.axis_size("row")
    row_bits, img_bits = bits_of(count), bits_of(lax.axis_size("img"))
    steps = len(row_bits) + len(img_bits)
    whole = pl.BlockSpec(memory_space=pltpu.VMEM)
    return pl.pallas_call(
        functools.partial(vectors_kernel, count, row_bits, img_bits),
        in_specs=[whole, whole],
        out_specs=[whole, whole],
        out_shape=[
            jax.ShapeDtypeStruct(vec.shape, f32),
            jax.ShapeDtypeStruct(slots.shape[1:], f32),
        ],
        scratch_shapes=[
            pltpu.VMEM((steps,) + vec.shape, f32),
            pltpu.VMEM((count - 1,) + slots.shape[1:], bf16),
            pltpu.SemaphoreType.DMA((steps,)),
            pltpu.SemaphoreType.DMA((steps,)),
            pltpu.SemaphoreType.DMA((count - 1,)),
            pltpu.SemaphoreType.DMA((count - 1,)),
        ],
        compiler_params=pltpu.CompilerParams(
            collective_id=0, has_side_effects=True, vmem_limit_bytes=32 << 20
        ),
        cost_estimate=pl.CostEstimate(flops=1 << 34, bytes_accessed=1 << 10, transcendentals=0),
    )(vec, slots)


def rows_of(array, index, length):
    return lax.dynamic_slice_in_dim(array, index * length, length, 0)


def on_device(
    tokens,
    counts,
    owner,
    w_qkv,
    qv_bias,
    w_out,
    out_bias,
    w_up,
    up_bias,
    w_down,
    down_bias,
    norm_gain,
    norm_bias,
    learn_in,
    learn_in_bias,
    learn_out,
    learn_out_bias,
    cotangent,
):
    width = tokens.shape[2]
    local_rows = tokens.shape[1]
    row_count = lax.axis_size("row")
    images_count = lax.axis_size("img")
    device = lax.axis_index("row")
    image_device = lax.axis_index("img")
    features = width // row_count
    wide = min(features, 128)
    splits = features // wide
    slots_here = IMGS // row_count
    group_counts = counts[0]
    partners = [device ^ d for d in range(row_count)]
    row_bits, img_bits = stages()
    n_img = len(img_bits)

    piece_rows = BLK // row_count
    blocks = pl.cdiv(local_rows, piece_rows)
    images = jnp.stack([row_images(group_counts, p, local_rows, row_count) for p in partners])
    extra = blocks * piece_rows - local_rows
    images = jnp.pad(images, ((0, 0), (0, extra)), constant_values=IMGS + 1)
    image_here = images[0].reshape(-1, 1)
    images = images.reshape(row_count, blocks, piece_rows).transpose(1, 0, 2).reshape(blocks, BLK)
    least, most = jnp.min(images, axis=1), jnp.max(images, axis=1)
    lo = jnp.sum((most[None, :] < least[:, None]).astype(jnp.int32), axis=1)
    hi = jnp.sum((least[None, :] <= most[:, None]).astype(jnp.int32), axis=1)
    imgq, imgk = images.reshape(1, -1), images.reshape(-1, 1)

    me = device.reshape(1)
    w_out_here = jnp.concatenate([rows_of(w_out, p, features) for p in partners], axis=0)
    bias_here = lax.dynamic_slice_in_dim(qv_bias, device * features, features, 1)
    half_count = row_count // 2
    first_norm = (w_qkv, bias_here, norm_gain[0:1], norm_bias[0:1], splits)
    far_tokens = jump(tokens[0], half_count)
    pieces = gather_pieces(tokens[0], half_count)
    filled = qkv_call(me, pieces, 0, *first_norm)
    tables = (imgq, imgk, lo, hi, image_here, w_out_here)
    far_tokens, filled, tables = lax.optimization_barrier((far_tokens, filled, tables))
    imgq, imgk, lo, hi, image_here, w_out_here = tables
    pieces = gather_pieces(far_tokens, half_count)
    unit, q, k, v, kt, vt = qkv_call(me, pieces, 1, *first_norm, filled)
    q, k, v = (a.reshape(-1, features) for a in (q, k, v))
    slot_grads = behind(cotangent[0].reshape(slots_here, LT * width).astype(bf16), [lo, unit])
    grads_in = gather_pieces(slot_grads, row_count)
    *upper, ot, lse = attend_call(q, k, vt, imgq, imgk, lo, hi, row_count, 0)
    upper = send_pieces(upper)
    *lower, ot, lse = attend_call(q, k, vt, imgq, imgk, lo, hi, row_count, 1, (ot, lse))
    upper[1:], ot, lse, lower = lax.optimization_barrier((upper[1:], ot, lse, lower))
    attended = upper + send_pieces(lower)

    slot_rel = ((owner[0] // slots_here) ^ device) * slots_here + owner[0] % slots_here
    select = (slot_rel[:, None] == jnp.arange(IMGS, dtype=jnp.int32)[None, :]).astype(f32)
    scale = lax.rsqrt(group_counts.astype(f32))
    incoming = jnp.concatenate(grads_in, axis=0).astype(f32)
    grad_pooled = jnp.dot(select, incoming, precision=highest) * scale[:, None]
    grad_pooled_low = grad_pooled.reshape(IMGS * LT, width).astype(bf16)

    vecs = jnp.concatenate(
        [
            out_bias[None],
            down_bias[None],
            norm_gain[1:2],
            norm_bias[1:2],
            norm_gain[2:3],
            norm_bias[2:3],
            learn_in_bias[None],
            jnp.zeros((1, width), f32),
        ],
        axis=0,
    )
    out = rows_call(
        tokens[0],
        image_here,
        attended,
        w_out_here,
        w_up,
        w_down,
        learn_in,
        jnp.tile(learn_out, (1, IMGS)),
        vecs,
        up_bias[None],
        jnp.tile(learn_out_bias, IMGS)[None],
        grad_pooled_low,
        splits,
    )
    n2, gated, gup, gres, n3, glearn, inner, glogit, ghid, grad_hidden = out[:10]
    grad_attended = out[10 : 10 + row_count * splits]
    pooled, vec_sums, up_sums, logit_sums = out[10 + row_count * splits :]
    grad_attended = [send_pieces(grad_attended[s::splits]) for s in range(splits)]

    core, far_row = row_bits[:1], row_bits[1:]
    y_bits, z_bits = img_bits[:1], [[bit] for bit in img_bits[1:]]
    half = lambda value, bits: Halving(value, bits, n_img)

    def core_flight(keep, send):
        flight = Exchange(keep, [])
        flight.moved = [jump(send, 1)]
        return flight

    keep_small, send_small, grad_learn_out = small_grad_call(
        me, n3, glearn, ghid, inner, glogit, attended
    )
    keep_down, send_down = down_grad_call(me, gated, gres, [send_small])
    keep_up, send_up = up_grad_call(me, n2, gup, [send_down])
    small, down = arrive(
        [core_flight(keep_small, send_small), core_flight(keep_down, send_down)], [send_up]
    )
    small, down = spread_img(small), spread_img(down)

    def back_call(s, after):
        *parts, sums = attend_back_call(
            grad_attended[s], q, k, v, kt, ot, lse, imgq, imgk, lo, hi, s, after
        )
        return parts, sums

    def grad_qkv_call(s, parts, after):
        turned = [norm_gain[0].reshape(-1, 1), norm_bias[0].reshape(-1, 1)]
        return qkv_grad_call(me, unit, parts, w_qkv, *turned, s, splits, after)

    groups = row_count // 2
    far_masks = [(2 * g, 0) for g in range(1, groups)]
    same, qkv_sums, norm_sums, grad_qkv = [], [], [], []
    after, far = [small, down, send_up], None
    for s in range(splits):
        parts, sums = back_call(s, after)
        qkv_sums.append(sums[0:2])
        if s == 0:
            small, down, ups = arrive(
                [half(small, y_bits), half(down, z_bits[0]), core_flight(keep_up, send_up)], [sums]
            )
            ups = spread_img(ups)
        if s == splits - 1:
            flights = [half(ups, y_bits), half(down, z_bits[1]), half(small, z_bits[0])]
            if far is not None:
                flights.append(far)
            ups, down, small, *arrived = arrive(flights, [sums])
            for pieces_far in arrived:
                same += pieces_far
        same.append(parts[0])
        far = Moved(parts[1:], far_masks)
        grad, norm_sum = grad_qkv_call(s, parts, [ups, down])
        if s == splits - 1:
            (ups, arrived, down, small), (grad, norm_sum) = arrive_with(
                [half(ups, z_bits[0]), far, half(down, y_bits), half(small, z_bits[1])],
                (grad, norm_sum),
            )
            same += arrived
        norm_sums.append(norm_sum)
        grad_qkv.append(spread_img(grad))
        after = [grad]
    grad_qkv = jnp.concatenate(grad_qkv, axis=-1)
    near = Moved([jnp.stack([p[1] for p in same])], [(1, 0)])

    by_slot = jnp.dot(select.T, pooled.reshape(IMGS, LT * width), precision=highest)
    by_slot = by_slot.astype(bf16).reshape(row_count, -1, 128)
    late = lax.dynamic_update_slice(
        jnp.zeros((2, width), f32), jnp.concatenate(qkv_sums, axis=1), (0, device * features)
    )
    vectors = jnp.concatenate(
        [
            up_sums.reshape(-1),
            vec_sums.reshape(-1),
            jnp.sum(grad_learn_out.reshape(-1, IMGS, LT), axis=1).reshape(-1),
            late.reshape(-1),
            sum(norm_sums).T.reshape(-1),
            jnp.sum(logit_sums.reshape(IMGS, LT), axis=0),
        ]
    )
    vectors = jnp.pad(vectors, (0, -vectors.shape[0] % 1024)).reshape(-1, 128)
    made = vectors_call(vectors, by_slot)

    for bits in z_bits[2:]:
        down, small = arrive([half(down, bits), half(small, bits)])
    ((others,), grad_qkv, ups, down, small), (vectors, learned) = arrive_with(
        [
            near,
            half(grad_qkv, y_bits),
            half(ups, z_bits[1]),
            half(down, far_row),
            Exchange(small, far_row),
        ],
        tuple(made),
    )
    for bits in z_bits[2:]:
        ups, grad_qkv = arrive([half(ups, bits), half(grad_qkv, bits)])
    other = [others[s * groups : (s + 1) * groups] for s in range(splits)]
    grad_tokens = tokens_call(
        me,
        tokens[0],
        behind(grad_hidden, [ups, grad_qkv, down, small]),
        w_qkv,
        norm_gain[0:1],
        same,
        other,
        row_count,
    )
    (grad_qkv, ups), grad_tokens = arrive_with(
        [half(grad_qkv, z_bits[0]), Exchange(ups, far_row)], grad_tokens
    )
    (grad_qkv,) = arrive([half(grad_qkv, z_bits[1])])
    vectors, learned = behind((vectors, learned), [grad_tokens])
    vectors = vectors.reshape(-1)
    scale_here = jnp.dot(scale, select, precision=highest)[:slots_here]
    learned = learned.reshape(slots_here, LT * width) * scale_here[:, None]
    learned = learned.reshape(1, slots_here, LT, width)

    share_down = finish_weight(down, row_bits)
    share_small = finish_weight(small, core, [grad_tokens])
    share_up = finish_weight(ups, core)
    share_learn = share_small[:, : learn_in.shape[1]]
    share_out = share_small[:, learn_in.shape[1] :]
    shares = gather_columns(grad_qkv.reshape(grad_qkv.shape[-2:]), lambda c: c, row_bits)
    share_qkv = jnp.concatenate(
        [
            shares[c][:, (3 * s + part) * wide : (3 * s + part + 1) * wide]
            for part in range(3)
            for c in range(row_count)
            for s in range(splits)
        ],
        axis=1,
    ).astype(f32)

    at = up_bias.shape[0]
    up_sum, vec_sums = vectors[:at], vectors[at : at + 8 * width].reshape(8, width)
    at += 8 * width
    learn_out_sum = vectors[at : at + learn_out.size].reshape(learn_out.shape)
    at += learn_out.size
    late = vectors[at : at + 4 * width].reshape(4, width)
    at += 4 * width
    out_sum, down_sum, gain_two, shift_two, gain_three, shift_three, learn_in_sum = vec_sums[:7]
    share_learn_out = rows_of(learn_out_sum, image_device, learn_out.shape[0] // images_count)
    return (
        learned,
        grad_tokens,
        share_qkv,
        late[0:2],
        share_out,
        out_sum,
        share_up,
        up_sum,
        share_down,
        down_sum,
        jnp.stack([late[2], gain_two, gain_three]),
        jnp.stack([late[3], shift_two, shift_three]),
        share_learn,
        learn_in_sum,
        share_learn_out,
        vectors[at : at + learn_out.shape[1]],
    )


def solution(mesh):
    by_image = P("img", None)
    in_specs = (
        (P("img", "row", None), by_image, by_image) + (P(),) * 14 + (P("img", "row", None, None),)
    )
    out_specs = (
        P("img", "row", None, None),
        P("img", "row", None),
        by_image,
        P(),
        by_image,
        P(),
        by_image,
        P(),
        by_image,
        P(),
        P(),
        P(),
        by_image,
        P(),
        by_image,
        P(),
    )
    return jax.shard_map(
        on_device, mesh=mesh, in_specs=in_specs, out_specs=out_specs, check_vma=False
    )
```

```python
import functools

import jax
import jax.numpy as jnp
from jax import lax
from jax.experimental import pallas as pl
from jax.experimental.pallas import tpu as pltpu
from jax.sharding import PartitionSpec as P

HEADS = 16
HEAD = 64
LT = 8
IMGS = 8
BLK = 256
NEG = -1e30
VMEM = 60 << 20
ROW_BLOCK = 256
UP_BLOCK = 1024
GRAD_BLOCK = 1024

highest = lax.Precision.HIGHEST
epsilon = 1e-06
f32 = jnp.float32
bf16 = jnp.bfloat16


def smooth_both(v):
    half = jnp.abs(v) * 0.7071067811865476
    t = 1.0 / (1.0 + 0.3275911 * half)
    bell = jnp.exp(-half * half)
    poly = t * (
        0.127414796
        + t * (-0.142248368 + t * (0.7107068705 + t * (-0.7265760135 + t * 0.5307027145)))
    )
    tail = poly * bell
    cdf = jnp.where(v >= 0.0, 1.0 - tail, tail)
    return v * cdf, cdf + v * (bell * 0.3989422804014327)


def matmul(left, right):
    return jnp.dot(left, right, preferred_element_type=f32)


def nt(left, right):
    return lax.dot_general(left, right, (((1,), (1,)), ((), ())), preferred_element_type=f32)


def tn(left, right):
    return lax.dot_general(left, right, (((0,), (0,)), ((), ())), preferred_element_type=f32)


def row_images(counts, device, local_rows, row_count):
    upper_end = counts * (device + 1) // row_count
    lower_end = counts * device // row_count
    run_ends = jnp.cumsum(upper_end - lower_end)
    positions = jnp.arange(local_rows, dtype=jnp.int32)
    return jnp.sum((positions[:, None] >= run_ends[None, :]).astype(jnp.int32), axis=1)


def bits_of(size):
    return [1 << i for i in range(size.bit_length() - 1)]


def jump(value, row_mask, img_mask=0):
    rows, imgs = lax.axis_size("row"), lax.axis_size("img")
    if img_mask == 0:
        return lax.ppermute(value, "row", [(i, i ^ row_mask) for i in range(rows)])
    if row_mask == 0:
        return lax.ppermute(value, "img", [(i, i ^ img_mask) for i in range(imgs)])
    mask = img_mask * rows + row_mask
    return lax.ppermute(value, ("img", "row"), [(i, i ^ mask) for i in range(rows * imgs)])


def masks_of(bits):
    masks = []
    for e in range(1 << len(bits)):
        masks.append(
            tuple(
                sum(bit for j, (axis, bit) in enumerate(bits) if axis == name and e >> j & 1)
                for name in ("row", "img")
            )
        )
    return masks


def gather_pieces(value, count):
    pieces = {0: value}
    order = sorted(range(1, count), key=lambda d: (d & 1, d))
    for d in order:
        low = d & -d
        pieces[d] = jump(pieces[d ^ low], low)
    return [pieces[d] for d in range(count)]


def send_pieces(pieces):
    far_first = sorted(range(1, len(pieces)), reverse=True)
    arrived = {d: jump(pieces[d], d) for d in far_first}
    return [pieces[0]] + [arrived[d] for d in range(1, len(pieces))]


def stages():
    row_bits = [("row", b) for b in bits_of(lax.axis_size("row"))]
    img_bits = [("img", b) for b in bits_of(lax.axis_size("img"))]
    return row_bits, img_bits


def tree(values):
    while len(values) > 1:
        values = [values[i] + values[i + 1] for i in range(0, len(values), 2)]
    return values[0]


def behind(value, after):
    return lax.optimization_barrier((value, tuple(after)))[0] if after else value


class Halving:
    def __init__(self, value, bits, img_count):
        mine = {"row": lax.axis_index("row"), "img": lax.axis_index("img")}

        def part(e):
            piece = value
            for j, (axis, bit) in enumerate(bits):
                want = (mine[axis] // bit) % 2 ^ (e >> j & 1)
                dim = value.ndim - 1 if axis == "row" else img_count - bit.bit_length()
                length = piece.shape[dim] // 2
                piece = lax.dynamic_slice_in_dim(piece, want * length, length, dim)
            return piece

        masks = masks_of(bits)
        self.kept = part(0)
        self.moved = [jump(part(e), *masks[e]) for e in range(1, len(masks))]

    def finish(self):
        values = [self.kept, *self.moved]
        return tree([v.astype(f32) for v in values]).astype(bf16)


class Exchange(Halving):
    def __init__(self, value, bits):
        self.kept = value
        self.moved = [jump(value, *mask) for mask in masks_of(bits)[1:]]


class Moved(Halving):
    def __init__(self, values, masks):
        self.moved = [jump(v, *mask) for v, mask in zip(values, masks)]

    def finish(self):
        return self.moved


def arrive(flights, after=()):
    return arrive_with(flights, tuple(after))[0]


def arrive_with(flights, beside):
    flat = [m for flight in flights for m in flight.moved]
    flat, beside = lax.optimization_barrier((flat, beside))
    for flight in flights:
        flight.moved, flat = flat[: len(flight.moved)], flat[len(flight.moved) :]
    return [flight.finish() for flight in flights], beside


def spread_img(grad):
    rows, columns = grad.shape
    images = lax.axis_size("img")
    return grad.reshape((2,) * len(bits_of(images)) + (rows // images, columns))


def gather_columns(value, order, bits, after=()):
    masks = [row_mask for row_mask, _ in masks_of(bits)]
    device = lax.axis_index("row") % len(masks)
    stack = jnp.stack([value if m == 0 else behind(jump(value, m), after) for m in masks])
    return [
        lax.dynamic_index_in_dim(stack, order(c) ^ device, 0, False) for c in range(len(masks))
    ]


def reversed_bits(index, size):
    width = size.bit_length() - 1
    return int(format(index, f"0{width}b")[::-1], 2) if width else 0


def finish_weight(value, bits, after=()):
    value = value.reshape(value.shape[-2:])
    count = 1 << len(bits)
    blocks = gather_columns(value, lambda c: reversed_bits(c, count), bits, after)
    return jnp.concatenate(blocks, axis=1).astype(f32)


def params(flags=("arbitrary",)):
    return pltpu.CompilerParams(dimension_semantics=flags, vmem_limit_bytes=VMEM)


ANYWHERE = pl.BlockSpec(memory_space=pl.ANY)


def own_columns(w_qkv, features, splits, chosen):
    width = w_qkv.shape[0]
    wide = features // splits

    def spec(s, part):
        def index(b, me):
            return 0, part * (width // wide) + me[0] * splits + s

        return pl.BlockSpec((width, wide), index, pipeline_mode=pl.Buffered(1))

    return [spec(s, part) for s in chosen for part in range(3)], [w_qkv] * (3 * len(chosen))


def valid_rows(block, piece_rows, local_rows):
    position = lax.broadcasted_iota(jnp.int32, (BLK, 1), 0) % piece_rows + block * piece_rows
    return position < local_rows


def load_block(refs, block, piece_rows, local_rows):
    value = jnp.concatenate([ref[...] for ref in refs], axis=0).astype(f32)
    return jnp.where(valid_rows(block, piece_rows, local_rows), value, 0.0)


def norm_parts(value):
    centre = value - jnp.mean(value, axis=-1, keepdims=True)
    rstd = lax.rsqrt(jnp.mean(centre * centre, axis=-1, keepdims=True) + epsilon)
    return centre * rstd, rstd


def qkv_kernel(count, splits, local_rows, features, held, me_ref, *refs):
    n_w = 3 * splits
    pieces, columns = refs[:count], refs[count : count + n_w]
    bias_ref, gain_ref, shift_ref = refs[count + n_w : count + n_w + 3]
    n_ref, q_ref, k_ref, v_ref, kt_ref, vt_ref, w_ref = refs[count + n_w + 3 + held :]
    step = pl.program_id(0)
    wide = features // splits
    half = BLK // 2
    rows = half // count

    @pl.when(step == 0)
    def _():
        for i, ref in enumerate(columns):
            w_ref[:, i * wide : (i + 1) * wide] = ref[...]

    places = [(b, d) for b in range(2) for d in range(count)]
    value = jnp.concatenate(
        [pieces[d][b * rows : (b + 1) * rows, :] for b, d in places], axis=0
    ).astype(f32)
    row = lax.broadcasted_iota(jnp.int32, (BLK, 1), 0)
    position = (2 * step + row // half) * rows + row % rows
    unit, _ = norm_parts(jnp.where(position < local_rows, value, 0.0))
    normed = (unit * gain_ref[...] + shift_ref[...]).astype(bf16)
    low = unit.astype(bf16)
    for i, (b, d) in enumerate(places):
        n_ref[d, b * rows : (b + 1) * rows, :] = low[i * rows : (i + 1) * rows]
    mixed = matmul(normed, w_ref[...])
    for s in range(splits):
        at = slice(s * wide, (s + 1) * wide)
        part = mixed[:, 3 * s * wide : 3 * (s + 1) * wide]
        queries = ((part[:, :wide] + bias_ref[0:1, at]) * 0.125).astype(bf16)
        keys = part[:, wide : 2 * wide]
        values = part[:, 2 * wide :] + bias_ref[1:2, at]
        keys_low, values_low = keys.astype(bf16), values.astype(bf16)
        keys_turned, values_turned = keys.T.astype(bf16), values.T.astype(bf16)
        for b in range(2):
            here = slice(b * half, (b + 1) * half)
            q_ref[b, 0, :, at] = queries[here]
            k_ref[b, 0, :, at] = keys_low[here]
            v_ref[b, 0, :, at] = values_low[here]
            kt_ref[b, at, :] = keys_turned[:, here]
            vt_ref[b, at, :] = values_turned[:, here]


def qkv_call(me, pieces, part, w_qkv, bias, gain, shift, splits, held=()):
    count, (local_rows, width) = len(pieces), pieces[0].shape
    features = width // (2 * count)
    rows = BLK // 2 // count
    blocks = pl.cdiv(local_rows, rows)
    whole = lambda a: pl.BlockSpec(a.shape, lambda b, m: (0,) * a.ndim)
    flat = pl.BlockSpec((2, 1, BLK // 2, features), lambda b, m: (b, part, 0, 0))
    turned = pl.BlockSpec((2, features, BLK // 2), lambda b, m: (b, 0, part))
    specs, operands = own_columns(w_qkv, features, splits, range(splits))
    at = 1 + count + 3 * splits + 3
    return pl.pallas_call(
        functools.partial(qkv_kernel, count, splits, local_rows, features, len(held)),
        grid_spec=pltpu.PrefetchScalarGridSpec(
            num_scalar_prefetch=1,
            grid=(blocks // 2,),
            in_specs=[pl.BlockSpec((2 * rows, width), lambda b, m: (b, 0))] * count
            + specs
            + [whole(bias), whole(gain), whole(shift)]
            + [ANYWHERE] * len(held),
            out_specs=[
                pl.BlockSpec((count, 2 * rows, width), lambda b, m: (part, b, 0)),
                flat,
                flat,
                flat,
                turned,
                turned,
            ],
            scratch_shapes=[pltpu.VMEM((width, 3 * features), bf16)],
        ),
        out_shape=[jax.ShapeDtypeStruct((2 * count, blocks * rows, width), bf16)]
        + [jax.ShapeDtypeStruct((blocks, 2, BLK // 2, features), bf16)] * 3
        + [jax.ShapeDtypeStruct((blocks, features, BLK), bf16)] * 2,
        input_output_aliases={at + i: i for i in range(len(held))},
        compiler_params=params(),
        cost_estimate=pl.CostEstimate(
            flops=6 * blocks * BLK * width * 3 * features,
            bytes_accessed=blocks * BLK * (2 * width + 5 * features),
            transcendentals=0,
        ),
    )(me, *pieces, *operands, bias, gain, shift, *held)


def per_head(stack_ref, value, heads):
    lane = lax.broadcasted_iota(jnp.int32, value.shape, 1) // HEAD
    for h in range(heads):
        stack_ref[h * BLK : (h + 1) * BLK] = jnp.where(lane == h, value, jnp.zeros_like(value))


def in_pairs(lo, hi, step, carry):
    pairs = (hi - lo) // 2
    carry = lax.fori_loop(0, pairs, lambda i, c: step(lo + 2 * i, 2, c), carry)
    return lax.fori_loop(lo + 2 * pairs, hi, lambda kb, c: step(kb, 1, c), carry)


def attend_kernel(count, heads, start, held, lo_ref, hi_ref, *refs):
    q_ref, k_ref, vt_ref, imgq_ref, imgk_ref = refs[:5]
    refs = refs[5 + held :]
    outs, (ot_ref, lse_ref), (s_ref, qs_ref, acc_ref) = refs[:count], refs[count : count + 2], refs[count + 2 :]
    block = pl.program_id(0) + start
    lo, hi = lo_ref[block], hi_ref[block]
    per_head(qs_ref, q_ref[...], heads)
    imgq = imgq_ref[...]

    def first(kb, width, tops):
        rows = pl.ds(pl.multiple_of(kb * BLK, BLK), width * BLK)
        allowed = imgk_ref[rows, :] == imgq
        s = nt(k_ref[rows, :], qs_ref[...])
        new = []
        for h in range(heads):
            cols = slice(h * BLK, (h + 1) * BLK)
            part = jnp.where(allowed, s[:, cols], NEG)
            for j in range(width):
                s_ref[kb - lo + j, :, cols] = part[j * BLK : (j + 1) * BLK]
            high = jnp.max(part.reshape(width * BLK // 8, 8, BLK), axis=0)
            new.append(jnp.maximum(tops[h], high))
        return tuple(new)

    tops = in_pairs(lo, hi, first, (jnp.full((8, BLK), NEG, f32),) * heads)
    tops = [jnp.max(t, axis=0, keepdims=True) for t in tops]
    acc_ref[...] = jnp.zeros_like(acc_ref)

    def second(kb, width, sums):
        new = []
        for h in range(heads):
            rows, cols = slice(h * HEAD, (h + 1) * HEAD), slice(h * BLK, (h + 1) * BLK)
            part, weights = 0.0, sums[h]
            for j in range(width):
                p = jnp.exp(s_ref[kb - lo + j, :, cols] - tops[h])
                weights = weights + jnp.sum(p.reshape(BLK // 8, 8, BLK), axis=0)
                part = part + matmul(vt_ref[kb + j, rows, :], p.astype(bf16))
            new.append(weights)
            acc_ref[rows, :] += part
        return tuple(new)

    sums = in_pairs(lo, hi, second, (jnp.zeros((8, BLK), f32),) * heads)
    sums = [jnp.sum(t, axis=0, keepdims=True) for t in sums]
    for h in range(heads):
        rows = slice(h * HEAD, (h + 1) * HEAD)
        acc_ref[rows, :] = acc_ref[rows, :] / sums[h]
    lse_ref[...] = jnp.concatenate(
        [t + jnp.log(s) for t, s in zip(tops, sums)] + [jnp.zeros((8 - heads, BLK), f32)], axis=0
    )
    ot_ref[0] = acc_ref[...]
    out = acc_ref[...].T.astype(bf16)
    for d in range(count):
        outs[d][...] = out[d * (BLK // count) : (d + 1) * (BLK // count)]


def attend_call(q, k, vt, imgq, imgk, lo, hi, count, part, held=()):
    blocks, features = vt.shape[0], q.shape[1]
    heads = features // HEAD
    piece_rows = BLK // count
    steps = blocks // 2
    start = part * steps
    whole = lambda a: pl.BlockSpec(
        a.shape, lambda b, *_: (0,) * a.ndim, pipeline_mode=pl.Buffered(1)
    )
    return pl.pallas_call(
        functools.partial(attend_kernel, count, heads, start, len(held)),
        grid_spec=pltpu.PrefetchScalarGridSpec(
            num_scalar_prefetch=2,
            grid=(steps,),
            in_specs=[
                pl.BlockSpec((BLK, features), lambda b, *_: (b + start, 0)),
                whole(k),
                whole(vt),
                pl.BlockSpec((1, BLK), lambda b, *_: (0, b + start)),
                whole(imgk),
            ]
            + [ANYWHERE] * len(held),
            out_specs=[pl.BlockSpec((piece_rows, features), lambda b, *_: (b, 0))] * count
            + [
                pl.BlockSpec((1, features, BLK), lambda b, *_: (b + start, 0, 0)),
                pl.BlockSpec((8, BLK), lambda b, *_: (0, b + start)),
            ],
            scratch_shapes=[
                pltpu.VMEM((blocks, BLK, heads * BLK), f32),
                pltpu.VMEM((heads * BLK, features), bf16),
                pltpu.VMEM((features, BLK), f32),
            ],
        ),
        out_shape=[jax.ShapeDtypeStruct((steps * piece_rows, features), bf16)] * count
        + [
            jax.ShapeDtypeStruct((blocks, features, BLK), f32),
            jax.ShapeDtypeStruct((8, blocks * BLK), f32),
        ],
        input_output_aliases={7 + i: count + i for i in range(len(held))},
        compiler_params=params(),
        cost_estimate=pl.CostEstimate(
            flops=5 * (blocks * BLK) ** 2 * features,
            bytes_accessed=2 * blocks * BLK * features * 6,
            transcendentals=0,
        ),
    )(lo, hi, q, k, vt, imgq, imgk, *held)


def attend_back_kernel(count, heads, first, waits, lo_ref, hi_ref, *refs):
    pieces, refs = refs[:count], refs[:count] + refs[count + waits :]
    q_ref, k_ref, v_ref, kt_ref, ot_ref, lse_ref, imgq_ref, imgk_ref = refs[count : count + 8]
    groups = count // 2
    outs, sums_ref = refs[count + 8 : count + groups + 8], refs[count + groups + 8]
    qs_ref, dos_ref, p_ref, ds_ref, dqt_ref, dk_ref, dv_ref = refs[count + groups + 9 :]
    block = pl.program_id(0)
    lo, hi = lo_ref[block], hi_ref[block]
    piece_rows = BLK // count
    wide = heads * HEAD

    @pl.when(block == 0)
    def _():
        dk_ref[...] = jnp.zeros_like(dk_ref)
        dv_ref[...] = jnp.zeros_like(dv_ref)
        sums_ref[...] = jnp.zeros_like(sums_ref)

    grad = jnp.concatenate([ref[...] for ref in pieces], axis=0)
    query = q_ref[...]
    lane = lax.broadcasted_iota(jnp.int32, grad.shape, 1) // HEAD
    for h in range(heads):
        dos_ref[h * BLK : (h + 1) * BLK] = jnp.where(lane == h, grad, jnp.zeros_like(grad))
        qs_ref[h * BLK : (h + 1) * BLK] = jnp.where(lane == h, query, jnp.zeros_like(query))
    both = grad.astype(f32).T * ot_ref[0]
    delta = [
        jnp.sum(both[h * HEAD : (h + 1) * HEAD], axis=0, keepdims=True) for h in range(heads)
    ]
    logsum = [lse_ref[first + h : first + h + 1, :] for h in range(heads)]
    imgq = imgq_ref[...]
    dqt_ref[...] = jnp.zeros_like(dqt_ref)

    def step(kb, width):
        length = width * BLK
        rows = pl.ds(pl.multiple_of(kb * BLK, BLK), length)
        keys, values = k_ref[rows, :], v_ref[rows, :]
        allowed = imgk_ref[rows, :] == imgq
        s = nt(keys, qs_ref[...])
        dp = nt(values, dos_ref[...])
        for h in range(heads):
            cols = slice(h * BLK, (h + 1) * BLK)
            p = jnp.exp(jnp.where(allowed, s[:, cols] - logsum[h], NEG))
            p_ref[:length, cols] = p.astype(bf16)
            ds_ref[:length, cols] = (p * (dp[:, cols] - delta[h])).astype(bf16)
        dv_ref[rows, :] += matmul(p_ref[:length], dos_ref[...])
        dk_ref[rows, :] += matmul(ds_ref[:length], qs_ref[...])
        for h in range(heads):
            cols, feats = slice(h * BLK, (h + 1) * BLK), slice(h * HEAD, (h + 1) * HEAD)
            total = 0.0
            for j in range(width):
                ds = ds_ref[j * BLK : (j + 1) * BLK, cols]
                total = total + matmul(kt_ref[kb + j, feats, :], ds)
            dqt_ref[feats, :] += total

    def pair(i, _):
        step(lo + 2 * i, 2)
        return 0

    lax.fori_loop(0, (hi - lo) // 2, pair, 0)

    @pl.when((hi - lo) % 2 == 1)
    def _():
        step(hi - 1, 1)

    dq = dqt_ref[...].T * 0.125
    sums_ref[0:1, :] += jnp.sum(dq, axis=0, keepdims=True)
    here = pl.ds(pl.multiple_of(block * piece_rows, piece_rows), piece_rows)
    for d in range(count):
        outs[d // 2][d % 2, here, :wide] = dq[d * piece_rows : (d + 1) * piece_rows].astype(bf16)

    @pl.when(block == pl.num_programs(0) - 1)
    def _():
        sums_ref[1:2, :] = jnp.sum(dv_ref[...], axis=0, keepdims=True)

        def move(b, _):
            to = pl.ds(pl.multiple_of(b * piece_rows, piece_rows), piece_rows)
            for d in range(count):
                at = pl.ds(pl.multiple_of(b * BLK + d * piece_rows, piece_rows), piece_rows)
                outs[d // 2][d % 2, to, wide : 2 * wide] = dk_ref[at, :].astype(bf16)
                outs[d // 2][d % 2, to, 2 * wide :] = dv_ref[at, :].astype(bf16)
            return 0

        lax.fori_loop(0, pl.num_programs(0), move, 0)


def attend_back_call(pieces, q, k, v, kt, ot, lse, imgq, imgk, lo, hi, split, after):
    count, (rows, wide) = len(pieces), pieces[0].shape
    blocks = kt.shape[0]
    heads = wide // HEAD
    once = pl.Buffered(1)
    half = pl.BlockSpec((blocks * BLK, wide), lambda b, *_: (0, split), pipeline_mode=once)
    out = jax.ShapeDtypeStruct((2, rows, 3 * wide), bf16)
    return pl.pallas_call(
        functools.partial(attend_back_kernel, count, heads, split * heads, len(after)),
        grid_spec=pltpu.PrefetchScalarGridSpec(
            num_scalar_prefetch=2,
            grid=(blocks,),
            in_specs=[pl.BlockSpec((BLK // count, wide), lambda b, *_: (b, 0))] * count
            + [ANYWHERE] * len(after)
            + [
                pl.BlockSpec((BLK, wide), lambda b, *_: (b, split)),
                half,
                half,
                pl.BlockSpec((blocks, wide, BLK), lambda b, *_: (0, split, 0), pipeline_mode=once),
                pl.BlockSpec((1, wide, BLK), lambda b, *_: (b, split, 0)),
                pl.BlockSpec((8, BLK), lambda b, *_: (0, b)),
                pl.BlockSpec((1, BLK), lambda b, *_: (0, b)),
                pl.BlockSpec(imgk.shape, lambda b, *_: (0, 0), pipeline_mode=once),
            ],
            out_specs=[pl.BlockSpec(out.shape, lambda b, *_: (0, 0, 0), pipeline_mode=once)] * (count // 2)
            + [pl.BlockSpec((8, wide), lambda b, *_: (0, 0))],
            scratch_shapes=[
                pltpu.VMEM((heads * BLK, wide), bf16),
                pltpu.VMEM((heads * BLK, wide), bf16),
                pltpu.VMEM((2 * BLK, heads * BLK), bf16),
                pltpu.VMEM((2 * BLK, heads * BLK), bf16),
                pltpu.VMEM((wide, BLK), f32),
                pltpu.VMEM((blocks * BLK, wide), f32),
                pltpu.VMEM((blocks * BLK, wide), f32),
            ],
        ),
        out_shape=[out] * (count // 2) + [jax.ShapeDtypeStruct((8, wide), f32)],
        compiler_params=params(),
        cost_estimate=pl.CostEstimate(
            flops=16 * (blocks * BLK) ** 2 * wide,
            bytes_accessed=2 * blocks * BLK * wide * 12,
            transcendentals=0,
        ),
    )(lo, hi, *pieces, *after, q, k, v, kt, ot, lse, imgq, imgk)


def norm_back(grad, unit, rstd, gain):
    e = grad * gain
    mean = jnp.mean(e, axis=-1, keepdims=True)
    return (e - mean - unit * jnp.mean(e * unit, axis=-1, keepdims=True)) * rstd


def total(value):
    return jnp.sum(value, axis=0, keepdims=True)


def rows_kernel(count, splits, local_rows, *refs):
    (
        tok_ref,
        img_ref,
        w_out_ref,
        w_up_far,
        w_down_far,
        learn_in_far,
        learn_out_ref,
        vec_ref,
        up_bias_ref,
        out_bias_ref,
        pooled_grad_ref,
    ) = refs[:11]
    upper, lower = refs[11 : 11 + count], refs[11 + count : 11 + 2 * count]
    at = 11 + 2 * count
    (
        n2_ref,
        gated_ref,
        gup_ref,
        gres_ref,
        n3_ref,
        glearn_ref,
        inner_ref,
        glogit_ref,
        ghid_ref,
        ghid_f32_ref,
    ) = refs[at : at + 10]
    gatt = refs[at + 10 : at + 10 + count * splits]
    at += 10 + count * splits
    pooled_ref, vsum_ref, usum_ref, lsum_ref = refs[at : at + 4]
    hid_ref, res_ref, dgate_ref, up0_ref, up1_ref = refs[at + 4 : at + 9]
    w_up_ref, w_down_ref, learn_in_ref, sems = refs[at + 9 :]
    step = pl.program_id(0)
    rows, width = tok_ref.shape
    hidden_units = w_up_ref.shape[1]
    chunk = up0_ref.shape[1]
    chunks = hidden_units // chunk
    copies = [
        pltpu.make_async_copy(w_up_far, w_up_ref, sems.at[0]),
        pltpu.make_async_copy(w_down_far, w_down_ref, sems.at[1]),
        pltpu.make_async_copy(learn_in_far, learn_in_ref, sems.at[2]),
    ]

    @pl.when(step == 0)
    def _():
        for copy in copies:
            copy.start()
        for ref in (pooled_ref, vsum_ref, usum_ref, lsum_ref):
            ref[...] = jnp.zeros_like(ref)

    def need(i):
        @pl.when(step == 0)
        def _():
            copies[i].wait()

    def vec(i):
        return vec_ref[i : i + 1, :]

    position = lax.broadcasted_iota(jnp.int32, (rows, 1), 0) + step * rows
    tok = jnp.where(position < local_rows, tok_ref[...].astype(f32), 0.0)
    early = step < pl.num_programs(0) // 2
    low = jnp.concatenate(
        [jnp.where(early, a[...], b[...]) for a, b in zip(upper, lower)], axis=1
    )
    hidden = tok + matmul(low, w_out_ref[...]) + vec(0)
    hid_ref[...] = hidden
    unit, _ = norm_parts(hidden)
    n2_ref[...] = (unit * vec(2) + vec(3)).astype(bf16)

    def columns(j):
        return pl.ds(pl.multiple_of(j * chunk, chunk), chunk)

    def up(ref, j):
        ref[...] = matmul(n2_ref[...], w_up_ref[:, columns(j)])

    def gate(ref, j):
        value, slope = smooth_both(ref[...] + up_bias_ref[:, columns(j)])
        gated_ref[:, columns(j)] = value.astype(bf16)
        dgate_ref[:, columns(j)] = slope

    need(0)
    up(up0_ref, 0)

    def pair(i, _):
        up(up1_ref, 2 * i + 1)
        gate(up0_ref, 2 * i)
        up(up0_ref, jnp.minimum(2 * i + 2, chunks - 1))
        gate(up1_ref, 2 * i + 1)
        return 0

    lax.fori_loop(0, chunks // 2, pair, 0)
    need(1)
    need(2)
    result = hid_ref[...] + matmul(gated_ref[...], w_down_ref[...]) + vec(1)
    res_ref[...] = result
    unit, rstd = norm_parts(result)
    n3_ref[...] = (unit * vec(4) + vec(5)).astype(bf16)
    inner, slope = smooth_both(matmul(n3_ref[...], learn_in_ref[...]) + vec(6))
    inner_ref[...] = inner.astype(bf16)
    maps = jax.nn.sigmoid(matmul(inner_ref[...], learn_out_ref[...]) + out_bias_ref[...])
    member = lax.broadcasted_iota(jnp.int32, maps.shape, 1) // LT == img_ref[...]
    spread = jnp.where(member, maps, 0.0).astype(bf16)
    result_low = res_ref[...].astype(bf16)
    pooled_ref[...] += tn(spread, result_low)
    grad_spread = nt(result_low, pooled_grad_ref[...])
    grad_logit = jnp.where(member, grad_spread * maps * (1.0 - maps), 0.0)
    lsum_ref[...] += total(grad_logit)
    glogit_ref[...] = grad_logit.astype(bf16)
    grad_pre = nt(glogit_ref[...], learn_out_ref[...]) * slope
    vsum_ref[6:7, :] += total(grad_pre)
    glearn_ref[...] = grad_pre.astype(bf16)
    back = nt(glearn_ref[...], learn_in_ref[...])
    unit, rstd = norm_parts(res_ref[...])
    vsum_ref[4:5, :] += total(back * unit)
    vsum_ref[5:6, :] += total(back)
    grad_result = matmul(spread, pooled_grad_ref[...]) + norm_back(back, unit, rstd, vec(4))
    vsum_ref[1:2, :] += total(grad_result)
    res_ref[...] = grad_result
    gres_ref[...] = grad_result.astype(bf16)

    def down_back(j, _):
        grad = nt(gres_ref[...], w_down_ref[columns(j), :]) * dgate_ref[:, columns(j)]
        usum_ref[:, columns(j)] += total(grad)
        gup_ref[:, columns(j)] = grad.astype(bf16)
        return 0

    lax.fori_loop(0, chunks, down_back, 0)
    back = nt(gup_ref[...], w_up_ref[...])
    unit, rstd = norm_parts(hid_ref[...])
    vsum_ref[2:3, :] += total(back * unit)
    vsum_ref[3:4, :] += total(back)
    grad_hidden = res_ref[...] + norm_back(back, unit, rstd, vec(2))
    vsum_ref[0:1, :] += total(grad_hidden)
    ghid_f32_ref[...] = grad_hidden
    ghid_ref[...] = grad_hidden.astype(bf16)
    grad = nt(ghid_ref[...], w_out_ref[...]).astype(bf16)
    wide = width // (count * splits)
    for i in range(count * splits):
        gatt[i][...] = grad[:, i * wide : (i + 1) * wide]


def rows_call(tok, img, attended, w_out, w_up, w_down, learn_in, learn_out, vecs, up_bias, out_bias, pooled_grad, splits):
    count, (rows, features) = len(attended) // 2, attended[0].shape
    rows *= 2
    local_rows, width = tok.shape
    hidden_units = w_up.shape[1]
    inner = learn_in.shape[1]
    spread = learn_out.shape[1]
    block = min(ROW_BLOCK, rows // 2)
    half = rows // block // 2
    chunk = UP_BLOCK
    wide = features // splits
    once = lambda a: pl.BlockSpec(a.shape, lambda i: (0,) * a.ndim, pipeline_mode=pl.Buffered(1))
    by_rows = lambda n: pl.BlockSpec((block, n), lambda i: (i, 0))
    kept = lambda a: pl.BlockSpec(a.shape, lambda i: (0, 0))
    low = lambda n: jax.ShapeDtypeStruct((rows, n), bf16)
    lows = [width, hidden_units, hidden_units, width, width, inner, inner, spread, width]
    sums = [
        jax.ShapeDtypeStruct((spread, width), f32),
        jax.ShapeDtypeStruct((8, width), f32),
        jax.ShapeDtypeStruct((1, hidden_units), f32),
        jax.ShapeDtypeStruct((1, spread), f32),
    ]
    resident = [w_out, w_up, w_down, learn_in, learn_out, vecs, up_bias, out_bias, pooled_grad]
    return pl.pallas_call(
        functools.partial(rows_kernel, count, splits, local_rows),
        grid=(rows // block,),
        in_specs=[by_rows(width), by_rows(1)]
        + [ANYWHERE if a.size >= width * inner and i else once(a) for i, a in enumerate(resident)]
        + [pl.BlockSpec((block, features), lambda i: (jnp.minimum(i, half - 1), 0))] * count
        + [pl.BlockSpec((block, features), lambda i: (jnp.maximum(i - half, 0), 0))] * count,
        out_specs=[by_rows(n) for n in lows]
        + [by_rows(width)]
        + [by_rows(wide)] * (count * splits)
        + [kept(a) for a in sums],
        out_shape=[low(n) for n in lows]
        + [jax.ShapeDtypeStruct((rows, width), f32)]
        + [low(wide)] * (count * splits)
        + sums,
        scratch_shapes=[
            pltpu.VMEM((block, width), f32),
            pltpu.VMEM((block, width), f32),
            pltpu.VMEM((block, hidden_units), f32),
            pltpu.VMEM((block, chunk), f32),
            pltpu.VMEM((block, chunk), f32),
            pltpu.VMEM(w_up.shape, bf16),
            pltpu.VMEM(w_down.shape, bf16),
            pltpu.VMEM(learn_in.shape, bf16),
            pltpu.SemaphoreType.DMA((3,)),
        ],
        compiler_params=params(),
        cost_estimate=pl.CostEstimate(
            flops=4 * rows * width * (width + 2 * hidden_units + inner),
            bytes_accessed=2 * (rows * 20 * width + 2 * width * hidden_units),
            transcendentals=0,
        ),
    )(tok, img, *resident, *attended)


def part_halves(me_ref, value, keep_ref, send_ref, whole_ref):
    half = value.shape[1] // 2
    core = me_ref[0] % 2
    whole_ref[...] = value
    keep_ref[...] = whole_ref[:, pl.ds(pl.multiple_of(core * half, half), half)]
    send_ref[...] = whole_ref[:, pl.ds(pl.multiple_of((1 - core) * half, half), half)]


def down_grad_kernel(waits, me_ref, left_ref, right_ref, *refs):
    part_halves(me_ref, tn(left_ref[...], right_ref[...]).astype(bf16), *refs[waits:])


def down_grad_call(me, left, right, after=()):
    rows, m = left.shape
    n = right.shape[1]
    out = pl.BlockSpec((GRAD_BLOCK, n // 2), lambda j, m: (j, 0))
    return pl.pallas_call(
        functools.partial(down_grad_kernel, len(after)),
        grid_spec=pltpu.PrefetchScalarGridSpec(
            num_scalar_prefetch=1,
            grid=(m // GRAD_BLOCK,),
            in_specs=[
                pl.BlockSpec((rows, GRAD_BLOCK), lambda j, m: (0, j)),
                pl.BlockSpec((rows, n), lambda j, m: (0, 0), pipeline_mode=pl.Buffered(1)),
            ]
            + [ANYWHERE] * len(after),
            out_specs=[out, out],
            scratch_shapes=[pltpu.VMEM((GRAD_BLOCK, n), bf16)],
        ),
        out_shape=[jax.ShapeDtypeStruct((m, n // 2), bf16)] * 2,
        compiler_params=params(),
        cost_estimate=pl.CostEstimate(
            flops=3 * rows * m * n, bytes_accessed=4 * m * n, transcendentals=0
        ),
    )(me, left, right, *after)


def up_grad_kernel(half, waits, me_ref, left_ref, right_ref, *refs):
    keep_ref, send_ref = refs[waits:]
    value = tn(left_ref[...], right_ref[...]).astype(bf16)

    @pl.when(pl.program_id(0) < half)
    def _():
        send_ref[...] = value

    @pl.when(pl.program_id(0) >= half)
    def _():
        keep_ref[...] = value


def up_grad_call(me, left, right, after=()):
    rows, m = left.shape
    n = right.shape[1]
    half = n // GRAD_BLOCK // 2

    def column(j, core):
        return jnp.where(j < half, (1 - core) * half + j, core * half + j - half)

    return pl.pallas_call(
        functools.partial(up_grad_kernel, half, len(after)),
        grid_spec=pltpu.PrefetchScalarGridSpec(
            num_scalar_prefetch=1,
            grid=(2 * half,),
            in_specs=[
                pl.BlockSpec((rows, m), lambda j, me: (0, 0), pipeline_mode=pl.Buffered(1)),
                pl.BlockSpec((rows, GRAD_BLOCK), lambda j, me: (0, column(j, me[0] % 2))),
            ]
            + [ANYWHERE] * len(after),
            out_specs=[
                pl.BlockSpec((m, GRAD_BLOCK), lambda j, me: (0, jnp.maximum(j - half, 0))),
                pl.BlockSpec((m, GRAD_BLOCK), lambda j, me: (0, jnp.minimum(j, half - 1))),
            ],
        ),
        out_shape=[jax.ShapeDtypeStruct((m, n // 2), bf16)] * 2,
        compiler_params=params(),
        cost_estimate=pl.CostEstimate(
            flops=3 * rows * m * n, bytes_accessed=4 * m * n, transcendentals=0
        ),
    )(me, left, right, *after)


def small_grad_kernel(count, me_ref, *refs):
    n3_ref, glearn_ref, ghid_ref, inner_ref, glogit_ref = refs[:5]
    attended = refs[5 : 5 + 2 * count]
    keep_ref, send_ref, lout_ref, learn_ref, wout_ref = refs[5 + 2 * count :]
    half = attended[0].shape[0]
    learn_ref[...] = tn(n3_ref[...], glearn_ref[...]).astype(bf16)
    lout_ref[...] = tn(inner_ref[...], glogit_ref[...])
    features = attended[0].shape[1]
    for d in range(count):
        owner = jnp.bitwise_xor(me_ref[0], d)
        to = pl.ds(pl.multiple_of(owner * features, features), features)
        part = tn(attended[d][...], ghid_ref[:half])
        part = part + tn(attended[count + d][...], ghid_ref[half:])
        wout_ref[to, :] = part.astype(bf16)
    first = me_ref[0] % 2 == 0

    @pl.when(first)
    def _():
        keep_ref[...] = learn_ref[...]
        send_ref[...] = wout_ref[...]

    @pl.when(jnp.logical_not(first))
    def _():
        keep_ref[...] = wout_ref[...]
        send_ref[...] = learn_ref[...]


def small_grad_call(me, n3, glearn, ghid, inner, glogit, attended):
    rows, width = n3.shape
    operands = [n3, glearn, ghid, inner, glogit, *attended]
    out = jax.ShapeDtypeStruct((width, ghid.shape[1]), bf16)
    lout = jax.ShapeDtypeStruct((inner.shape[1], glogit.shape[1]), f32)
    once = lambda a: pl.BlockSpec(a.shape, lambda j, m: (0, 0), pipeline_mode=pl.Buffered(1))
    return pl.pallas_call(
        functools.partial(small_grad_kernel, len(attended) // 2),
        grid_spec=pltpu.PrefetchScalarGridSpec(
            num_scalar_prefetch=1,
            grid=(1,),
            in_specs=[once(a) for a in operands],
            out_specs=[once(out), once(out), once(lout)],
            scratch_shapes=[pltpu.VMEM(out.shape, bf16), pltpu.VMEM(out.shape, bf16)],
        ),
        out_shape=[out, out, lout],
        compiler_params=params(),
        cost_estimate=pl.CostEstimate(
            flops=6 * rows * width * width, bytes_accessed=20 * width * width, transcendentals=0
        ),
    )(me, *operands)


def qkv_grad_kernel(groups, waits, me_ref, n_ref, gain_ref, shift_ref, *refs):
    parts, weights = refs[:groups], refs[groups : groups + 3]
    out_ref, sums_ref, acc_ref, sum_ref = refs[groups + 3 + waits :]
    step = pl.program_id(0)
    wide = weights[0].shape[1]
    for d in range(2 * groups):

        @pl.when(step == d)
        def _():
            mixed = parts[d // 2][d % 2]
            part = tn(n_ref[0], mixed)
            column = total(mixed.astype(f32))
            acc_ref[...] = part if d == 0 else acc_ref[...] + part
            sum_ref[...] = column if d == 0 else sum_ref[...] + column

    @pl.when(step == 2 * groups - 1)
    def _():
        by_unit, column = acc_ref[...], sum_ref[...]
        out_ref[...] = (by_unit * gain_ref[...] + shift_ref[...] * column).astype(bf16)
        weight = jnp.concatenate([ref[...].astype(f32) for ref in weights], axis=1)
        sums_ref[:, 0:1] = jnp.sum(by_unit * weight, axis=1, keepdims=True)
        sums_ref[:, 1:2] = jnp.sum(weight * column, axis=1, keepdims=True)


def qkv_grad_call(me, unit, parts, w_qkv, gain, shift, split, splits, after=()):
    count, rows, width = unit.shape
    columns = parts[0].shape[2]
    once = lambda a: pl.BlockSpec(
        a.shape, lambda d, m: (0,) * len(a.shape), pipeline_mode=pl.Buffered(1)
    )
    specs, operands = own_columns(w_qkv, width // count, splits, [split])
    return pl.pallas_call(
        functools.partial(qkv_grad_kernel, count // 2, len(after)),
        grid_spec=pltpu.PrefetchScalarGridSpec(
            num_scalar_prefetch=1,
            grid=(count,),
            in_specs=[pl.BlockSpec((1, rows, width), lambda d, m: (d, 0, 0)), once(gain), once(shift)]
            + [once(a) for a in parts]
            + specs
            + [ANYWHERE] * len(after),
            out_specs=[
                pl.BlockSpec((width, columns), lambda d, m: (0, 0)),
                pl.BlockSpec((width, 2), lambda d, m: (0, 0)),
            ],
            scratch_shapes=[pltpu.VMEM((width, columns), f32), pltpu.VMEM((1, columns), f32)],
        ),
        out_shape=[
            jax.ShapeDtypeStruct((width, columns), bf16),
            jax.ShapeDtypeStruct((width, 2), f32),
        ],
        compiler_params=params(),
        cost_estimate=pl.CostEstimate(flops=1 << 34, bytes_accessed=1 << 10, transcendentals=0),
    )(me, unit, gain, shift, *parts, *operands, *after)


def tokens_kernel(groups, splits, me_ref, tok_ref, ghid_ref, w_ref, gain_ref, *refs):
    same, other = refs[: groups * splits], refs[groups * splits : groups * splits + splits]
    out_ref, mixed_ref = refs[groups * splits + splits :]
    width = tok_ref.shape[1]
    features = width // (2 * groups)
    wide = features // splits
    for d in range(2 * groups):
        owner = jnp.bitwise_xor(me_ref[0], d) * features
        for s in range(splits):
            for part in range(3):
                to = pl.ds(pl.multiple_of(part * width + owner + s * wide, wide), wide)
                at = slice(part * wide, (part + 1) * wide)
                if d % 2 == 0:
                    mixed_ref[:, to] = same[s * groups + d // 2][0, :, at]
                else:
                    mixed_ref[:, to] = other[s][d // 2, :, at]
    back = nt(mixed_ref[...], w_ref[...])
    unit, rstd = norm_parts(tok_ref[...].astype(f32))
    out_ref[0] = ghid_ref[...] + norm_back(back, unit, rstd, gain_ref[...])


def tokens_call(me, tok, ghid, w_qkv, gain, same, other, count):
    local_rows, width = tok.shape
    columns = same[0].shape[2]
    groups, splits = count // 2, len(other)
    block = 256
    by_rows = lambda n: pl.BlockSpec((block, n), lambda i, m: (i, 0))
    return pl.pallas_call(
        functools.partial(tokens_kernel, groups, splits),
        grid_spec=pltpu.PrefetchScalarGridSpec(
            num_scalar_prefetch=1,
            grid=(pl.cdiv(local_rows, block),),
            in_specs=[
                by_rows(width),
                by_rows(width),
                pl.BlockSpec(w_qkv.shape, lambda i, m: (0, 0), pipeline_mode=pl.Buffered(1)),
                pl.BlockSpec(gain.shape, lambda i, m: (0, 0)),
            ]
            + [pl.BlockSpec((1, block, columns), lambda i, m: (0, i, 0))] * len(same)
            + [pl.BlockSpec((groups, block, columns), lambda i, m: (0, i, 0))] * splits,
            out_specs=pl.BlockSpec((1, block, width), lambda i, m: (0, i, 0)),
            scratch_shapes=[pltpu.VMEM((block, 3 * width), bf16)],
        ),
        out_shape=jax.ShapeDtypeStruct((1, local_rows, width), f32),
        compiler_params=params(),
        cost_estimate=pl.CostEstimate(flops=1 << 34, bytes_accessed=1 << 10, transcendentals=0),
    )(me, tok, ghid, w_qkv, gain, *same, *other)


def flip(index, bit):
    return index + bit - 2 * bit * ((index // bit) % 2)


def vectors_kernel(count, row_bits, img_bits, vec_ref, slot_ref, out_ref, sum_ref, *scratch):
    recv, slot_recv, send_sem, recv_sem, slot_send, slot_got = scratch
    row, img = lax.axis_index("row"), lax.axis_index("img")

    def partner(row_mask, img_mask=0):
        r, g = row, img
        for bit in row_bits:
            r = flip(r, bit) if row_mask & bit else r
        for bit in img_bits:
            g = flip(g, bit) if img_mask & bit else g
        return (g, r)

    steps = [(bit, 0) for bit in row_bits] + [(0, bit) for bit in img_bits]
    everyone = sorted(set(steps) | {(d, 0) for d in range(1, count)})
    barrier = pltpu.get_barrier_semaphore()
    for masks in everyone:
        pl.semaphore_signal(
            barrier, inc=1, device_id=partner(*masks), device_id_type=pl.DeviceIdType.MESH
        )
    pl.semaphore_wait(barrier, len(everyone))
    slots = []
    for d in range(1, count):
        copy = pltpu.make_async_remote_copy(
            src_ref=slot_ref.at[d],
            dst_ref=slot_recv.at[d - 1],
            send_sem=slot_send.at[d - 1],
            recv_sem=slot_got.at[d - 1],
            device_id=partner(d),
            device_id_type=pl.DeviceIdType.MESH,
        )
        copy.start()
        slots.append(copy)
    out_ref[...] = vec_ref[...]
    for i, masks in enumerate(steps):
        copy = pltpu.make_async_remote_copy(
            src_ref=out_ref,
            dst_ref=recv.at[i],
            send_sem=send_sem.at[i],
            recv_sem=recv_sem.at[i],
            device_id=partner(*masks),
            device_id_type=pl.DeviceIdType.MESH,
        )
        copy.start()
        copy.wait()
        out_ref[...] = out_ref[...] + recv[i]
    for copy in slots:
        copy.wait()
    sum_ref[...] = tree(
        [slot_ref[0].astype(f32)] + [slot_recv[d - 1].astype(f32) for d in range(1, count)]
    )


def vectors_call(vec, slots):
    count = lax.axis_size("row")
    row_bits, img_bits = bits_of(count), bits_of(lax.axis_size("img"))
    steps = len(row_bits) + len(img_bits)
    whole = pl.BlockSpec(memory_space=pltpu.VMEM)
    return pl.pallas_call(
        functools.partial(vectors_kernel, count, row_bits, img_bits),
        in_specs=[whole, whole],
        out_specs=[whole, whole],
        out_shape=[
            jax.ShapeDtypeStruct(vec.shape, f32),
            jax.ShapeDtypeStruct(slots.shape[1:], f32),
        ],
        scratch_shapes=[
            pltpu.VMEM((steps,) + vec.shape, f32),
            pltpu.VMEM((count - 1,) + slots.shape[1:], bf16),
            pltpu.SemaphoreType.DMA((steps,)),
            pltpu.SemaphoreType.DMA((steps,)),
            pltpu.SemaphoreType.DMA((count - 1,)),
            pltpu.SemaphoreType.DMA((count - 1,)),
        ],
        compiler_params=pltpu.CompilerParams(
            collective_id=0, has_side_effects=True, vmem_limit_bytes=32 << 20
        ),
        cost_estimate=pl.CostEstimate(flops=1 << 34, bytes_accessed=1 << 10, transcendentals=0),
    )(vec, slots)


def rows_of(array, index, length):
    return lax.dynamic_slice_in_dim(array, index * length, length, 0)


def on_device(
    tokens,
    counts,
    owner,
    w_qkv,
    qv_bias,
    w_out,
    out_bias,
    w_up,
    up_bias,
    w_down,
    down_bias,
    norm_gain,
    norm_bias,
    learn_in,
    learn_in_bias,
    learn_out,
    learn_out_bias,
    cotangent,
):
    width = tokens.shape[2]
    local_rows = tokens.shape[1]
    row_count = lax.axis_size("row")
    images_count = lax.axis_size("img")
    device = lax.axis_index("row")
    image_device = lax.axis_index("img")
    features = width // row_count
    wide = min(features, 128)
    splits = features // wide
    slots_here = IMGS // row_count
    group_counts = counts[0]
    partners = [device ^ d for d in range(row_count)]
    row_bits, img_bits = stages()
    n_img = len(img_bits)

    piece_rows = BLK // row_count
    blocks = pl.cdiv(local_rows, piece_rows)
    images = jnp.stack([row_images(group_counts, p, local_rows, row_count) for p in partners])
    extra = blocks * piece_rows - local_rows
    images = jnp.pad(images, ((0, 0), (0, extra)), constant_values=IMGS + 1)
    image_here = images[0].reshape(-1, 1)
    images = images.reshape(row_count, blocks, piece_rows).transpose(1, 0, 2).reshape(blocks, BLK)
    least, most = jnp.min(images, axis=1), jnp.max(images, axis=1)
    lo = jnp.sum((most[None, :] < least[:, None]).astype(jnp.int32), axis=1)
    hi = jnp.sum((least[None, :] <= most[:, None]).astype(jnp.int32), axis=1)
    imgq, imgk = images.reshape(1, -1), images.reshape(-1, 1)

    me = device.reshape(1)
    w_out_here = jnp.concatenate([rows_of(w_out, p, features) for p in partners], axis=0)
    bias_here = lax.dynamic_slice_in_dim(qv_bias, device * features, features, 1)
    half_count = row_count // 2
    first_norm = (w_qkv, bias_here, norm_gain[0:1], norm_bias[0:1], splits)
    far_tokens = jump(tokens[0], half_count)
    pieces = gather_pieces(tokens[0], half_count)
    filled = qkv_call(me, pieces, 0, *first_norm)
    tables = (imgq, imgk, lo, hi, image_here, w_out_here)
    far_tokens, filled, tables = lax.optimization_barrier((far_tokens, filled, tables))
    imgq, imgk, lo, hi, image_here, w_out_here = tables
    pieces = gather_pieces(far_tokens, half_count)
    unit, q, k, v, kt, vt = qkv_call(me, pieces, 1, *first_norm, filled)
    q, k, v = (a.reshape(-1, features) for a in (q, k, v))
    slot_grads = behind(cotangent[0].reshape(slots_here, LT * width).astype(bf16), [lo, unit])
    grads_in = gather_pieces(slot_grads, row_count)
    *upper, ot, lse = attend_call(q, k, vt, imgq, imgk, lo, hi, row_count, 0)
    upper = send_pieces(upper)
    *lower, ot, lse = attend_call(q, k, vt, imgq, imgk, lo, hi, row_count, 1, (ot, lse))
    upper[1:], ot, lse, lower = lax.optimization_barrier((upper[1:], ot, lse, lower))
    attended = upper + send_pieces(lower)

    slot_rel = ((owner[0] // slots_here) ^ device) * slots_here + owner[0] % slots_here
    select = (slot_rel[:, None] == jnp.arange(IMGS, dtype=jnp.int32)[None, :]).astype(f32)
    scale = lax.rsqrt(group_counts.astype(f32))
    incoming = jnp.concatenate(grads_in, axis=0).astype(f32)
    grad_pooled = jnp.dot(select, incoming, precision=highest) * scale[:, None]
    grad_pooled_low = grad_pooled.reshape(IMGS * LT, width).astype(bf16)

    vecs = jnp.concatenate(
        [
            out_bias[None],
            down_bias[None],
            norm_gain[1:2],
            norm_bias[1:2],
            norm_gain[2:3],
            norm_bias[2:3],
            learn_in_bias[None],
            jnp.zeros((1, width), f32),
        ],
        axis=0,
    )
    out = rows_call(
        tokens[0],
        image_here,
        attended,
        w_out_here,
        w_up,
        w_down,
        learn_in,
        jnp.tile(learn_out, (1, IMGS)),
        vecs,
        up_bias[None],
        jnp.tile(learn_out_bias, IMGS)[None],
        grad_pooled_low,
        splits,
    )
    n2, gated, gup, gres, n3, glearn, inner, glogit, ghid, grad_hidden = out[:10]
    grad_attended = out[10 : 10 + row_count * splits]
    pooled, vec_sums, up_sums, logit_sums = out[10 + row_count * splits :]
    grad_attended = [send_pieces(grad_attended[s::splits]) for s in range(splits)]

    core, far_row = row_bits[:1], row_bits[1:]
    y_bits, z_bits = img_bits[:1], [[bit] for bit in img_bits[1:]]
    half = lambda value, bits: Halving(value, bits, n_img)

    def core_flight(keep, send):
        flight = Exchange(keep, [])
        flight.moved = [jump(send, 1)]
        return flight

    keep_small, send_small, grad_learn_out = small_grad_call(
        me, n3, glearn, ghid, inner, glogit, attended
    )
    keep_down, send_down = down_grad_call(me, gated, gres, [send_small])
    keep_up, send_up = up_grad_call(me, n2, gup, [send_down])
    small, down = arrive(
        [core_flight(keep_small, send_small), core_flight(keep_down, send_down)], [send_up]
    )
    small, down = spread_img(small), spread_img(down)

    def back_call(s, after):
        *parts, sums = attend_back_call(
            grad_attended[s], q, k, v, kt, ot, lse, imgq, imgk, lo, hi, s, after
        )
        return parts, sums

    def grad_qkv_call(s, parts, after):
        turned = [norm_gain[0].reshape(-1, 1), norm_bias[0].reshape(-1, 1)]
        return qkv_grad_call(me, unit, parts, w_qkv, *turned, s, splits, after)

    groups = row_count // 2
    far_masks = [(2 * g, 0) for g in range(1, groups)]
    same, qkv_sums, norm_sums, grad_qkv = [], [], [], []
    after, far = [small, down, send_up], None
    for s in range(splits):
        parts, sums = back_call(s, after)
        qkv_sums.append(sums[0:2])
        if s == 0:
            small, down, ups = arrive(
                [half(small, y_bits), half(down, z_bits[0]), core_flight(keep_up, send_up)], [sums]
            )
            ups = spread_img(ups)
        if s == splits - 1:
            flights = [half(ups, y_bits), half(down, z_bits[1]), half(small, z_bits[0])]
            if far is not None:
                flights.append(far)
            ups, down, small, *arrived = arrive(flights, [sums])
            for pieces_far in arrived:
                same += pieces_far
        same.append(parts[0])
        far = Moved(parts[1:], far_masks)
        grad, norm_sum = grad_qkv_call(s, parts, [ups, down])
        if s == splits - 1:
            (ups, arrived, down, small), (grad, norm_sum) = arrive_with(
                [half(ups, z_bits[0]), far, half(down, y_bits), half(small, z_bits[1])],
                (grad, norm_sum),
            )
            same += arrived
        norm_sums.append(norm_sum)
        grad_qkv.append(spread_img(grad))
        after = [grad]
    grad_qkv = jnp.concatenate(grad_qkv, axis=-1)
    near = Moved([jnp.stack([p[1] for p in same])], [(1, 0)])

    by_slot = jnp.dot(select.T, pooled.reshape(IMGS, LT * width), precision=highest)
    by_slot = by_slot.astype(bf16).reshape(row_count, -1, 128)
    late = lax.dynamic_update_slice(
        jnp.zeros((2, width), f32), jnp.concatenate(qkv_sums, axis=1), (0, device * features)
    )
    vectors = jnp.concatenate(
        [
            up_sums.reshape(-1),
            vec_sums.reshape(-1),
            jnp.sum(grad_learn_out.reshape(-1, IMGS, LT), axis=1).reshape(-1),
            late.reshape(-1),
            sum(norm_sums).T.reshape(-1),
            jnp.sum(logit_sums.reshape(IMGS, LT), axis=0),
        ]
    )
    vectors = jnp.pad(vectors, (0, -vectors.shape[0] % 1024)).reshape(-1, 128)
    made = vectors_call(vectors, by_slot)

    for bits in z_bits[2:]:
        down, small = arrive([half(down, bits), half(small, bits)])
    ((others,), grad_qkv, ups, down, small), (vectors, learned) = arrive_with(
        [
            near,
            half(grad_qkv, y_bits),
            half(ups, z_bits[1]),
            half(down, far_row),
            Exchange(small, far_row),
        ],
        tuple(made),
    )
    for bits in z_bits[2:]:
        ups, grad_qkv = arrive([half(ups, bits), half(grad_qkv, bits)])
    other = [others[s * groups : (s + 1) * groups] for s in range(splits)]
    grad_tokens = tokens_call(
        me,
        tokens[0],
        behind(grad_hidden, [ups, grad_qkv, down, small]),
        w_qkv,
        norm_gain[0:1],
        same,
        other,
        row_count,
    )
    (grad_qkv, ups), grad_tokens = arrive_with(
        [half(grad_qkv, z_bits[0]), Exchange(ups, far_row)], grad_tokens
    )
    (grad_qkv,) = arrive([half(grad_qkv, z_bits[1])])
    vectors, learned = behind((vectors, learned), [grad_tokens])
    vectors = vectors.reshape(-1)
    scale_here = jnp.dot(scale, select, precision=highest)[:slots_here]
    learned = learned.reshape(slots_here, LT * width) * scale_here[:, None]
    learned = learned.reshape(1, slots_here, LT, width)

    share_down = finish_weight(down, row_bits)
    share_small = finish_weight(small, core, [grad_tokens])
    share_up = finish_weight(ups, core)
    share_learn = share_small[:, : learn_in.shape[1]]
    share_out = share_small[:, learn_in.shape[1] :]
    shares = gather_columns(grad_qkv.reshape(grad_qkv.shape[-2:]), lambda c: c, row_bits)
    share_qkv = jnp.concatenate(
        [
            shares[c][:, (3 * s + part) * wide : (3 * s + part + 1) * wide]
            for part in range(3)
            for c in range(row_count)
            for s in range(splits)
        ],
        axis=1,
    ).astype(f32)

    at = up_bias.shape[0]
    up_sum, vec_sums = vectors[:at], vectors[at : at + 8 * width].reshape(8, width)
    at += 8 * width
    learn_out_sum = vectors[at : at + learn_out.size].reshape(learn_out.shape)
    at += learn_out.size
    late = vectors[at : at + 4 * width].reshape(4, width)
    at += 4 * width
    out_sum, down_sum, gain_two, shift_two, gain_three, shift_three, learn_in_sum = vec_sums[:7]
    share_learn_out = rows_of(learn_out_sum, image_device, learn_out.shape[0] // images_count)
    return (
        learned,
        grad_tokens,
        share_qkv,
        late[0:2],
        share_out,
        out_sum,
        share_up,
        up_sum,
        share_down,
        down_sum,
        jnp.stack([late[2], gain_two, gain_three]),
        jnp.stack([late[3], shift_two, shift_three]),
        share_learn,
        learn_in_sum,
        share_learn_out,
        vectors[at : at + learn_out.shape[1]],
    )


def solution(mesh):
    by_image = P("img", None)
    in_specs = (
        (P("img", "row", None), by_image, by_image) + (P(),) * 14 + (P("img", "row", None, None),)
    )
    out_specs = (
        P("img", "row", None, None),
        P("img", "row", None),
        by_image,
        P(),
        by_image,
        P(),
        by_image,
        P(),
        by_image,
        P(),
        P(),
        P(),
        by_image,
        P(),
        by_image,
        P(),
    )
    return jax.shard_map(
        on_device, mesh=mesh, in_specs=in_specs, out_specs=out_specs, check_vma=False
    )
```
